128 devices in a mesh: vel: 4 (over x_lo, core), gx: 16 (over z, y), gy: 2 (over x_hi).
Axes of the slice: x: 4 (x_hi: 2, x_lo: 2; x = x_hi * 2 + x_lo), y: 4, z: 4, core: 2. Of those that a mesh axis runs over, the one named last changes fastest.
Arguments:
- previous: bfloat16 [4096, 128, 256], P('vel', 'gx', 'gy'), may hold values from 0 to 4, as said below
- relax_time: float32 [128, 256], P('gx', 'gy'), may hold values from 0.05 to 20
- left_right_kind: int32 [2, 256], P(None, 'gy'), may hold values from 0 to 1
- bottom_top_kind: int32 [2, 128], P(None, 'gx'), may hold values from 0 to 1
- left_right_inflow: bfloat16 [4096, 2, 256], P('vel', None, 'gy'), may hold values from 0.049804688 to 1
- bottom_top_inflow: bfloat16 [4096, 2, 128], P('vel', None, 'gx'), may hold values from 0.049804688 to 1
Outputs:
- updated: bfloat16 [4096, 128, 256], P('vel', 'gx', 'gy')
The draws below stay inside these ranges and needn't reach their ends.
Inputs may be any that keep to these rules, and one draw needn't show every extreme that they name: previous is positive in every entry. `left_right_kind`: 1 marks an inflow edge cell, 0 a diffuse wall. `bottom_top_kind`: 1 marks an inflow edge cell, 0 a diffuse wall.
All inputs are finite; a program needn't handle non-finite values.
Results may differ from the reference program's by a relative error of at most 0.0042.
Values may be sent and summed in bfloat16 or wider, within the bound.
A program may use at most 128 MiB of HBM per device.

```python
import math
import jax
import jax.numpy as jnp
from jax import lax

NVX = 64
V = 4096
NEWTON = 2
SWEEPS = 4
HORIZONTAL_CELLS = 128
VERTICAL_CELLS = 256


def draw_previous(key, part):
    random_seeds = jax.random.split(jax.random.fold_in(key, 11), 10)
    peak = jax.random.uniform(random_seeds[0], (1, HORIZONTAL_CELLS, VERTICAL_CELLS), jnp.float32, 0.5, 2.0)
    cool_x = jax.random.uniform(random_seeds[1], (1, HORIZONTAL_CELLS, VERTICAL_CELLS), jnp.float32, -1.2, 1.2)
    cool_y = jax.random.uniform(random_seeds[2], (1, HORIZONTAL_CELLS, VERTICAL_CELLS), jnp.float32, -1.2, 1.2)
    chilly_thermal_level = jax.random.uniform(random_seeds[3], (1, HORIZONTAL_CELLS, VERTICAL_CELLS), jnp.float32, 1.0, 3.0)
    hotspot_indicator = jax.random.randint(random_seeds[5], (1, HORIZONTAL_CELLS, VERTICAL_CELLS), 0, 2) == 1
    sign_x = (2 * jax.random.randint(random_seeds[6], (1, HORIZONTAL_CELLS, VERTICAL_CELLS), 0, 2) - 1).astype(jnp.float32)
    sign_y = (2 * jax.random.randint(random_seeds[7], (1, HORIZONTAL_CELLS, VERTICAL_CELLS), 0, 2) - 1).astype(jnp.float32)
    hot_x = sign_x * jax.random.uniform(random_seeds[8], (1, HORIZONTAL_CELLS, VERTICAL_CELLS), jnp.float32, 1.8, 2.8)
    hot_y = sign_y * jax.random.uniform(random_seeds[9], (1, HORIZONTAL_CELLS, VERTICAL_CELLS), jnp.float32, 1.8, 2.8)
    tepid_thermal_level = jax.random.uniform(jax.random.fold_in(random_seeds[3], 5), (1, HORIZONTAL_CELLS, VERTICAL_CELLS), jnp.float32, 4.0, 8.0)
    drift_horizontal = jnp.where(hotspot_indicator, hot_x, cool_x)
    drift_vertical = jnp.where(hotspot_indicator, hot_y, cool_y)
    pointwise_thermal_state = jnp.where(hotspot_indicator, tepid_thermal_level, chilly_thermal_level)
    rough = jnp.clip(1.0 + 0.25 * jax.random.normal(random_seeds[4], (V, HORIZONTAL_CELLS, VERTICAL_CELLS), jnp.float32), 0.4, 1.6)
    spacing = 12.0 / NVX
    vel_index = jnp.arange(V, dtype=jnp.int32)
    lattice_abscissa_horizontal = (((vel_index % NVX).astype(jnp.float32) - (NVX - 1) / 2.0) * spacing).reshape(V, 1, 1)
    lattice_abscissa_vertical = (((vel_index // NVX).astype(jnp.float32) - (NVX - 1) / 2.0) * spacing).reshape(V, 1, 1)
    normal_curve_power = -((lattice_abscissa_horizontal - drift_horizontal) ** 2 + (lattice_abscissa_vertical - drift_vertical) ** 2) / (2.0 * pointwise_thermal_state)
    return (peak * jnp.exp(normal_curve_power) * rough).astype(jnp.bfloat16)


def touch_ends(array, stream_key, smallest, high):
    dims = array.shape
    spot = [jax.random.randint(jax.random.fold_in(stream_key, axis), (), 0, dims[axis]) for axis in range(len(dims))]
    array = array.at[tuple(spot)].set(smallest)
    longest = dims.index(max(dims))
    spot[longest] = (spot[longest] + 1) % dims[longest]
    return array.at[tuple(spot)].set(high)


def steps_of(own_key, dims, pieces, smallest, largest):
    loudness = 1.0
    for axis_at, shards_of in pieces:
        heights = jax.random.uniform(jax.random.fold_in(jax.random.fold_in(own_key, 6), axis_at), (shards_of,), jnp.float32, smallest / len(pieces), largest / len(pieces))
        loudness = loudness * jnp.repeat(jnp.exp(heights), dims[axis_at] // shards_of).reshape((-1,) + (1,) * (len(dims) - 1 - axis_at))
    return loudness


def setup_inputs(seed: int = 0) -> dict:
    arg_keys = jax.random.split(jax.random.key(seed), 7)
    return {
        "previous": draw_previous(jax.random.fold_in(arg_keys[6], 71), 0),
        "relax_time": jnp.clip(jnp.exp(math.log(20.0) - 5.9914645 * jax.random.uniform(arg_keys[1], (HORIZONTAL_CELLS, VERTICAL_CELLS), jnp.float32) ** steps_of(arg_keys[1], (HORIZONTAL_CELLS, VERTICAL_CELLS), ((0, 16), (1, 2)), -0.2, 0.2)), 0.05, 20.0),
        "left_right_kind": touch_ends(jax.random.randint(arg_keys[2], (2, VERTICAL_CELLS), 0, 2), jax.random.fold_in(arg_keys[2], 1), 0, 1).astype(jnp.int32),
        "bottom_top_kind": touch_ends(jax.random.randint(arg_keys[3], (2, HORIZONTAL_CELLS), 0, 2), jax.random.fold_in(arg_keys[3], 1), 0, 1).astype(jnp.int32),
        "left_right_inflow": jnp.clip(0.049804688 + 0.9501953 * jax.random.uniform(arg_keys[4], (V, 2, VERTICAL_CELLS), jnp.float32) ** steps_of(arg_keys[4], (V, 2, VERTICAL_CELLS), ((0, 4), (2, 2)), -0.2, 0.2), 0.049804688, 1.0).astype(jnp.bfloat16),
        "bottom_top_inflow": jnp.clip(0.049804688 + 0.9501953 * jax.random.uniform(arg_keys[5], (V, 2, HORIZONTAL_CELLS), jnp.float32) ** steps_of(arg_keys[5], (V, 2, HORIZONTAL_CELLS), ((0, 4), (2, 16)), -0.2, 0.2), 0.049804688, 1.0).astype(jnp.bfloat16),
    }


courant = 100.0


def velocity_grid(first_vel, vel_count):
    spacing = 12.0 / NVX
    vel_index = first_vel + jnp.arange(vel_count, dtype=jnp.int32)
    lattice_abscissa_horizontal = ((vel_index % NVX).astype(jnp.float32) - (NVX - 1) / 2.0) * spacing
    lattice_abscissa_vertical = ((vel_index // NVX).astype(jnp.float32) - (NVX - 1) / 2.0) * spacing
    return lattice_abscissa_horizontal, lattice_abscissa_vertical


def basis_rows(lattice_abscissa_horizontal, lattice_abscissa_vertical, weight):
    energy = (lattice_abscissa_horizontal * lattice_abscissa_horizontal + lattice_abscissa_vertical * lattice_abscissa_vertical) / 2.0
    ones_row = jnp.ones_like(lattice_abscissa_horizontal)
    moment_basis = jnp.stack([ones_row, lattice_abscissa_horizontal, lattice_abscissa_vertical, energy]) * weight
    product_basis = jnp.stack([ones_row, lattice_abscissa_horizontal, lattice_abscissa_vertical, energy, lattice_abscissa_horizontal * lattice_abscissa_horizontal, lattice_abscissa_horizontal * lattice_abscissa_vertical, lattice_abscissa_horizontal * energy,
                               lattice_abscissa_vertical * lattice_abscissa_vertical, lattice_abscissa_vertical * energy, energy * energy]) * weight
    return moment_basis, product_basis


def equilibrium(params, lattice_abscissa_horizontal, lattice_abscissa_vertical):
    energy = (lattice_abscissa_horizontal * lattice_abscissa_horizontal + lattice_abscissa_vertical * lattice_abscissa_vertical) / 2.0
    normal_curve_power = (params[0][None, :] + lattice_abscissa_horizontal[:, None] * params[1][None, :]
                + lattice_abscissa_vertical[:, None] * params[2][None, :] + energy[:, None] * params[3][None, :])
    return jnp.exp(normal_curve_power)


def start_params(integral_statistics):
    particle_concentration = integral_statistics[0]
    mean_flow_horizontal = integral_statistics[1] / particle_concentration
    mean_flow_vertical = integral_statistics[2] / particle_concentration
    kinetic_norm_square = mean_flow_horizontal * mean_flow_horizontal + mean_flow_vertical * mean_flow_vertical
    pointwise_thermal_state = integral_statistics[3] / particle_concentration - kinetic_norm_square / 2.0
    return jnp.stack([jnp.log(particle_concentration / pointwise_thermal_state) - kinetic_norm_square / (2.0 * pointwise_thermal_state),
                      mean_flow_horizontal / pointwise_thermal_state, mean_flow_vertical / pointwise_thermal_state, -1.0 / pointwise_thermal_state])


def solve_four(hessian, gradient):
    matrix = [list(row_list) for row_list in hessian]
    target = list(gradient)
    for pivot in range(4):
        for lower in range(pivot + 1, 4):
            factor = matrix[lower][pivot] / matrix[pivot][pivot]
            for column_at in range(pivot, 4):
                matrix[lower][column_at] = matrix[lower][column_at] - factor * matrix[pivot][column_at]
            target[lower] = target[lower] - factor * target[pivot]
    result = [None, None, None, None]
    for pivot in (3, 2, 1, 0):
        accum = target[pivot]
        for column_at in range(pivot + 1, 4):
            accum = accum - matrix[pivot][column_at] * result[column_at]
        result[pivot] = accum / matrix[pivot][pivot]
    return result


def newton_update(params, partials, integral_statistics):
    layout = [[0, 1, 2, 3], [1, 4, 5, 6], [2, 5, 7, 8], [3, 6, 8, 9]]
    gradient = [partials[place] - integral_statistics[place] for place in range(4)]
    hessian = [[partials[layout[row_at][column_at]] for column_at in range(4)] for row_at in range(4)]
    correction = solve_four(hessian, gradient)
    return params - jnp.stack(correction)


def reference(previous, relax_time, left_right_kind, bottom_top_kind, left_right_inflow, bottom_top_inflow):
    spacing = 12.0 / NVX
    weight = spacing * spacing / (2.0 * math.pi)
    time_step = courant / ((NVX - 1) * spacing)
    lattice_abscissa_horizontal, lattice_abscissa_vertical = velocity_grid(0, V)
    moment_basis, product_basis = basis_rows(lattice_abscissa_horizontal, lattice_abscissa_vertical, weight)
    highest = lax.Precision.HIGHEST

    def row_source(row_item):
        column, relax_row = row_item
        integral_statistics = jnp.dot(moment_basis, column.astype(jnp.float32), precision=highest)
        params = start_params(integral_statistics)
        for number in range(NEWTON):
            partials = jnp.dot(product_basis, equilibrium(params, lattice_abscissa_horizontal, lattice_abscissa_vertical), precision=highest)
            params = newton_update(params, partials, integral_statistics)
        maxwell = equilibrium(params, lattice_abscissa_horizontal, lattice_abscissa_vertical)
        return column.astype(jnp.float32) / time_step + maxwell / relax_row[None, :]

    source = lax.map(row_source, (jnp.moveaxis(previous, 1, 0), relax_time))
    source = jnp.moveaxis(source, 0, 1)
    wall_all = jnp.exp(-(lattice_abscissa_horizontal * lattice_abscissa_horizontal + lattice_abscissa_vertical * lattice_abscissa_vertical) / 2.0)
    wall_norm = jnp.sum(jnp.maximum(lattice_abscissa_horizontal, 0.0) * wall_all) * weight
    pos_x = jnp.maximum(lattice_abscissa_horizontal, 0.0)[:, None, None]
    neg_x = jnp.maximum(-lattice_abscissa_horizontal, 0.0)[:, None, None]
    pos_y = jnp.maximum(lattice_abscissa_vertical, 0.0)[:, None, None]
    neg_y = jnp.maximum(-lattice_abscissa_vertical, 0.0)[:, None, None]
    denominator = 1.0 / time_step + 1.0 / relax_time[None, :, :] + (jnp.abs(lattice_abscissa_horizontal) + jnp.abs(lattice_abscissa_vertical))[:, None, None]
    out_left = jnp.maximum(-lattice_abscissa_horizontal, 0.0) * weight
    out_right = jnp.maximum(lattice_abscissa_horizontal, 0.0) * weight
    out_bottom = jnp.maximum(-lattice_abscissa_vertical, 0.0) * weight
    out_top = jnp.maximum(lattice_abscissa_vertical, 0.0) * weight
    current = previous
    for number in range(SWEEPS):
        values = current.astype(jnp.float32)
        flux_left = jnp.dot(out_left, values[:, 0, :], precision=highest)
        flux_right = jnp.dot(out_right, values[:, -1, :], precision=highest)
        flux_bottom = jnp.dot(out_bottom, values[:, :, 0], precision=highest)
        flux_top = jnp.dot(out_top, values[:, :, -1], precision=highest)
        ghost_left = jnp.where(left_right_kind[0][None, :] == 1, left_right_inflow[:, 0, :].astype(jnp.float32),
                               (flux_left / wall_norm)[None, :] * wall_all[:, None])
        ghost_right = jnp.where(left_right_kind[1][None, :] == 1, left_right_inflow[:, 1, :].astype(jnp.float32),
                                (flux_right / wall_norm)[None, :] * wall_all[:, None])
        ghost_bottom = jnp.where(bottom_top_kind[0][None, :] == 1, bottom_top_inflow[:, 0, :].astype(jnp.float32),
                                 (flux_bottom / wall_norm)[None, :] * wall_all[:, None])
        ghost_top = jnp.where(bottom_top_kind[1][None, :] == 1, bottom_top_inflow[:, 1, :].astype(jnp.float32),
                              (flux_top / wall_norm)[None, :] * wall_all[:, None])
        from_left = jnp.concatenate([ghost_left[:, None, :], values[:, :-1, :]], axis=1)
        from_right = jnp.concatenate([values[:, 1:, :], ghost_right[:, None, :]], axis=1)
        from_below = jnp.concatenate([ghost_bottom[:, :, None], values[:, :, :-1]], axis=2)
        from_above = jnp.concatenate([values[:, :, 1:], ghost_top[:, :, None]], axis=2)
        numerator = source + pos_x * from_left + neg_x * from_right + pos_y * from_below + neg_y * from_above
        current = (numerator / denominator).astype(jnp.bfloat16)
    return current
```

```python
import functools
import math

import jax
import jax.numpy as jnp
import numpy as np
from jax import lax
from jax.experimental import pallas as pl
from jax.experimental.pallas import tpu as pltpu
from jax.sharding import PartitionSpec as P

NVX = 64
HALF = NVX // 2
NEWTON = 2
SWEEPS = 4
CHUNKS = 4
STEP = 12.0 / NVX
WEIGHT = STEP * STEP / (2.0 * math.pi)
DT_INV = (NVX - 1) * STEP / 100.0
PITCH = 9

NODES = (np.arange(NVX) - (NVX - 1) / 2.0) * STEP
ABS = [float((j + 0.5) * STEP) for j in range(HALF)]
WALL_1D = np.exp(-NODES * NODES / 2.0)
WALL_NORM = float(np.sum(np.maximum(NODES, 0.0) * WALL_1D) * np.sum(WALL_1D) * WEIGHT)
FLUX_SCALE = WEIGHT / WALL_NORM

F32 = jnp.float32
BF16 = jnp.bfloat16
MESH = pl.DeviceIdType.MESH


def dot_nt(a, b, **kw):
    return lax.dot_general(a, b, (((1,), (1,)), ((), ())), preferred_element_type=F32, **kw)


def dot_tn(a, b, **kw):
    return lax.dot_general(a, b, (((0,), (0,)), ((), ())), preferred_element_type=F32, **kw)


def loop(low, high, step):
    lax.fori_loop(low, high, lambda n, carry: (step(n), carry)[1], 0)


def iota(shape, dim):
    return lax.broadcasted_iota(jnp.int32, shape, dim)


def one_dim(lin, quad):
    top = None
    size = jnp.abs(lin)
    for x in ABS:
        e = (size + quad * x) * x
        top = e if top is None else jnp.maximum(top, e)
    for x in ABS:
        even = quad * (x * x) - top
        odd = lin * x
        yield x, jnp.exp(even + odd), jnp.exp(even - odd)
    yield None, top, None


def power_sums(lin, quad):
    sums = [None] * 5
    top = None
    for x, plus, minus in one_dim(lin, quad):
        if x is None:
            top = plus
            break
        s, d = plus + minus, plus - minus
        for n in range(5):
            term = (s if n % 2 == 0 else d) * (x**n)
            sums[n] = term if sums[n] is None else sums[n] + term
    return sums, top


def start_params(u):
    rho = u[0]
    inv = 1.0 / rho
    ux, uy = u[1] * inv, u[2] * inv
    sq = ux * ux + uy * uy
    t = u[3] * inv - sq / 2.0
    it = 1.0 / t
    return jnp.log(rho * it) - sq * 0.5 * it, ux * it, uy * it, -it


def solve_four(hessian, gradient):
    m = [list(r) for r in hessian]
    t = list(gradient)
    inv = [None] * 4
    for p in range(4):
        inv[p] = 1.0 / m[p][p]
        for low in range(p + 1, 4):
            f = m[low][p] * inv[p]
            for c in range(p + 1, 4):
                m[low][c] = m[low][c] - f * m[p][c]
            t[low] = t[low] - f * t[p]
    r = [None] * 4
    for p in (3, 2, 1, 0):
        a = t[p]
        for c in range(p + 1, 4):
            a = a - m[p][c] * r[c]
        r[p] = a * inv[p]
    return r


def newton_step(p, u):
    s, top_x = power_sums(p[1], p[3] * 0.5)
    q, top_y = power_sums(p[2], p[3] * 0.5)
    c = jnp.exp(p[0] + top_x + top_y) * WEIGHT
    s = [c * a for a in s]
    w = [
        s[0] * q[0],
        s[1] * q[0],
        s[0] * q[1],
        (s[2] * q[0] + s[0] * q[2]) * 0.5,
        s[2] * q[0],
        s[1] * q[1],
        (s[3] * q[0] + s[1] * q[2]) * 0.5,
        s[0] * q[2],
        (s[2] * q[1] + s[0] * q[3]) * 0.5,
        (s[4] * q[0] + 2.0 * s[2] * q[2] + s[0] * q[4]) * 0.25,
    ]
    layout = [[0, 1, 2, 3], [1, 4, 5, 6], [2, 5, 7, 8], [3, 6, 8, 9]]
    corr = solve_four([[w[layout[a][b]] for b in range(4)] for a in range(4)], [w[a] - u[a] for a in range(4)])
    return tuple(p[a] - corr[a] for a in range(4))


def kernel(
    nv, nx, ny, rows,
    prev_h, relax, lrk, btk, lri, bti,
    out_h,
    prev, gmain, src, afac, invd, sr, sl, rr, rl, moms, momr,
    strip, ssrc, sinv, xg, yg, xsr, xsl, xrr, xrl, xpr, xpl, ysend, yrecv,
    fys, fyr, fxs, fxr, inf, tmp, infs, yinf, mwy, wyt, vxl, kinds, ins, par,
    ld, st, mom_s, mom_r, r_s, r_r, l_s, l_r, xr_s, xr_r, xl_s, xl_r,
    y_s, y_r, fy_s, fy_r, fx_s, fx_r,
):
    v, gx, gy = lax.axis_index("vel"), lax.axis_index("gx"), lax.axis_index("gy")
    kyn = rows // NVX
    per = kyn // CHUNKS
    up = v >= nv // 2
    first, last = gx == 0, gx == nx - 1
    not_first, not_last = gx > 0, gx < nx - 1
    edge = jnp.logical_or(first, last)
    upwind = lax.rem(v // (nv // 2) + gy, 2) == 1
    downwind = lax.rem(v // (nv // 2) + gy, 2) == 0
    roll_by = jnp.where(up, 1, 127)

    barrier = pltpu.get_barrier_semaphore()

    def greet(*dev):
        pl.semaphore_signal(barrier, inc=1, device_id=dev, device_id_type=MESH)

    for k in range(1, nv):
        greet(lax.rem(v + k, nv), gx, gy)
    greet(v, gx, 1 - gy)
    pl.when(not_first)(lambda: greet(v, gx - 1, gy))
    pl.when(not_last)(lambda: greet(v, gx + 1, gy))

    part = rows * 8 // CHUNKS

    def load(c):
        at = pl.ds(pl.multiple_of(c * part, part), part)
        return pltpu.make_async_copy(prev_h.at[at], prev.at[at], ld.at[c])

    for c in range(CHUNKS):
        load(c).start()

    def remote(s, d, ss, rs, *dev):
        return pltpu.make_async_remote_copy(s, d, ss, rs, device_id=dev, device_id_type=MESH)

    hrow = rows // 2 // CHUNKS

    def halo(s, c, side):
        at = pl.ds(pl.multiple_of(c * hrow, hrow), hrow)
        if side == 0:
            return remote(sr.at[s, at], rr.at[s, at], r_s.at[s, c], r_r.at[s, c], v, gx + 1, gy)
        return remote(sl.at[s, at], rl.at[s, at], l_s.at[s, c], l_r.at[s, c], v, gx - 1, gy)

    def shalo(s, side):
        if side == 0:
            return remote(xsr.at[s], xrr.at[s], xr_s.at[s], xr_r.at[s], v, gx + 1, gy)
        return remote(xsl.at[s], xrl.at[s], xl_s.at[s], xl_r.at[s], v, gx - 1, gy)

    def yhalo(s):
        return remote(ysend.at[s], yrecv.at[s], y_s.at[s], y_r.at[s], v, gx, 1 - gy)

    def moment(k):
        return remote(moms, momr.at[k - 1], mom_s.at[k - 1], mom_r.at[k - 1], lax.rem(v + k, nv), gx, gy)

    def fluxx(s, k):
        return remote(fxs.at[s], fxr.at[s, k - 1], fx_s.at[s, k - 1], fx_r.at[s, k - 1], lax.rem(v + k, nv), gx, gy)

    half = nv // 2

    def fluxy(s, k):
        mine = lax.rem(v, half)
        return remote(fys.at[s], fyr.at[s, mine], fy_s.at[s, k], fy_r.at[s, mine], (1 - v // half) * half + k, gx, gy)

    def fluxy_in(s, k):
        return remote(fys.at[s], fyr.at[s, k], fy_s.at[s, k], fy_r.at[s, k], (1 - v // half) * half + k, gx, gy)

    lane = iota((8, 128), 1)
    sub = iota((8, 128), 0)
    cell = lax.rem(lane, 8)
    in_tile = lane // 8
    irel = 1.0 / relax[...]

    def inv_of(m):
        at = pl.ds(pl.multiple_of(m * 8, 8), 8)
        invd[at, :] = 1.0 / (DT_INV + irel + (m + 1).astype(F32) * STEP)

    loop(0, NVX - 1, inv_of)
    for t in range(4):
        vxl[t * 8 : t * 8 + 8, :] = ((t * 16 + in_tile).astype(F32) - (NVX - 1) / 2.0) * STEP
    for b in range(kyn * 4 // 8):
        t = b * 8 + sub
        ky = (v * kyn + t // 4).astype(F32)
        yy = (ky - (NVX - 1) / 2.0) * STEP
        xx = ((lax.rem(t, 4) * 16 + in_tile).astype(F32) - (NVX - 1) / 2.0) * STEP
        at = slice(b * 8, b * 8 + 8)
        mwy[at, :] = jnp.exp((xx * xx + yy * yy) * -0.5)
        wyt[at, :] = jnp.abs(yy) * FLUX_SCALE
    posn = jnp.where(up, lane, 127 - lane)
    want = sub + jnp.where(sub >= 4, 120, 0)
    sel = (posn == want).astype(F32)
    sel16 = sel.astype(BF16)
    sel_up = jnp.where(sub < 4, sel, 0.0)
    in_strip = posn < 4
    rep8 = (cell == sub).astype(F32)

    pl.semaphore_wait(barrier, nv + not_first.astype(jnp.int32) + not_last.astype(jnp.int32))

    def gat(ky, off, stride=1):
        return pl.ds(ky * (NVX * PITCH) + off, 8, stride=stride)

    def pack_halo(ky, s):
        for q in range(0, HALF // 8, 2):
            right = [gmain[gat(ky, PITCH * (HALF + 8 * (q + d)) + 8, PITCH), :] for d in range(2)]
            left = [gmain[gat(ky, PITCH * 8 * (q + d), PITCH), :] for d in range(2)]
            at = pl.ds(pl.multiple_of(ky * HALF + q * 8, 16), 16)
            sr[s, at, :] = jnp.concatenate(right, axis=0).astype(BF16)
            sl[s, at, :] = jnp.concatenate(left, axis=0).astype(BF16)

    def send_chunk(s, c):
        pl.when(not_last)(lambda: halo(s, c, 0).start())
        pl.when(not_first)(lambda: halo(s, c, 1).start())

    def take_row(ky, u):
        base = pl.multiple_of(ky * (NVX * 8), NVX * 8)
        s0 = s1 = s2 = jnp.zeros((8, 128), F32)
        for i in range(0, HALF, 2):
            pos = prev[pl.ds(base + (HALF + i) * 8, 16), :].astype(F32)
            neg = prev[pl.ds(base + (HALF - 2 - i) * 8, 16), :].astype(F32)
            for d in range(2):
                a, b = pos[8 * d : 8 * d + 8], neg[8 - 8 * d : 16 - 8 * d]
                gmain[gat(ky, PITCH * (HALF + i + d) + 1), :] = a
                gmain[gat(ky, PITCH * (HALF - 1 - i - d)), :] = b
                x = ABS[i + d]
                both = a + b
                s0 = s0 + both
                s1 = s1 + (a - b) * x
                s2 = s2 + both * (x * x)
        yy = ((v * kyn + ky).astype(F32) - (NVX - 1) / 2.0) * STEP
        pack_halo(ky, 0)
        return (u[0] + s0, u[1] + s1, u[2] + s0 * yy, u[3] + (s2 + s0 * (yy * yy)) * 0.5)

    def take_chunk(c, u):
        load(c).wait()
        u = lax.fori_loop(c * per, c * per + per, take_row, u)
        send_chunk(0, c)
        return u

    zero = jnp.zeros((8, 128), F32)
    u = lax.fori_loop(0, CHUNKS, take_chunk, (zero, zero, zero, zero))
    for a in range(4):
        moms[a * 8 : a * 8 + 8, :] = u[a] * WEIGHT
    for k in range(1, nv):
        moment(k).start()

    def take_strip(ky):
        block = prev[pl.ds(pl.multiple_of(ky * 512, 512), 512), :]
        got = dot_nt(sel16, block)
        for t in range(4):
            strip[pl.ds(pl.multiple_of(ky * 32 + t * 8, 8), 8), :] = got[:, t * 128 : t * 128 + 128]

    loop(0, kyn, take_strip)

    def tile(ky, t):
        return pl.ds(pl.multiple_of(ky * 32 + t * 8, 8), 8)

    groups = kyn // 4

    def send_strips(s):
        def pack(g):
            right = left = jnp.zeros((8, 128), F32)
            for r in range(4):
                for h in range(2):
                    k = r * 2 + h
                    c = strip[tile(g * 4 + r, 2 + h), :]
                    right = jnp.where(cell == k, c if k == 7 else pltpu.roll(c, (k - 7) % 128, 1), right)
                    c = strip[tile(g * 4 + r, h), :]
                    left = jnp.where(cell == k, c if k == 0 else pltpu.roll(c, k, 1), left)
            at = pl.ds(pl.multiple_of(g * 8, 8), 8)
            xpr[at, :] = right
            xpl[at, :] = left

        loop(0, groups, pack)
        xsr[s] = xpr[...].astype(BF16)
        xsl[s] = xpl[...].astype(BF16)
        pl.when(not_last)(lambda: shalo(s, 0).start())
        pl.when(not_first)(lambda: shalo(s, 1).start())

        acc = jnp.zeros((8, 128), F32)
        for b in range(0, kyn * 4 // 8, 2):
            two = []
            for d in range(2):
                row = strip[pl.ds((b + d) * 64 + 7, 8, stride=8), :]
                acc = acc + row * wyt[(b + d) * 8 : (b + d) * 8 + 8, :]
                two.append(row)
            ysend[s, b * 8 : b * 8 + 16, :] = jnp.concatenate(two, axis=0).astype(BF16)
        fys[s] = acc

        @pl.when(upwind)
        def _():
            yhalo(s).start()

        @pl.when(downwind)
        def _():
            for k in range(half):
                fluxy(s, k).start()

    def send_edges(s):
        def partial(rows_ref, tile_off, spot):
            def add(ky, carry):
                main, thin = carry
                block = rows_ref[s, pl.ds(pl.multiple_of(ky * HALF, HALF), HALF), :].astype(F32)
                for q in range(HALF // 8):
                    j = (q * 8 + sub).astype(F32)
                    x = (j + 0.5) * STEP if tile_off else (HALF - 0.5 - j) * STEP
                    main = main + block[q * 8 : q * 8 + 8] * x
                for h in range(2):
                    c = strip[tile(ky, tile_off + h), :]
                    x = jnp.abs(vxl[(tile_off + h) * 8 : (tile_off + h) * 8 + 8, :])
                    thin = thin + c * jnp.where(cell == spot, x, 0.0)
                return main, thin

            main, thin = lax.fori_loop(0, kyn, add, (zero, zero))
            thin = jnp.broadcast_to(jnp.sum(thin, axis=1, keepdims=True), (8, 128)) * sel_up
            fxs[s] = (jnp.where(in_strip, 0.0, main) + thin) * FLUX_SCALE
            for k in range(1, nv):
                fluxx(s, k).start()

        pl.when(first)(lambda: partial(sl, 0, 0))
        pl.when(last)(lambda: partial(sr, 2, 7))

    send_strips(0)
    send_edges(0)

    @pl.when(edge)
    def _():
        side = jnp.where(first, 0, 1)
        off = jnp.where(first, HALF, 0)

        def take(ky):
            at = pl.ds(pl.multiple_of((ky * NVX + off) * 2, 2 * HALF), 2 * HALF)
            tmp[...] = lri[at, :].astype(F32)
            for q in range(HALF // 8):
                at = pl.ds(pl.multiple_of(ky * HALF + q * 8, 8), 8)
                inf[at, :] = tmp[pl.ds(q * 16 + side, 8, stride=2), :]

        loop(0, kyn, take)
        kind = jnp.where(first, lrk[0:1, :], lrk[1:2, :]).astype(F32)
        kinds[0:8, :] = jnp.broadcast_to(kind, (8, 128))
        kinds[8:16, :] = dot_nt(sel, jnp.broadcast_to(kind, (128, 128)))

        def spread(b):
            got = dot_nt(sel, inf[pl.ds(pl.multiple_of(b * 128, 128), 128), :])
            for w in range(8):
                rep = (iota((128, 128), 0) == w * 16 + iota((128, 128), 1) // 8).astype(F32)
                infs[pl.ds(pl.multiple_of(b * 64 + w * 8, 8), 8), :] = jnp.dot(got, rep, preferred_element_type=F32)

        loop(0, kyn * HALF // 128, spread)

    @pl.when(upwind)
    def _():
        side = jnp.where(up, 0, 1)
        row = iota((512, 128), 0)
        keep = jnp.logical_and(lax.rem(row, 2) == side, lax.rem(row // 2, 16) == iota((512, 128), 1) // 8)
        gather = (iota((16, 512), 1) // 32 == iota((16, 512), 0)).astype(F32)

        def take(b):
            block = bti[pl.ds(pl.multiple_of(b * 512, 512), 512), :].astype(F32)
            wide = jnp.dot(block, rep8, preferred_element_type=F32)
            wide = jnp.where(keep, wide, 0.0)
            yinf[pl.ds(pl.multiple_of(b * 16, 16), 16), :] = jnp.dot(gather, wide, preferred_element_type=F32)

        loop(0, rows * 2 // 512, take)
        kind = jnp.where(up, btk[0:1, :], btk[1:2, :]).astype(F32)
        kinds[16:24, :] = jnp.dot(jnp.broadcast_to(kind, (8, 8)), rep8, preferred_element_type=F32)

    for k in range(1, nv):
        moment(k).wait_recv()
    u = [moms[a * 8 : a * 8 + 8, :] for a in range(4)]
    for k in range(nv - 1):
        u = [u[a] + momr[k, a * 8 : a * 8 + 8, :] for a in range(4)]
    p = start_params(u)
    p = lax.fori_loop(0, NEWTON, lambda n, q: newton_step(q, u), p)

    pq = p[3] * 0.5
    top_x = None
    for j, (x, plus, minus) in enumerate(one_dim(p[1], pq)):
        if x is None:
            top_x = plus
        else:
            afac[(HALF + j) * 8 : (HALF + j) * 8 + 8, :] = plus
            afac[(HALF - 1 - j) * 8 : (HALF - j) * 8, :] = minus
    height = p[0] + top_x

    thin = [
        dot_nt(sel, jnp.broadcast_to(a[None], (16, 8, 128)).reshape(128, 128), precision=lax.Precision.HIGHEST)
        for a in (*p, irel)
    ]

    def speed_y(ky):
        return ((v * kyn + ky).astype(F32) - (NVX - 1) / 2.0) * STEP

    def edge_flux(s):
        total = fxs[s]
        for k in range(nv - 1):
            total = total + fxr[s, k]
        return jnp.broadcast_to(jnp.sum(total, axis=0, keepdims=True), (8, 128))

    def sweep_strips(s):
        @pl.when(not_first)
        def _():
            shalo(s, 0).wait_recv()
            xpr[...] = xrr[s].astype(F32)

            def put(g):
                c = xpr[pl.ds(pl.multiple_of(g * 8, 8), 8), :]
                for k in range(8):
                    xg[tile(g * 4 + k // 2, 2 + k % 2), :] = c if k == 0 else pltpu.roll(c, 128 - k, 1)

            loop(0, groups, put)

        @pl.when(not_last)
        def _():
            shalo(s, 1).wait_recv()
            xpl[...] = xrl[s].astype(F32)

            def put(g):
                c = xpl[pl.ds(pl.multiple_of(g * 8, 8), 8), :]
                for k in range(8):
                    xg[tile(g * 4 + k // 2, k % 2), :] = c if k == 7 else pltpu.roll(c, 7 - k, 1)

            loop(0, groups, put)

        @pl.when(edge)
        def _():
            for k in range(1, nv):
                fluxx(s, k).wait_recv()
            kind = kinds[8:16, :]
            flux = jnp.broadcast_to(jnp.sum(edge_flux(s) * sel, axis=1, keepdims=True), (8, 128)) * (1.0 - kind)

            def fill(ky, t0):
                for h in range(2):
                    wall = mwy[pl.ds(ky * 4 + t0 + h, 1), :]
                    inflow = infs[pl.ds(pl.multiple_of(ky * 16 + h * 8, 8), 8), :]
                    xg[tile(ky, t0 + h), :] = kind * inflow + flux * wall

            pl.when(first)(lambda: loop(0, kyn, lambda ky: fill(ky, 2)))
            pl.when(last)(lambda: loop(0, kyn, lambda ky: fill(ky, 0)))

        @pl.when(downwind)
        def _():
            yhalo(s).wait_recv()
            yg[...] = yrecv[s].astype(F32)

        @pl.when(upwind)
        def _():
            for k in range(half):
                fluxy_in(s, k).wait_recv()
            total = fyr[s, 0]
            for k in range(1, half):
                total = total + fyr[s, k]
            flux = jnp.broadcast_to(jnp.sum(total, axis=0, keepdims=True), (8, 128))
            for k in (8, 16, 32, 64):
                flux = flux + pltpu.roll(flux, k, 1)
            kind = kinds[16:24, :]
            flux = flux * (1.0 - kind)
            for b in range(kyn * 4 // 8):
                at = slice(b * 8, b * 8 + 8)
                yg[at, :] = kind * yinf[at, :] + flux * mwy[at, :]

        def step(ky):
            yy = speed_y(ky)
            ay = jnp.abs(yy)
            for t in range(4):
                c = strip[tile(ky, t), :]
                xx = vxl[t * 8 : t * 8 + 8, :]
                ax = jnp.abs(xx)
                if s == 0:
                    power = thin[0] + xx * thin[1] + yy * thin[2] + (xx * xx + yy * yy) * 0.5 * thin[3]
                    source = c * DT_INV + jnp.exp(power) * thin[4]
                    inv = 1.0 / (DT_INV + thin[4] + ax + ay)
                    ssrc[tile(ky, t), :] = source
                    sinv[tile(ky, t), :] = inv
                else:
                    source = ssrc[tile(ky, t), :]
                    inv = sinv[tile(ky, t), :]
                from_y = jnp.where(sub == 0, yg[pl.ds(ky * 4 + t, 1), :], pltpu.roll(c, 1, 0))
                if t >= 2:
                    from_x = jnp.where(cell == 0, xg[tile(ky, t), :], pltpu.roll(c, 1, 1))
                else:
                    from_x = jnp.where(cell == 7, xg[tile(ky, t), :], pltpu.roll(c, 127, 1))
                strip[tile(ky, t), :] = (source + ax * from_x + ay * from_y) * inv

        loop(0, kyn, step)

    def fill_main(s, c):
        @pl.when(not_first)
        def _():
            halo(s, c, 0).wait_recv()

            def put(ky):
                block = rr[s, pl.ds(pl.multiple_of(ky * HALF, HALF), HALF), :].astype(F32)
                for q in range(HALF // 8):
                    gmain[gat(ky, PITCH * (HALF + 8 * q), PITCH), :] = block[q * 8 : q * 8 + 8]

            loop(c * per, c * per + per, put)

        @pl.when(not_last)
        def _():
            halo(s, c, 1).wait_recv()

            def put(ky):
                block = rl[s, pl.ds(pl.multiple_of(ky * HALF, HALF), HALF), :].astype(F32)
                for q in range(HALF // 8):
                    gmain[gat(ky, PITCH * 8 * q + 8, PITCH), :] = block[q * 8 : q * 8 + 8]

            loop(c * per, c * per + per, put)

        @pl.when(edge)
        def _():
            kind = kinds[0:8, :]
            flux = edge_flux(s) * (1.0 - kind)

            def rows_of(ky, q, positive):
                j = (q * 8 + sub).astype(F32)
                x = (j + 0.5) * STEP if positive else (HALF - 0.5 - j) * STEP
                yy = speed_y(ky)
                wall = jnp.exp((x * x + yy * yy) * -0.5)
                return kind * inf[pl.ds(pl.multiple_of(ky * HALF + q * 8, 8), 8), :] + flux * wall

            def put_low(ky):
                for q in range(HALF // 8):
                    gmain[gat(ky, PITCH * (HALF + 8 * q), PITCH), :] = rows_of(ky, q, True)

            def put_high(ky):
                for q in range(HALF // 8):
                    gmain[gat(ky, PITCH * 8 * q + 8, PITCH), :] = rows_of(ky, q, False)

            pl.when(first)(lambda: loop(c * per, c * per + per, put_low))
            pl.when(last)(lambda: loop(c * per, c * per + per, put_high))

    def main_row(ky, s, b_of):
        yy = speed_y(ky)
        ay = jnp.abs(yy)
        kyg = v * kyn + ky
        jj = jnp.where(kyg >= HALF, kyg - HALF, HALF - 1 - kyg)
        base = pl.multiple_of(ky * (NVX * 8), NVX * 8)
        if s == 0:
            bfac = b_of(yy)
        for i in range(0, HALF, 2):
            inv = [invd[pl.ds(pl.multiple_of((jj + i + d) * 8, 8), 8), :] for d in range(2)]
            for positive in (True, False):
                done = []
                for d in range(2):
                    kx = HALF + i + d if positive else HALF - 1 - i - d
                    own_off = PITCH * kx + (1 if positive else 0)
                    own = gmain[gat(ky, own_off), :]
                    moved = gmain[gat(ky, PITCH * kx + (0 if positive else 1)), :]
                    turned = pltpu.roll(own, roll_by, 1)
                    at = pl.ds(base + kx * 8, 8)
                    if s == 0:
                        source = own * DT_INV + afac[kx * 8 : kx * 8 + 8, :] * bfac
                        src[at, :] = source
                    else:
                        source = src[at, :]
                    new = (source + moved * ABS[i + d] + turned * ay) * inv[d]
                    if s < SWEEPS - 1:
                        gmain[gat(ky, own_off), :] = new
                    else:
                        done.append(jnp.where(in_strip, ins[at, :], new))
                if s == SWEEPS - 1:
                    kx = HALF + i if positive else HALF - 2 - i
                    if not positive:
                        done = done[::-1]
                    prev[pl.ds(base + kx * 8, 16), :] = jnp.concatenate(done, axis=0).astype(BF16)

    def store(c):
        at = pl.ds(pl.multiple_of(c * part, part), part)
        return pltpu.make_async_copy(prev.at[at], out_h.at[at], st.at[c])

    size_y = jnp.abs(p[2])
    top_y = None
    for y in ABS:
        e = (size_y + pq * y) * y
        top_y = e if top_y is None else jnp.maximum(top_y, e)
    amp = jnp.exp(height + top_y) * irel

    def b_of(yy):
        return amp * jnp.exp((p[2] + pq * yy) * yy - top_y)

    for s in range(SWEEPS):
        sweep_strips(s)
        if s < SWEEPS - 1:
            send_strips(s + 1)
        else:

            def put(ky):
                for t in range(4):
                    at = pl.ds(pl.multiple_of(ky * 512 + t * 128, 128), 128)
                    ins[at, :] = dot_tn(strip[tile(ky, t), :], sel_up)

            loop(0, kyn, put)

        def chunk(c):
            fill_main(s, c)

            def one(ky):
                main_row(ky, s, b_of)
                if s < SWEEPS - 1:
                    pack_halo(ky, s + 1)

            loop(c * per, c * per + per, one)
            if s < SWEEPS - 1:
                send_chunk(s + 1, c)
            else:
                store(c).start()

        loop(0, CHUNKS, chunk)
        if s < SWEEPS - 1:
            send_edges(s + 1)

    for k in range(1, nv):
        moment(k).wait_send()

    def drain(s):
        def both(c):
            pl.when(not_last)(lambda: halo(s, c, 0).wait_send())
            pl.when(not_first)(lambda: halo(s, c, 1).wait_send())

        loop(0, CHUNKS, both)
        pl.when(not_last)(lambda: shalo(s, 0).wait_send())
        pl.when(not_first)(lambda: shalo(s, 1).wait_send())
        pl.when(upwind)(lambda: yhalo(s).wait_send())

        @pl.when(downwind)
        def _():
            for k in range(half):
                fluxy(s, k).wait_send()

        @pl.when(edge)
        def _():
            for k in range(1, nv):
                fluxx(s, k).wait_send()


    loop(0, SWEEPS, drain)
    for c in range(CHUNKS):
        store(c).wait()


def body(previous, relax_time, left_right_kind, bottom_top_kind, left_right_inflow, bottom_top_inflow, *, sizes):
    nv, nx, ny = sizes
    rows, cx, cy = previous.shape
    kyn = rows // NVX
    thin = rows * 8 // 128 * 8
    dma = pltpu.SemaphoreType.DMA
    vm = pltpu.VMEM
    hr = rows // 2
    ur = kyn * 4
    xr = kyn * 2
    scratch = [
        vm((rows * 8, 128), BF16), vm((rows * PITCH, 128), F32), vm((rows * 8, 128), F32),
        vm((NVX * 8, 128), F32), vm((NVX * 8, 128), F32),
        vm((SWEEPS, hr, 128), BF16), vm((SWEEPS, hr, 128), BF16),
        vm((SWEEPS, hr, 128), BF16), vm((SWEEPS, hr, 128), BF16),
        vm((32, 128), F32), vm((nv - 1, 32, 128), F32),
        vm((thin, 128), F32), vm((thin, 128), F32), vm((thin, 128), F32), vm((thin, 128), F32),
        vm((ur, 128), F32),
        vm((SWEEPS, xr, 128), BF16), vm((SWEEPS, xr, 128), BF16),
        vm((SWEEPS, xr, 128), BF16), vm((SWEEPS, xr, 128), BF16),
        vm((xr, 128), F32), vm((xr, 128), F32),
        vm((SWEEPS, ur, 128), BF16), vm((SWEEPS, ur, 128), BF16),
        vm((SWEEPS, 8, 128), F32), vm((SWEEPS, nv // 2, 8, 128), F32),
        vm((SWEEPS, 8, 128), F32), vm((SWEEPS, nv - 1, 8, 128), F32),
        vm((hr, 128), F32), vm((NVX, 128), F32), vm((thin // 2, 128), F32),
        vm((ur, 128), F32), vm((ur, 128), F32), vm((ur, 128), F32),
        vm((32, 128), F32), vm((24, 128), F32), vm((rows * 8, 128), F32), vm((8, 128), F32),
        dma((CHUNKS,)), dma((CHUNKS,)), dma((nv - 1,)), dma((nv - 1,)),
        dma((SWEEPS, CHUNKS)), dma((SWEEPS, CHUNKS)), dma((SWEEPS, CHUNKS)), dma((SWEEPS, CHUNKS)),
        dma((SWEEPS,)), dma((SWEEPS,)), dma((SWEEPS,)), dma((SWEEPS,)),
        dma((SWEEPS,)), dma((SWEEPS,)), dma((SWEEPS, nv // 2)), dma((SWEEPS, nv // 2)),
        dma((SWEEPS, nv - 1)), dma((SWEEPS, nv - 1)),
    ]
    whole = pl.BlockSpec(memory_space=pltpu.VMEM)
    far = pl.BlockSpec(memory_space=pl.ANY)
    out = pl.pallas_call(
        functools.partial(kernel, nv, nx, ny, rows),
        out_shape=jax.ShapeDtypeStruct((rows * 8, 128), BF16),
        in_specs=[far, whole, whole, whole, whole, whole],
        out_specs=far,
        scratch_shapes=scratch,
        compiler_params=pltpu.CompilerParams(
            collective_id=0, has_side_effects=True, vmem_limit_bytes=48 * 1024 * 1024
        ),
        name="bgk_step",
    )(
        previous.reshape(rows * 8, 128),
        relax_time,
        left_right_kind,
        bottom_top_kind,
        left_right_inflow.reshape(rows * 2, 128),
        bottom_top_inflow.reshape(rows * 2, 8),
    )
    return out.reshape(rows, cx, cy)


def solution(mesh):
    sizes = (mesh.shape["vel"], mesh.shape["gx"], mesh.shape["gy"])
    return jax.shard_map(
        functools.partial(body, sizes=sizes),
        mesh=mesh,
        in_specs=(
            P("vel", "gx", "gy"),
            P("gx", "gy"),
            P(None, "gy"),
            P(None, "gx"),
            P("vel", None, "gy"),
            P("vel", None, "gx"),
        ),
        out_specs=P("vel", "gx", "gy"),
        check_vma=False,
    )
```

```python
import functools
import math

import jax
import jax.numpy as jnp
import numpy as np
from jax import lax
from jax.experimental import pallas as pl
from jax.experimental.pallas import tpu as pltpu
from jax.sharding import PartitionSpec as P

NVX = 64
HALF = NVX // 2
NEWTON = 2
SWEEPS = 4
CHUNKS = 4
STEP = 12.0 / NVX
WEIGHT = STEP * STEP / (2.0 * math.pi)
DT_INV = (NVX - 1) * STEP / 100.0
PITCH = 9

NODES = (np.arange(NVX) - (NVX - 1) / 2.0) * STEP
ABS = [float((j + 0.5) * STEP) for j in range(HALF)]
WALL_1D = np.exp(-NODES * NODES / 2.0)
WALL_NORM = float(np.sum(np.maximum(NODES, 0.0) * WALL_1D) * np.sum(WALL_1D) * WEIGHT)
FLUX_SCALE = WEIGHT / WALL_NORM

F32 = jnp.float32
BF16 = jnp.bfloat16
MESH = pl.DeviceIdType.MESH


def dot_nt(a, b, **kw):
    return lax.dot_general(a, b, (((1,), (1,)), ((), ())), preferred_element_type=F32, **kw)


def dot_tn(a, b, **kw):
    return lax.dot_general(a, b, (((0,), (0,)), ((), ())), preferred_element_type=F32, **kw)


def loop(low, high, step):
    lax.fori_loop(low, high, lambda n, carry: (step(n), carry)[1], 0)


def iota(shape, dim):
    return lax.broadcasted_iota(jnp.int32, shape, dim)


def one_dim(lin, quad):
    top = None
    size = jnp.abs(lin)
    for x in ABS:
        e = (size + quad * x) * x
        top = e if top is None else jnp.maximum(top, e)
    for x in ABS:
        even = quad * (x * x) - top
        odd = lin * x
        yield x, jnp.exp(even + odd), jnp.exp(even - odd)
    yield None, top, None


def power_sums(lin, quad):
    sums = [None] * 5
    top = None
    for x, plus, minus in one_dim(lin, quad):
        if x is None:
            top = plus
            break
        s, d = plus + minus, plus - minus
        for n in range(5):
            term = (s if n % 2 == 0 else d) * (x**n)
            sums[n] = term if sums[n] is None else sums[n] + term
    return sums, top


def start_params(u):
    rho = u[0]
    inv = 1.0 / rho
    ux, uy = u[1] * inv, u[2] * inv
    sq = ux * ux + uy * uy
    t = u[3] * inv - sq / 2.0
    it = 1.0 / t
    return jnp.log(rho * it) - sq * 0.5 * it, ux * it, uy * it, -it


def solve_four(hessian, gradient):
    m = [list(r) for r in hessian]
    t = list(gradient)
    inv = [None] * 4
    for p in range(4):
        inv[p] = 1.0 / m[p][p]
        for low in range(p + 1, 4):
            f = m[low][p] * inv[p]
            for c in range(p + 1, 4):
                m[low][c] = m[low][c] - f * m[p][c]
            t[low] = t[low] - f * t[p]
    r = [None] * 4
    for p in (3, 2, 1, 0):
        a = t[p]
        for c in range(p + 1, 4):
            a = a - m[p][c] * r[c]
        r[p] = a * inv[p]
    return r


def newton_step(p, u):
    s, top_x = power_sums(p[1], p[3] * 0.5)
    q, top_y = power_sums(p[2], p[3] * 0.5)
    c = jnp.exp(p[0] + top_x + top_y) * WEIGHT
    s = [c * a for a in s]
    w = [
        s[0] * q[0],
        s[1] * q[0],
        s[0] * q[1],
        (s[2] * q[0] + s[0] * q[2]) * 0.5,
        s[2] * q[0],
        s[1] * q[1],
        (s[3] * q[0] + s[1] * q[2]) * 0.5,
        s[0] * q[2],
        (s[2] * q[1] + s[0] * q[3]) * 0.5,
        (s[4] * q[0] + 2.0 * s[2] * q[2] + s[0] * q[4]) * 0.25,
    ]
    layout = [[0, 1, 2, 3], [1, 4, 5, 6], [2, 5, 7, 8], [3, 6, 8, 9]]
    corr = solve_four([[w[layout[a][b]] for b in range(4)] for a in range(4)], [w[a] - u[a] for a in range(4)])
    return tuple(p[a] - corr[a] for a in range(4))


def kernel(
    nv, nx, ny, rows,
    prev_h, relax_h, lrk_h, btk_h, lri_h, bti_h,
    out_h,
    prev, gmain, src, afac, invd, sr, sl, rr, rl, moms, momr,
    strip, ssrc, sinv, yg, xsr, xsl, xrr, xrl, esrc, einv, ysend, yrecv,
    fys, fyr, fxs, fxr, inf, infp, mwp, yinf, mwy, wyt, vxl, kinds, ins,
    relax, lrk, btk, lri, bti,
    ld, small, st, mom_s, mom_r, r_s, r_r, l_s, l_r, xr_s, xr_r, xl_s, xl_r,
    y_s, y_r, fy_s, fy_r, fx_s, fx_r,
):
    v, gx, gy = lax.axis_index("vel"), lax.axis_index("gx"), lax.axis_index("gy")
    kyn = rows // NVX
    per = kyn // CHUNKS
    up = v >= nv // 2
    first, last = gx == 0, gx == nx - 1
    not_first, not_last = gx > 0, gx < nx - 1
    edge = jnp.logical_or(first, last)
    upwind = lax.rem(v // (nv // 2) + gy, 2) == 1
    downwind = lax.rem(v // (nv // 2) + gy, 2) == 0
    roll_by = jnp.where(up, 1, 127)

    barrier = pltpu.get_barrier_semaphore()

    def greet(*dev):
        pl.semaphore_signal(barrier, inc=1, device_id=dev, device_id_type=MESH)

    for k in range(1, nv):
        greet(lax.rem(v + k, nv), gx, gy)
    greet(v, gx, 1 - gy)
    pl.when(not_first)(lambda: greet(v, gx - 1, gy))
    pl.when(not_last)(lambda: greet(v, gx + 1, gy))

    part = rows * 8 // CHUNKS

    def load(c):
        at = pl.ds(pl.multiple_of(c * part, part), part)
        return pltpu.make_async_copy(prev_h.at[at], prev.at[at], ld.at[c])

    def fetch(n):
        pair = ((relax_h, relax), (lrk_h, lrk), (btk_h, btk), (bti_h, bti), (lri_h, lri))[n]
        return pltpu.make_async_copy(*pair, small.at[n])

    fetch(0).start()
    for c in range(CHUNKS):
        load(c).start()
    for n in (1, 2, 3):
        fetch(n).start()
    pl.when(edge)(lambda: fetch(4).start())

    def remote(s, d, ss, rs, *dev):
        return pltpu.make_async_remote_copy(s, d, ss, rs, device_id=dev, device_id_type=MESH)

    hrow = rows // 2 // CHUNKS

    def halo(s, c, side):
        at = pl.ds(pl.multiple_of(c * hrow, hrow), hrow)
        if side == 0:
            return remote(sr.at[s, at], rr.at[s, at], r_s.at[s, c], r_r.at[s, c], v, gx + 1, gy)
        return remote(sl.at[s, at], rl.at[s, at], l_s.at[s, c], l_r.at[s, c], v, gx - 1, gy)

    def shalo(s, side):
        if side == 0:
            return remote(xsr.at[s], xrr.at[s], xr_s.at[s], xr_r.at[s], v, gx + 1, gy)
        return remote(xsl.at[s], xrl.at[s], xl_s.at[s], xl_r.at[s], v, gx - 1, gy)

    def yhalo(s):
        return remote(ysend.at[s], yrecv.at[s], y_s.at[s], y_r.at[s], v, gx, 1 - gy)

    def moment(k):
        return remote(moms, momr.at[k - 1], mom_s.at[k - 1], mom_r.at[k - 1], lax.rem(v + k, nv), gx, gy)

    def fluxx(s, k):
        return remote(fxs.at[s], fxr.at[s, k - 1], fx_s.at[s, k - 1], fx_r.at[s, k - 1], lax.rem(v + k, nv), gx, gy)

    half = nv // 2

    def fluxy(s, k):
        mine = lax.rem(v, half)
        return remote(fys.at[s], fyr.at[s, mine], fy_s.at[s, k], fy_r.at[s, mine], (1 - v // half) * half + k, gx, gy)

    def fluxy_in(s, k):
        return remote(fys.at[s], fyr.at[s, k], fy_s.at[s, k], fy_r.at[s, k], (1 - v // half) * half + k, gx, gy)

    lane = iota((8, 128), 1)
    sub = iota((8, 128), 0)
    cell = lax.rem(lane, 8)
    in_tile = lane // 8
    for t in range(4):
        vxl[t * 8 : t * 8 + 8, :] = ((t * 16 + in_tile).astype(F32) - (NVX - 1) / 2.0) * STEP
    for b in range(kyn * 4 // 8):
        t = b * 8 + sub
        ky = (v * kyn + t // 4).astype(F32)
        yy = (ky - (NVX - 1) / 2.0) * STEP
        xx = ((lax.rem(t, 4) * 16 + in_tile).astype(F32) - (NVX - 1) / 2.0) * STEP
        at = slice(b * 8, b * 8 + 8)
        mwy[at, :] = jnp.exp((xx * xx + yy * yy) * -0.5)
        wyt[at, :] = jnp.abs(yy) * FLUX_SCALE
    posn = jnp.where(up, lane, 127 - lane)
    want = sub + jnp.where(sub >= 4, 120, 0)
    sel = (posn == want).astype(F32)
    sel16 = sel.astype(BF16)
    sel_up = jnp.where(sub < 4, sel, 0.0)
    in_strip = posn < 4
    rep8 = (cell == sub).astype(F32)

    def gat(ky, off, stride=1):
        return pl.ds(ky * (NVX * PITCH) + off, 8, stride=stride)

    def pack_halo(ky, s):
        for q in range(0, HALF // 8, 2):
            right = [gmain[gat(ky, PITCH * (HALF + 8 * (q + d)) + 8, PITCH), :] for d in range(2)]
            left = [gmain[gat(ky, PITCH * 8 * (q + d), PITCH), :] for d in range(2)]
            at = pl.ds(pl.multiple_of(ky * HALF + q * 8, 16), 16)
            sr[s, at, :] = jnp.concatenate(right, axis=0).astype(BF16)
            sl[s, at, :] = jnp.concatenate(left, axis=0).astype(BF16)

    def send_chunk(s, c):
        pl.when(not_last)(lambda: halo(s, c, 0).start())
        pl.when(not_first)(lambda: halo(s, c, 1).start())

    def tile(ky, t):
        return pl.ds(pl.multiple_of(ky * 32 + t * 8, 8), 8)

    def take_row(ky, u):
        base = pl.multiple_of(ky * (NVX * 8), NVX * 8)
        s0 = s1 = s2 = jnp.zeros((8, 128), F32)
        for i in range(0, HALF, 2):
            pos = prev[pl.ds(base + (HALF + i) * 8, 16), :].astype(F32)
            neg = prev[pl.ds(base + (HALF - 2 - i) * 8, 16), :].astype(F32)
            for d in range(2):
                a, b = pos[8 * d : 8 * d + 8], neg[8 - 8 * d : 16 - 8 * d]
                gmain[gat(ky, PITCH * (HALF + i + d) + 1), :] = a
                gmain[gat(ky, PITCH * (HALF - 1 - i - d)), :] = b
                x = ABS[i + d]
                both = a + b
                s0 = s0 + both
                s1 = s1 + (a - b) * x
                s2 = s2 + both * (x * x)
        yy = ((v * kyn + ky).astype(F32) - (NVX - 1) / 2.0) * STEP
        got = dot_nt(sel16, prev[pl.ds(base, NVX * 8), :])
        for t in range(4):
            strip[tile(ky, t), :] = got[:, t * 128 : t * 128 + 128]
        pack_halo(ky, 0)
        return (u[0] + s0, u[1] + s1, u[2] + s0 * yy, u[3] + (s2 + s0 * (yy * yy)) * 0.5)

    def take_chunk(c, u):
        load(c).wait()
        u = lax.fori_loop(c * per, c * per + per, take_row, u)
        send_chunk(0, c)
        return u

    pl.semaphore_wait(barrier, nv + not_first.astype(jnp.int32) + not_last.astype(jnp.int32))
    zero = jnp.zeros((8, 128), F32)
    u = lax.fori_loop(0, CHUNKS, take_chunk, (zero, zero, zero, zero))
    for a in range(4):
        moms[a * 8 : a * 8 + 8, :] = u[a] * WEIGHT
    for k in range(1, nv):
        moment(k).start()

    groups = kyn // 4

    masks = [(lax.rem(iota((16, 128), 1), 8) == k).astype(F32).astype(BF16) for k in range(8)]

    def pair(a, b):
        return jnp.concatenate([a, b], axis=0).astype(BF16)

    def turn(a, by):
        return a if by % 128 == 0 else pltpu.roll(a, by % 128, 1)

    def pack_strips(s, g, tiles):
        right = left = None
        for k in range(8):
            r, h = k // 2, k % 2
            c = turn(pair(tiles[0, r, 2 + h], tiles[1, r, 2 + h]), k - 7) * masks[k]
            right = c if right is None else right + c
            c = turn(pair(tiles[0, r, h], tiles[1, r, h]), k) * masks[k]
            left = c if left is None else left + c
        at = pl.ds(pl.multiple_of(g * 16, 16), 16)
        xsr[s, at, :] = right
        xsl[s, at, :] = left

    def pack_first(g):
        pack_strips(
            0, g, {(n, r, t): strip[tile((g * 2 + n) * 4 + r, t), :] for n in range(2) for r in range(4) for t in range(4)}
        )

    def send_strips(s):
        pl.when(not_last)(lambda: shalo(s, 0).start())
        pl.when(not_first)(lambda: shalo(s, 1).start())

        acc = jnp.zeros((8, 128), F32)
        for b in range(0, kyn * 4 // 8, 2):
            two = []
            for d in range(2):
                row = strip[pl.ds((b + d) * 64 + 7, 8, stride=8), :]
                acc = acc + row * wyt[(b + d) * 8 : (b + d) * 8 + 8, :]
                two.append(row)
            ysend[s, b * 8 : b * 8 + 16, :] = jnp.concatenate(two, axis=0).astype(BF16)
        fys[s] = acc

        @pl.when(upwind)
        def _():
            yhalo(s).start()

        @pl.when(downwind)
        def _():
            for k in range(half):
                fluxy(s, k).start()

    def speed_rows(q, positive):
        j = (q * 8 + sub).astype(F32)
        return (j + 0.5) * STEP if positive else (HALF - 0.5 - j) * STEP

    def send_edges(s):
        def partial(rows_ref, tile_off, spot):
            def add(g, carry):
                main, thin = list(carry[:4]), list(carry[4:])
                for r in range(4):
                    ky = g * 4 + r
                    block = rows_ref[s, pl.ds(pl.multiple_of(ky * HALF, HALF), HALF), :].astype(F32)
                    for q in range(HALF // 8):
                        main[q] = main[q] + block[q * 8 : q * 8 + 8]
                    for h in range(2):
                        thin[h] = thin[h] + strip[tile(ky, tile_off + h), :]
                return (*main, *thin)

            got = lax.fori_loop(0, groups, add, (zero,) * 6)
            main = thin = zero
            for q in range(HALF // 8):
                main = main + got[q] * speed_rows(q, tile_off > 0)
            for h in range(2):
                x = jnp.abs(vxl[(tile_off + h) * 8 : (tile_off + h) * 8 + 8, :])
                thin = thin + got[4 + h] * jnp.where(cell == spot, x, 0.0)
            thin = jnp.broadcast_to(jnp.sum(thin, axis=1, keepdims=True), (8, 128)) * sel_up
            fxs[s] = (jnp.where(in_strip, 0.0, main) + thin) * FLUX_SCALE
            for k in range(1, nv):
                fluxx(s, k).start()

        pl.when(first)(lambda: partial(sl, 0, 0))
        pl.when(last)(lambda: partial(sr, 2, 7))

    loop(0, groups // 2, pack_first)
    send_strips(0)
    send_edges(0)

    fetch(0).wait()
    irel = 1.0 / relax[...]
    base_inv = DT_INV + irel

    def inv_of(m):
        for d in range(7):
            at = pl.ds(pl.multiple_of(m * 56 + d * 8, 8), 8)
            invd[at, :] = 1.0 / (base_inv + (m * 7 + (d + 1)).astype(F32) * STEP)

    loop(0, (NVX - 1) // 7, inv_of)

    permute = (iota((128, 128), 0) == lax.rem(iota((128, 128), 1), 8) * 16 + iota((128, 128), 1) // 8).astype(F32)
    fetch(1).wait()
    fetch(2).wait()
    fetch(3).wait()

    @pl.when(edge)
    def _():
        fetch(4).wait()
        side = jnp.where(first, 0, 1)
        off = jnp.where(first, HALF, 0)
        kind = jnp.broadcast_to(jnp.where(first, lrk[0:1, :], lrk[1:2, :]).astype(F32), (8, 128))
        kinds[0:8, :] = 1.0 - kind
        kind8 = jnp.broadcast_to(jnp.sum(kind * sel, axis=1, keepdims=True), (8, 128))
        kinds[8:16, :] = 1.0 - kind8

        def take(g):
            for r in range(4):
                ky = g * 4 + r
                at = pl.ds(pl.multiple_of((ky * NVX + off) * 2, 2 * HALF), 2 * HALF)
                src[pl.ds(pl.multiple_of(ky * 2 * HALF, 2 * HALF), 2 * HALF), :] = lri[at, :].astype(F32)
            for r in range(4):
                ky = g * 4 + r
                for q in range(HALF // 8):
                    at = pl.ds(pl.multiple_of(ky * HALF + q * 8, 8), 8)
                    inf[at, :] = src[pl.ds(ky * 2 * HALF + q * 16 + side, 8, stride=2), :]
            got = dot_nt(sel, inf[pl.ds(pl.multiple_of(g * 128, 128), 128), :])
            at = pl.ds(pl.multiple_of(g * 8, 8), 8)
            infp[at, :] = kind8 * jnp.dot(got, permute, preferred_element_type=F32)
            kyg = (v * kyn + g * 4 + cell // 2).astype(F32)
            kxg = (off // 16 * 16 + lax.rem(cell, 2) * 16 + in_tile).astype(F32)
            yy, xx = (kyg - (NVX - 1) / 2.0) * STEP, (kxg - (NVX - 1) / 2.0) * STEP
            mwp[at, :] = jnp.exp((xx * xx + yy * yy) * -0.5)
            for q in range(16):
                at = pl.ds(pl.multiple_of(g * 128 + q * 8, 8), 8)
                inf[at, :] = inf[at, :] * kind

        loop(0, groups, take)

    @pl.when(upwind)
    def _():
        block = jnp.where(up, bti[0].astype(F32), bti[1].astype(F32))
        stack = jnp.concatenate([block[:, b * 128 : b * 128 + 128] for b in range(rows // 128)], axis=0)
        kind = jnp.broadcast_to(jnp.where(up, btk[0:1, :], btk[1:2, :]).astype(F32), (8, 8))
        kind = jnp.dot(kind, rep8, preferred_element_type=F32)
        kinds[16:24, :] = 1.0 - kind
        for w in range(8):
            spread = (iota((128, 128), 0) == w * 16 + iota((128, 128), 1) // 8).astype(F32)
            wide = jnp.dot(stack, spread, preferred_element_type=F32)
            for b in range(rows // 128):
                one = jnp.where(cell == sub, wide[b * 8 : b * 8 + 8], 0.0) * kind
                yinf[b * 8 + w : b * 8 + w + 1, :] = jnp.sum(one, axis=0, keepdims=True)

    for k in range(1, nv):
        moment(k).wait_recv()
    u = [moms[a * 8 : a * 8 + 8, :] for a in range(4)]
    for k in range(nv - 1):
        u = [u[a] + momr[k, a * 8 : a * 8 + 8, :] for a in range(4)]
    p = start_params(u)
    p = lax.fori_loop(0, NEWTON, lambda n, q: newton_step(q, u), p)

    pq = p[3] * 0.5
    top_x = None
    for j, (x, plus, minus) in enumerate(one_dim(p[1], pq)):
        if x is None:
            top_x = plus
        else:
            afac[(HALF + j) * 8 : (HALF + j) * 8 + 8, :] = plus
            afac[(HALF - 1 - j) * 8 : (HALF - j) * 8, :] = minus
    height = p[0] + top_x

    thin = [
        dot_nt(sel, jnp.broadcast_to(a[None], (16, 8, 128)).reshape(128, 128), precision=lax.Precision.HIGHEST)
        for a in (*p, irel)
    ]

    def speed_y(ky):
        return ((v * kyn + ky).astype(F32) - (NVX - 1) / 2.0) * STEP

    def edge_flux(s):
        total = fxs[s]
        for k in range(nv - 1):
            total = total + fxr[s, k]
        return jnp.broadcast_to(jnp.sum(total, axis=0, keepdims=True), (8, 128))

    def sweep_strips(s):
        pl.when(not_first)(lambda: shalo(s, 0).wait_recv())
        pl.when(not_last)(lambda: shalo(s, 1).wait_recv())

        @pl.when(edge)
        def _():
            for k in range(1, nv):
                fluxx(s, k).wait_recv()
            flux = jnp.broadcast_to(jnp.sum(edge_flux(s) * sel, axis=1, keepdims=True), (8, 128)) * kinds[8:16, :]

            def fill(ref):
                ghost = [infp[g * 8 : g * 8 + 8, :] + flux * mwp[g * 8 : g * 8 + 8, :] for g in range(groups)]
                ref[s] = jnp.concatenate(ghost, axis=0).astype(BF16)

            pl.when(first)(lambda: fill(xrr))
            pl.when(last)(lambda: fill(xrl))

        @pl.when(downwind)
        def _():
            yhalo(s).wait_recv()
            yg[...] = yrecv[s].astype(F32)

        @pl.when(upwind)
        def _():
            for k in range(half):
                fluxy_in(s, k).wait_recv()
            total = fyr[s, 0]
            for k in range(1, half):
                total = total + fyr[s, k]
            flux = jnp.broadcast_to(jnp.sum(total, axis=0, keepdims=True), (8, 128))
            for k in (8, 16, 32, 64):
                flux = flux + pltpu.roll(flux, k, 1)
            flux = flux * kinds[16:24, :]
            for b in range(kyn * 4 // 8):
                at = slice(b * 8, b * 8 + 8)
                yg[at, :] = yinf[at, :] + flux * mwy[at, :]

        def step(g):
            at = pl.ds(pl.multiple_of(g * 16, 16), 16)
            right, left = xrr[s, at, :], xrl[s, at, :]
            tiles = {}
            for r in range(4):
                for t in range(4):
                    old = [strip[tile((g * 2 + n) * 4 + r, t), :] for n in range(2)]
                    moved = turn(pair(*old), 1 if t >= 2 else -1).astype(F32)
                    k = r * 2 + t % 2
                    ghost = (turn(right, -k) if t >= 2 else turn(left, 7 - k)).astype(F32)
                    hole = cell == (0 if t >= 2 else 7)
                    xx = vxl[t * 8 : t * 8 + 8, :]
                    ax = jnp.abs(xx)
                    for n in range(2):
                        ky = (g * 2 + n) * 4 + r
                        yy = speed_y(ky)
                        ay = jnp.abs(yy)
                        c = old[n]
                        if s == 0:
                            power = thin[0] + xx * thin[1] + yy * thin[2] + (xx * xx + yy * yy) * 0.5 * thin[3]
                            source = c * DT_INV + jnp.exp(power) * thin[4]
                            inv = 1.0 / (DT_INV + thin[4] + ax + ay)
                            ssrc[tile(ky, t), :] = source
                            sinv[tile(ky, t), :] = inv
                        else:
                            source = ssrc[tile(ky, t), :]
                            inv = sinv[tile(ky, t), :]
                        from_y = jnp.where(sub == 0, yg[pl.ds(ky * 4 + t, 1), :], pltpu.roll(c, 1, 0))
                        from_x = jnp.where(hole, ghost[n * 8 : n * 8 + 8], moved[n * 8 : n * 8 + 8])
                        new = (source + ax * from_x + ay * from_y) * inv
                        tiles[n, r, t] = new
            for (n, r, t), new in tiles.items():
                strip[tile((g * 2 + n) * 4 + r, t), :] = new
            if s < SWEEPS - 1:
                pack_strips(s + 1, g, tiles)

        loop(0, groups // 2, step)

    def next_edges(s):
        off = jnp.where(first, 0, PITCH * HALF + 8)
        beside = jnp.where(first, 1, -1)
        kx0 = jnp.where(first, 0, HALF)
        row = jnp.where(first, 0, 7)
        speeds = [jnp.where(first, speed_rows(q, False), speed_rows(q, True)) for q in range(HALF // 8)]
        pick = (sub == row).astype(F32)

        def row_of(a):
            return jnp.broadcast_to(jnp.sum(a * pick, axis=0, keepdims=True), (8, 128))

        inv_row = row_of(base_inv) if s == 0 else None

        def add(g, carry):
            main = list(carry[:4])
            thin_sum = list(carry[4:])
            for r in range(4):
                ky = g * 4 + r
                yy = speed_y(ky)
                ay = jnp.abs(yy)
                if s == 0:
                    bfac = row_of(b_of(yy))
                for q in range(0, HALF // 8, 2):
                    own = [gmain[gat(ky, off + PITCH * 8 * (q + d), PITCH), :] for d in range(2)]
                    turned = pltpu.roll(pair(*own), roll_by, 1).astype(F32)
                    for d in range(2):
                        moved = gmain[gat(ky, off + beside + PITCH * 8 * (q + d), PITCH), :]
                        at = pl.ds(pl.multiple_of(ky * HALF + (q + d) * 8, 8), 8)
                        ax = speeds[q + d]
                        if s == 0:
                            fac = afac[pl.ds((kx0 + 8 * (q + d)) * 8 + row, 8, stride=8), :]
                            source = own[d] * DT_INV + fac * bfac
                            inv = 1.0 / (inv_row + ax + ay)
                            esrc[at, :] = source
                            einv[at, :] = inv
                        else:
                            source = esrc[at, :]
                            inv = einv[at, :]
                        new = (source + ax * moved + ay * turned[d * 8 : d * 8 + 8]) * inv
                        main[q + d] = main[q + d] + new
                for h in range(2):
                    thin_sum[h] = thin_sum[h] + strip[tile(ky, kx0 // 16 + h), :]
            return (*main, *thin_sum)

        got = lax.fori_loop(0, groups, add, (zero,) * 6)
        main = thin = zero
        for q in range(HALF // 8):
            main = main + got[q] * speeds[q]
        for h in range(2):
            x = jnp.abs(vxl[pl.ds(pl.multiple_of((kx0 // 16 + h) * 8, 8), 8), :])
            thin = thin + got[4 + h] * jnp.where(cell == row, x, 0.0)
        thin = jnp.broadcast_to(jnp.sum(thin, axis=1, keepdims=True), (8, 128)) * sel_up
        fxs[s + 1] = (jnp.where(in_strip, 0.0, main) + thin) * FLUX_SCALE
        for k in range(1, nv):
            fluxx(s + 1, k).start()

    def fill_main(s, c):
        def put(ref, off):
            for r in range(per):
                ky = c * per + r
                block = ref[s, pl.ds(pl.multiple_of(ky * HALF, HALF), HALF), :].astype(F32)
                for q in range(HALF // 8):
                    gmain[gat(ky, off + PITCH * 8 * q, PITCH), :] = block[q * 8 : q * 8 + 8]

        @pl.when(not_first)
        def _():
            halo(s, c, 0).wait_recv()
            put(rr, PITCH * HALF)

        @pl.when(not_last)
        def _():
            halo(s, c, 1).wait_recv()
            put(rl, 8)

        @pl.when(edge)
        def _():
            flux = edge_flux(s) * kinds[0:8, :]

            def put_wall(positive, off):
                walls = []
                for q in range(HALF // 8):
                    x = speed_rows(q, positive)
                    walls.append(flux * jnp.exp(x * x * -0.5))
                for r in range(per):
                    ky = c * per + r
                    yy = speed_y(ky)
                    scale = jnp.exp(jnp.full((8, 128), yy * yy * -0.5))
                    for q in range(HALF // 8):
                        brought = inf[pl.ds(pl.multiple_of(ky * HALF + q * 8, 8), 8), :]
                        gmain[gat(ky, off + PITCH * 8 * q, PITCH), :] = brought + walls[q] * scale

            pl.when(first)(lambda: put_wall(True, PITCH * HALF))
            pl.when(last)(lambda: put_wall(False, 8))

    def main_row(ky, s, b_of):
        yy = speed_y(ky)
        ay = jnp.abs(yy)
        kyg = v * kyn + ky
        jj = jnp.where(kyg >= HALF, kyg - HALF, HALF - 1 - kyg)
        base = pl.multiple_of(ky * (NVX * 8), NVX * 8)
        if s == 0:
            bfac = b_of(yy)
        for i in range(0, HALF, 2):
            inv = [invd[pl.ds(pl.multiple_of((jj + i + d) * 8, 8), 8), :] for d in range(2)]
            owns = {}
            for positive in (True, False):
                for d in range(2):
                    kx = HALF + i + d if positive else HALF - 1 - i - d
                    owns[positive, d] = gmain[gat(ky, PITCH * kx + (1 if positive else 0)), :]
            turned = {}
            for positive in (True, False):
                pair = jnp.concatenate([owns[positive, d] for d in range(2)], axis=0).astype(BF16)
                turned[positive] = pltpu.roll(pair, roll_by, 1).astype(F32)
            for positive in (True, False):
                done = []
                for d in range(2):
                    kx = HALF + i + d if positive else HALF - 1 - i - d
                    own_off = PITCH * kx + (1 if positive else 0)
                    moved = gmain[gat(ky, PITCH * kx + (0 if positive else 1)), :]
                    at = pl.ds(base + kx * 8, 8)
                    if s == 0:
                        source = owns[positive, d] * DT_INV + afac[kx * 8 : kx * 8 + 8, :] * bfac
                        src[at, :] = source
                    else:
                        source = src[at, :]
                    beside = turned[positive][d * 8 : d * 8 + 8]
                    new = (source + moved * ABS[i + d] + beside * ay) * inv[d]
                    if s < SWEEPS - 1:
                        gmain[gat(ky, own_off), :] = new
                    else:
                        done.append(jnp.where(in_strip, ins[at, :], new))
                if s == SWEEPS - 1:
                    kx = HALF + i if positive else HALF - 2 - i
                    if not positive:
                        done = done[::-1]
                    prev[pl.ds(base + kx * 8, 16), :] = jnp.concatenate(done, axis=0).astype(BF16)

    def place(t):
        row = iota((128, 128), 0)
        hit = jnp.logical_and(row // 8 == t, lax.rem(row, 8) < 4)
        there = jnp.where(up, iota((128, 128), 1), 127 - iota((128, 128), 1))
        return jnp.logical_and(hit, there == lax.rem(row, 8)).astype(BF16)

    back = [place(t) for t in range(16)]

    def store(c):
        at = pl.ds(pl.multiple_of(c * part, part), part)
        return pltpu.make_async_copy(prev.at[at], out_h.at[at], st.at[c])

    size_y = jnp.abs(p[2])
    top_y = None
    for y in ABS:
        e = (size_y + pq * y) * y
        top_y = e if top_y is None else jnp.maximum(top_y, e)
    amp = jnp.exp(height + top_y) * irel

    def b_of(yy):
        return amp * jnp.exp((p[2] + pq * yy) * yy - top_y)

    for s in range(SWEEPS):
        sweep_strips(s)
        if s < SWEEPS - 1:
            send_strips(s + 1)
            pl.when(edge)(lambda: next_edges(s))
        else:

            def put(g):
                flat = strip[pl.ds(pl.multiple_of(g * 128, 128), 128), :].T.astype(BF16)
                for t in range(16):
                    at = pl.ds(pl.multiple_of(g * 2048 + t * 128, 128), 128)
                    ins[at, :] = jnp.dot(flat, back[t], preferred_element_type=F32)

            loop(0, groups, put)

        def chunk(c):
            fill_main(s, c)

            def one(ky):
                main_row(ky, s, b_of)
                if s < SWEEPS - 1:
                    pack_halo(ky, s + 1)

            loop(c * per, c * per + per, one)
            if s < SWEEPS - 1:
                send_chunk(s + 1, c)
            else:
                store(c).start()

        loop(0, CHUNKS, chunk)

    for k in range(1, nv):
        moment(k).wait_send()

    def drain(s):
        def both(c):
            pl.when(not_last)(lambda: halo(s, c, 0).wait_send())
            pl.when(not_first)(lambda: halo(s, c, 1).wait_send())

        loop(0, CHUNKS, both)
        pl.when(not_last)(lambda: shalo(s, 0).wait_send())
        pl.when(not_first)(lambda: shalo(s, 1).wait_send())
        pl.when(upwind)(lambda: yhalo(s).wait_send())

        @pl.when(downwind)
        def _():
            for k in range(half):
                fluxy(s, k).wait_send()

        @pl.when(edge)
        def _():
            for k in range(1, nv):
                fluxx(s, k).wait_send()


    loop(0, SWEEPS, drain)
    for c in range(CHUNKS):
        store(c).wait()


def body(previous, relax_time, left_right_kind, bottom_top_kind, left_right_inflow, bottom_top_inflow, *, sizes):
    nv, nx, ny = sizes
    rows, cx, cy = previous.shape
    kyn = rows // NVX
    thin = rows * 8 // 128 * 8
    dma = pltpu.SemaphoreType.DMA
    vm = pltpu.VMEM
    hr = rows // 2
    ur = kyn * 4
    xr = kyn * 2
    scratch = [
        vm((rows * 8, 128), BF16), vm((rows * PITCH, 128), F32), vm((rows * 8, 128), F32),
        vm((NVX * 8, 128), F32), vm((NVX * 8, 128), F32),
        vm((SWEEPS, hr, 128), BF16), vm((SWEEPS, hr, 128), BF16),
        vm((SWEEPS, hr, 128), BF16), vm((SWEEPS, hr, 128), BF16),
        vm((32, 128), F32), vm((nv - 1, 32, 128), F32),
        vm((thin, 128), F32), vm((thin, 128), F32), vm((thin, 128), F32),
        vm((ur, 128), F32),
        vm((SWEEPS, xr, 128), BF16), vm((SWEEPS, xr, 128), BF16),
        vm((SWEEPS, xr, 128), BF16), vm((SWEEPS, xr, 128), BF16),
        vm((hr, 128), F32), vm((hr, 128), F32),
        vm((SWEEPS, ur, 128), BF16), vm((SWEEPS, ur, 128), BF16),
        vm((SWEEPS, 8, 128), F32), vm((SWEEPS, nv // 2, 8, 128), F32),
        vm((SWEEPS, 8, 128), F32), vm((SWEEPS, nv - 1, 8, 128), F32),
        vm((hr, 128), F32), vm((xr, 128), F32), vm((xr, 128), F32),
        vm((ur, 128), F32), vm((ur, 128), F32), vm((ur, 128), F32),
        vm((32, 128), F32), vm((24, 128), F32), vm((rows * 8, 128), F32),
        vm((8, 128), F32), vm((2, 128), jnp.int32), vm((2, 8), jnp.int32),
        vm((rows * 2, 128), BF16), vm((2, 8, rows), BF16),
        dma((CHUNKS,)), dma((5,)), dma((CHUNKS,)), dma((nv - 1,)), dma((nv - 1,)),
        dma((SWEEPS, CHUNKS)), dma((SWEEPS, CHUNKS)), dma((SWEEPS, CHUNKS)), dma((SWEEPS, CHUNKS)),
        dma((SWEEPS,)), dma((SWEEPS,)), dma((SWEEPS,)), dma((SWEEPS,)),
        dma((SWEEPS,)), dma((SWEEPS,)), dma((SWEEPS, nv // 2)), dma((SWEEPS, nv // 2)),
        dma((SWEEPS, nv - 1)), dma((SWEEPS, nv - 1)),
    ]
    far = pl.BlockSpec(memory_space=pl.ANY)
    out = pl.pallas_call(
        functools.partial(kernel, nv, nx, ny, rows),
        out_shape=jax.ShapeDtypeStruct((rows * 8, 128), BF16),
        in_specs=[far] * 6,
        out_specs=far,
        scratch_shapes=scratch,
        compiler_params=pltpu.CompilerParams(
            collective_id=0, has_side_effects=True, vmem_limit_bytes=62 * 1024 * 1024
        ),
        name="bgk_step",
    )(
        previous.reshape(rows * 8, 128),
        relax_time,
        left_right_kind,
        bottom_top_kind,
        left_right_inflow.reshape(rows * 2, 128),
        bottom_top_inflow.transpose(1, 2, 0),
    )
    return out.reshape(rows, cx, cy)


def solution(mesh):
    sizes = (mesh.shape["vel"], mesh.shape["gx"], mesh.shape["gy"])
    return jax.shard_map(
        functools.partial(body, sizes=sizes),
        mesh=mesh,
        in_specs=(
            P("vel", "gx", "gy"),
            P("gx", "gy"),
            P(None, "gy"),
            P(None, "gx"),
            P("vel", None, "gy"),
            P("vel", None, "gx"),
        ),
        out_specs=P("vel", "gx", "gy"),
        check_vma=False,
    )
```

```python
import functools
import math

import jax
import jax.numpy as jnp
import numpy as np
from jax import lax
from jax.experimental import pallas as pl
from jax.experimental.pallas import tpu as pltpu
from jax.sharding import PartitionSpec as P

NVX = 64
HALF = NVX // 2
NEWTON = 2
SWEEPS = 4
CHUNKS = 4
STEP = 12.0 / NVX
WEIGHT = STEP * STEP / (2.0 * math.pi)
DT_INV = (NVX - 1) * STEP / 100.0
PITCH = 9

NODES = (np.arange(NVX) - (NVX - 1) / 2.0) * STEP
ABS = [float((j + 0.5) * STEP) for j in range(HALF)]
WALL_1D = np.exp(-NODES * NODES / 2.0)
WALL_NORM = float(np.sum(np.maximum(NODES, 0.0) * WALL_1D) * np.sum(WALL_1D) * WEIGHT)
FLUX_SCALE = WEIGHT / WALL_NORM

F32 = jnp.float32
BF16 = jnp.bfloat16
MESH = pl.DeviceIdType.MESH


def dot_nt(a, b, **kw):
    return lax.dot_general(a, b, (((1,), (1,)), ((), ())), preferred_element_type=F32, **kw)


def dot_tn(a, b, **kw):
    return lax.dot_general(a, b, (((0,), (0,)), ((), ())), preferred_element_type=F32, **kw)


def loop(low, high, step):
    lax.fori_loop(low, high, lambda n, carry: (step(n), carry)[1], 0)


def iota(shape, dim):
    return lax.broadcasted_iota(jnp.int32, shape, dim)


def one_dim(lin, quad):
    top = None
    size = jnp.abs(lin)
    for x in ABS:
        e = (size + quad * x) * x
        top = e if top is None else jnp.maximum(top, e)
    for x in ABS:
        even = quad * (x * x) - top
        odd = lin * x
        yield x, jnp.exp(even + odd), jnp.exp(even - odd)
    yield None, top, None


def power_sums(lin, quad):
    sums = [None] * 5
    top = None
    for x, plus, minus in one_dim(lin, quad):
        if x is None:
            top = plus
            break
        s, d = plus + minus, plus - minus
        for n in range(5):
            term = (s if n % 2 == 0 else d) * (x**n)
            sums[n] = term if sums[n] is None else sums[n] + term
    return sums, top


def start_params(u):
    rho = u[0]
    inv = 1.0 / rho
    ux, uy = u[1] * inv, u[2] * inv
    sq = ux * ux + uy * uy
    t = u[3] * inv - sq / 2.0
    it = 1.0 / t
    return jnp.log(rho * it) - sq * 0.5 * it, ux * it, uy * it, -it


def solve_four(hessian, gradient):
    m = [list(r) for r in hessian]
    t = list(gradient)
    inv = [None] * 4
    for p in range(4):
        inv[p] = 1.0 / m[p][p]
        for low in range(p + 1, 4):
            f = m[low][p] * inv[p]
            for c in range(p + 1, 4):
                m[low][c] = m[low][c] - f * m[p][c]
            t[low] = t[low] - f * t[p]
    r = [None] * 4
    for p in (3, 2, 1, 0):
        a = t[p]
        for c in range(p + 1, 4):
            a = a - m[p][c] * r[c]
        r[p] = a * inv[p]
    return r


def newton_step(p, u):
    s, top_x = power_sums(p[1], p[3] * 0.5)
    q, top_y = power_sums(p[2], p[3] * 0.5)
    c = jnp.exp(p[0] + top_x + top_y) * WEIGHT
    s = [c * a for a in s]
    w = [
        s[0] * q[0],
        s[1] * q[0],
        s[0] * q[1],
        (s[2] * q[0] + s[0] * q[2]) * 0.5,
        s[2] * q[0],
        s[1] * q[1],
        (s[3] * q[0] + s[1] * q[2]) * 0.5,
        s[0] * q[2],
        (s[2] * q[1] + s[0] * q[3]) * 0.5,
        (s[4] * q[0] + 2.0 * s[2] * q[2] + s[0] * q[4]) * 0.25,
    ]
    layout = [[0, 1, 2, 3], [1, 4, 5, 6], [2, 5, 7, 8], [3, 6, 8, 9]]
    corr = solve_four([[w[layout[a][b]] for b in range(4)] for a in range(4)], [w[a] - u[a] for a in range(4)])
    return tuple(p[a] - corr[a] for a in range(4))


def kernel(
    nv, nx, ny, rows,
    prev_h, relax_h, lrk_h, btk_h, lri_h, bti_h,
    out_h,
    prev, gmain, src, afac, invd, sr, sl, rr, rl, moms, momr,
    strip, ssrc, sinv, yg, xsr, xsl, xrr, xrl, esrc, einv, ysend, yrecv,
    fys, fyr, fxs, fxr, inf, infp, mwp, yinf, mwy, wyt, vxl, kinds, ins, flat, back,
    relax, lrk, btk, lri, bti,
    ld, small, st, mom_s, mom_r, r_s, r_r, l_s, l_r, xr_s, xr_r, xl_s, xl_r,
    y_s, y_r, fy_s, fy_r, fx_s, fx_r,
):
    v, gx, gy = lax.axis_index("vel"), lax.axis_index("gx"), lax.axis_index("gy")
    kyn = rows // NVX
    per = kyn // CHUNKS
    up = v >= nv // 2
    first, last = gx == 0, gx == nx - 1
    not_first, not_last = gx > 0, gx < nx - 1
    edge = jnp.logical_or(first, last)
    upwind = lax.rem(v // (nv // 2) + gy, 2) == 1
    downwind = lax.rem(v // (nv // 2) + gy, 2) == 0
    roll_by = jnp.where(up, 1, 127)

    barrier = pltpu.get_barrier_semaphore()

    def greet(*dev):
        pl.semaphore_signal(barrier, inc=1, device_id=dev, device_id_type=MESH)

    for k in range(1, nv):
        greet(lax.rem(v + k, nv), gx, gy)
    greet(v, gx, 1 - gy)
    pl.when(not_first)(lambda: greet(v, gx - 1, gy))
    pl.when(not_last)(lambda: greet(v, gx + 1, gy))

    part = rows * 8 // CHUNKS

    def load(c):
        at = pl.ds(pl.multiple_of(c * part, part), part)
        return pltpu.make_async_copy(prev_h.at[at], prev.at[at], ld.at[c])

    def fetch(n):
        pair = ((relax_h, relax), (lrk_h, lrk), (btk_h, btk), (bti_h, bti), (lri_h, lri))[n]
        return pltpu.make_async_copy(*pair, small.at[n])

    fetch(0).start()
    for c in range(CHUNKS):
        load(c).start()
    for n in (1, 2, 3):
        fetch(n).start()
    pl.when(edge)(lambda: fetch(4).start())

    def remote(s, d, ss, rs, *dev):
        return pltpu.make_async_remote_copy(s, d, ss, rs, device_id=dev, device_id_type=MESH)

    hrow = rows // 2 // CHUNKS

    def halo(s, c, side):
        at = pl.ds(pl.multiple_of(c * hrow, hrow), hrow)
        if side == 0:
            return remote(sr.at[s, at], rr.at[s, at], r_s.at[s, c], r_r.at[s, c], v, gx + 1, gy)
        return remote(sl.at[s, at], rl.at[s, at], l_s.at[s, c], l_r.at[s, c], v, gx - 1, gy)

    def shalo(s, side):
        if side == 0:
            return remote(xsr.at[s], xrr.at[s], xr_s.at[s], xr_r.at[s], v, gx + 1, gy)
        return remote(xsl.at[s], xrl.at[s], xl_s.at[s], xl_r.at[s], v, gx - 1, gy)

    def yhalo(s):
        return remote(ysend.at[s], yrecv.at[s], y_s.at[s], y_r.at[s], v, gx, 1 - gy)

    def moment(k):
        return remote(moms, momr.at[k - 1], mom_s.at[k - 1], mom_r.at[k - 1], lax.rem(v + k, nv), gx, gy)

    def fluxx(s, k):
        return remote(fxs.at[s], fxr.at[s, k - 1], fx_s.at[s, k - 1], fx_r.at[s, k - 1], lax.rem(v + k, nv), gx, gy)

    half = nv // 2

    def fluxy(s, k):
        mine = lax.rem(v, half)
        return remote(fys.at[s], fyr.at[s, mine], fy_s.at[s, k], fy_r.at[s, mine], (1 - v // half) * half + k, gx, gy)

    def fluxy_in(s, k):
        return remote(fys.at[s], fyr.at[s, k], fy_s.at[s, k], fy_r.at[s, k], (1 - v // half) * half + k, gx, gy)

    lane = iota((8, 128), 1)
    sub = iota((8, 128), 0)
    cell = lax.rem(lane, 8)
    in_tile = lane // 8
    for t in range(4):
        vxl[t * 8 : t * 8 + 8, :] = ((t * 16 + in_tile).astype(F32) - (NVX - 1) / 2.0) * STEP
    for b in range(kyn * 4 // 8):
        t = b * 8 + sub
        ky = (v * kyn + t // 4).astype(F32)
        yy = (ky - (NVX - 1) / 2.0) * STEP
        xx = ((lax.rem(t, 4) * 16 + in_tile).astype(F32) - (NVX - 1) / 2.0) * STEP
        at = slice(b * 8, b * 8 + 8)
        mwy[at, :] = jnp.exp((xx * xx + yy * yy) * -0.5)
        wyt[at, :] = jnp.abs(yy) * FLUX_SCALE
    posn = jnp.where(up, lane, 127 - lane)
    want = sub + jnp.where(sub >= 4, 120, 0)
    sel = (posn == want).astype(F32)
    sel16 = sel.astype(BF16)
    sel_up = jnp.where(sub < 4, sel, 0.0)
    in_strip = posn < 4
    rep8 = (cell == sub).astype(F32)

    def gat(ky, off, stride=1):
        return pl.ds(ky * (NVX * PITCH) + off, 8, stride=stride)

    def pack_halo(ky, s):
        for q in range(0, HALF // 8, 2):
            right = [gmain[gat(ky, PITCH * (HALF + 8 * (q + d)) + 8, PITCH), :] for d in range(2)]
            left = [gmain[gat(ky, PITCH * 8 * (q + d), PITCH), :] for d in range(2)]
            at = pl.ds(pl.multiple_of(ky * HALF + q * 8, 16), 16)
            sr[s, at, :] = jnp.concatenate(right, axis=0).astype(BF16)
            sl[s, at, :] = jnp.concatenate(left, axis=0).astype(BF16)

    def send_chunk(s, c):
        pl.when(not_last)(lambda: halo(s, c, 0).start())
        pl.when(not_first)(lambda: halo(s, c, 1).start())

    def tile(ky, t):
        return pl.ds(pl.multiple_of(ky * 32 + t * 8, 8), 8)

    def take_row(ky, u):
        base = pl.multiple_of(ky * (NVX * 8), NVX * 8)
        s0 = s1 = s2 = jnp.zeros((8, 128), F32)
        for i in range(0, HALF, 2):
            pos = prev[pl.ds(base + (HALF + i) * 8, 16), :].astype(F32)
            neg = prev[pl.ds(base + (HALF - 2 - i) * 8, 16), :].astype(F32)
            for d in range(2):
                a, b = pos[8 * d : 8 * d + 8], neg[8 - 8 * d : 16 - 8 * d]
                gmain[gat(ky, PITCH * (HALF + i + d) + 1), :] = a
                gmain[gat(ky, PITCH * (HALF - 1 - i - d)), :] = b
                x = ABS[i + d]
                both = a + b
                s0 = s0 + both
                s1 = s1 + (a - b) * x
                s2 = s2 + both * (x * x)
        yy = ((v * kyn + ky).astype(F32) - (NVX - 1) / 2.0) * STEP
        return (u[0] + s0, u[1] + s1, u[2] + s0 * yy, u[3] + (s2 + s0 * (yy * yy)) * 0.5)

    def take_chunk(c, u):
        load(c).wait()
        return lax.fori_loop(c * per, c * per + per, take_row, u)

    zero = jnp.zeros((8, 128), F32)
    u = lax.fori_loop(0, CHUNKS, take_chunk, (zero, zero, zero, zero))
    for a in range(4):
        moms[a * 8 : a * 8 + 8, :] = u[a] * WEIGHT
    pl.semaphore_wait(barrier, nv + not_first.astype(jnp.int32) + not_last.astype(jnp.int32))
    for k in range(1, nv):
        moment(k).start()

    def take_strip(g):
        for r in range(4):
            ky = g * 4 + r
            got = dot_nt(sel16, prev[pl.ds(pl.multiple_of(ky * (NVX * 8), NVX * 8), NVX * 8), :])
            for t in range(4):
                strip[tile(ky, t), :] = got[:, t * 128 : t * 128 + 128]

    loop(0, kyn // 4, take_strip)

    groups = kyn // 4

    masks = [(lax.rem(iota((16, 128), 1), 8) == k).astype(F32).astype(BF16) for k in range(8)]

    def pair(a, b):
        return jnp.concatenate([a, b], axis=0).astype(BF16)

    def turn(a, by):
        return a if by % 128 == 0 else pltpu.roll(a, by % 128, 1)

    def pack_strips(s, g, tiles):
        right = left = None
        for k in range(8):
            r, h = k // 2, k % 2
            c = turn(pair(tiles[0, r, 2 + h], tiles[1, r, 2 + h]), k - 7) * masks[k]
            right = c if right is None else right + c
            c = turn(pair(tiles[0, r, h], tiles[1, r, h]), k) * masks[k]
            left = c if left is None else left + c
        at = pl.ds(pl.multiple_of(g * 16, 16), 16)
        xsr[s, at, :] = right
        xsl[s, at, :] = left

    def pack_first(g):
        pack_strips(
            0, g, {(n, r, t): strip[tile((g * 2 + n) * 4 + r, t), :] for n in range(2) for r in range(4) for t in range(4)}
        )

    def send_strips(s):
        pl.when(not_last)(lambda: shalo(s, 0).start())
        pl.when(not_first)(lambda: shalo(s, 1).start())

        acc = jnp.zeros((8, 128), F32)
        for b in range(0, kyn * 4 // 8, 2):
            two = []
            for d in range(2):
                row = strip[pl.ds((b + d) * 64 + 7, 8, stride=8), :]
                acc = acc + row * wyt[(b + d) * 8 : (b + d) * 8 + 8, :]
                two.append(row)
            ysend[s, b * 8 : b * 8 + 16, :] = jnp.concatenate(two, axis=0).astype(BF16)
        fys[s] = acc

        @pl.when(upwind)
        def _():
            yhalo(s).start()

        @pl.when(downwind)
        def _():
            for k in range(half):
                fluxy(s, k).start()

    def speed_rows(q, positive):
        j = (q * 8 + sub).astype(F32)
        return (j + 0.5) * STEP if positive else (HALF - 0.5 - j) * STEP

    def send_edges(s):
        def partial(rows_ref, tile_off, spot):
            def add(g, carry):
                main, thin = list(carry[:4]), list(carry[4:])
                for r in range(4):
                    ky = g * 4 + r
                    block = rows_ref[s, pl.ds(pl.multiple_of(ky * HALF, HALF), HALF), :].astype(F32)
                    for q in range(HALF // 8):
                        main[q] = main[q] + block[q * 8 : q * 8 + 8]
                    for h in range(2):
                        thin[h] = thin[h] + strip[tile(ky, tile_off + h), :]
                return (*main, *thin)

            got = lax.fori_loop(0, groups, add, (zero,) * 6)
            main = thin = zero
            for q in range(HALF // 8):
                main = main + got[q] * speed_rows(q, tile_off > 0)
            for h in range(2):
                x = jnp.abs(vxl[(tile_off + h) * 8 : (tile_off + h) * 8 + 8, :])
                thin = thin + got[4 + h] * jnp.where(cell == spot, x, 0.0)
            thin = jnp.broadcast_to(jnp.sum(thin, axis=1, keepdims=True), (8, 128)) * sel_up
            fxs[s] = (jnp.where(in_strip, 0.0, main) + thin) * FLUX_SCALE
            for k in range(1, nv):
                fluxx(s, k).start()

        pl.when(first)(lambda: partial(sl, 0, 0))
        pl.when(last)(lambda: partial(sr, 2, 7))

    loop(0, groups // 2, pack_first)
    send_strips(0)

    def first_halo(c):
        for r in range(per):
            pack_halo(c * per + r, 0)
        send_chunk(0, c)

    loop(0, CHUNKS, first_halo)
    send_edges(0)

    fetch(0).wait()
    irel = 1.0 / relax[...]
    base_inv = DT_INV + irel

    def inv_of(m):
        for d in range(7):
            at = pl.ds(pl.multiple_of(m * 56 + d * 8, 8), 8)
            invd[at, :] = 1.0 / (base_inv + (m * 7 + (d + 1)).astype(F32) * STEP)

    loop(0, (NVX - 1) // 7, inv_of)

    def place(t):
        row, col = iota((128, 128), 0), iota((128, 128), 1)
        there = jnp.where(up, col, 127 - col)
        hit = jnp.logical_and(row == t * 8 + there, there < 4)
        back[pl.ds(pl.multiple_of(t * 128, 128), 128), :] = hit.astype(F32).astype(BF16)

    loop(0, 16, place)

    permute = (iota((128, 128), 0) == lax.rem(iota((128, 128), 1), 8) * 16 + iota((128, 128), 1) // 8).astype(F32)
    fetch(1).wait()
    fetch(2).wait()
    fetch(3).wait()

    @pl.when(edge)
    def _():
        fetch(4).wait()
        side = jnp.where(first, 0, 1)
        off = jnp.where(first, HALF, 0)
        kind = jnp.broadcast_to(jnp.where(first, lrk[0:1, :], lrk[1:2, :]).astype(F32), (8, 128))
        kinds[0:8, :] = 1.0 - kind
        kind8 = jnp.broadcast_to(jnp.sum(kind * sel, axis=1, keepdims=True), (8, 128))
        kinds[8:16, :] = 1.0 - kind8

        def take(g):
            for r in range(4):
                ky = g * 4 + r
                at = pl.ds(pl.multiple_of((ky * NVX + off) * 2, 2 * HALF), 2 * HALF)
                src[pl.ds(pl.multiple_of(ky * 2 * HALF, 2 * HALF), 2 * HALF), :] = lri[at, :].astype(F32)
            for r in range(4):
                ky = g * 4 + r
                for q in range(HALF // 8):
                    at = pl.ds(pl.multiple_of(ky * HALF + q * 8, 8), 8)
                    inf[at, :] = src[pl.ds(ky * 2 * HALF + q * 16 + side, 8, stride=2), :]
            got = dot_nt(sel, inf[pl.ds(pl.multiple_of(g * 128, 128), 128), :])
            at = pl.ds(pl.multiple_of(g * 8, 8), 8)
            infp[at, :] = kind8 * jnp.dot(got, permute, preferred_element_type=F32)
            kyg = (v * kyn + g * 4 + cell // 2).astype(F32)
            kxg = (off // 16 * 16 + lax.rem(cell, 2) * 16 + in_tile).astype(F32)
            yy, xx = (kyg - (NVX - 1) / 2.0) * STEP, (kxg - (NVX - 1) / 2.0) * STEP
            mwp[at, :] = jnp.exp((xx * xx + yy * yy) * -0.5)
            for q in range(16):
                at = pl.ds(pl.multiple_of(g * 128 + q * 8, 8), 8)
                inf[at, :] = inf[at, :] * kind

        loop(0, groups, take)

    @pl.when(upwind)
    def _():
        block = jnp.where(up, bti[0].astype(F32), bti[1].astype(F32))
        stack = jnp.concatenate([block[:, b * 128 : b * 128 + 128] for b in range(rows // 128)], axis=0)
        kind = jnp.broadcast_to(jnp.where(up, btk[0:1, :], btk[1:2, :]).astype(F32), (8, 8))
        kind = jnp.dot(kind, rep8, preferred_element_type=F32)
        kinds[16:24, :] = 1.0 - kind
        for w in range(8):
            spread = (iota((128, 128), 0) == w * 16 + iota((128, 128), 1) // 8).astype(F32)
            wide = jnp.dot(stack, spread, preferred_element_type=F32)
            for b in range(rows // 128):
                one = jnp.where(cell == sub, wide[b * 8 : b * 8 + 8], 0.0) * kind
                yinf[b * 8 + w : b * 8 + w + 1, :] = jnp.sum(one, axis=0, keepdims=True)

    for k in range(1, nv):
        moment(k).wait_recv()
    u = [moms[a * 8 : a * 8 + 8, :] for a in range(4)]
    for k in range(nv - 1):
        u = [u[a] + momr[k, a * 8 : a * 8 + 8, :] for a in range(4)]
    p = start_params(u)
    p = lax.fori_loop(0, NEWTON, lambda n, q: newton_step(q, u), p)

    pq = p[3] * 0.5
    top_x = None
    for j, (x, plus, minus) in enumerate(one_dim(p[1], pq)):
        if x is None:
            top_x = plus
        else:
            afac[(HALF + j) * 8 : (HALF + j) * 8 + 8, :] = plus
            afac[(HALF - 1 - j) * 8 : (HALF - j) * 8, :] = minus
    height = p[0] + top_x

    def three(a):
        high = a.astype(BF16)
        rest = a - high.astype(F32)
        mid = rest.astype(BF16)
        low = (rest - mid.astype(F32)).astype(BF16)
        return high, mid, low

    def eightfold(a):
        twice = jnp.concatenate([a, a], axis=0)
        return jnp.concatenate([twice] * 8, axis=0)

    split = [three(a) for a in (*p, irel)]
    wide = jnp.concatenate(
        [jnp.concatenate([eightfold(part[n]) for part in split], axis=0) for n in range(3)], axis=1
    )
    wide = dot_nt(jnp.concatenate([sel16] * 3, axis=1), wide)
    thin = [wide[:, a * 128 : a * 128 + 128] for a in range(5)]

    def speed_y(ky):
        return ((v * kyn + ky).astype(F32) - (NVX - 1) / 2.0) * STEP

    def edge_flux(s):
        total = fxs[s]
        for k in range(nv - 1):
            total = total + fxr[s, k]
        return jnp.broadcast_to(jnp.sum(total, axis=0, keepdims=True), (8, 128))

    def sweep_strips(s):
        pl.when(not_first)(lambda: shalo(s, 0).wait_recv())
        pl.when(not_last)(lambda: shalo(s, 1).wait_recv())

        @pl.when(edge)
        def _():
            for k in range(1, nv):
                fluxx(s, k).wait_recv()
            flux = jnp.broadcast_to(jnp.sum(edge_flux(s) * sel, axis=1, keepdims=True), (8, 128)) * kinds[8:16, :]

            def fill(ref):
                ghost = [infp[g * 8 : g * 8 + 8, :] + flux * mwp[g * 8 : g * 8 + 8, :] for g in range(groups)]
                ref[s] = jnp.concatenate(ghost, axis=0).astype(BF16)

            pl.when(first)(lambda: fill(xrr))
            pl.when(last)(lambda: fill(xrl))

        @pl.when(downwind)
        def _():
            yhalo(s).wait_recv()
            yg[...] = yrecv[s].astype(F32)

        @pl.when(upwind)
        def _():
            for k in range(half):
                fluxy_in(s, k).wait_recv()
            total = fyr[s, 0]
            for k in range(1, half):
                total = total + fyr[s, k]
            flux = jnp.broadcast_to(jnp.sum(total, axis=0, keepdims=True), (8, 128))
            for k in (8, 16, 32, 64):
                flux = flux + pltpu.roll(flux, k, 1)
            flux = flux * kinds[16:24, :]
            for b in range(kyn * 4 // 8):
                at = slice(b * 8, b * 8 + 8)
                yg[at, :] = yinf[at, :] + flux * mwy[at, :]

        def step(g):
            at = pl.ds(pl.multiple_of(g * 16, 16), 16)
            right, left = xrr[s, at, :], xrl[s, at, :]
            tiles = {}
            for r in range(4):
                for t in range(4):
                    old = [strip[tile((g * 2 + n) * 4 + r, t), :] for n in range(2)]
                    moved = turn(pair(*old), 1 if t >= 2 else -1).astype(F32)
                    k = r * 2 + t % 2
                    ghost = (turn(right, -k) if t >= 2 else turn(left, 7 - k)).astype(F32)
                    hole = cell == (0 if t >= 2 else 7)
                    xx = vxl[t * 8 : t * 8 + 8, :]
                    ax = jnp.abs(xx)
                    for n in range(2):
                        ky = (g * 2 + n) * 4 + r
                        yy = speed_y(ky)
                        ay = jnp.abs(yy)
                        c = old[n]
                        if s == 0:
                            power = thin[0] + xx * thin[1] + yy * thin[2] + (xx * xx + yy * yy) * 0.5 * thin[3]
                            source = c * DT_INV + jnp.exp(power) * thin[4]
                            inv = 1.0 / (DT_INV + thin[4] + ax + ay)
                            ssrc[tile(ky, t), :] = source
                            sinv[tile(ky, t), :] = inv
                        else:
                            source = ssrc[tile(ky, t), :]
                            inv = sinv[tile(ky, t), :]
                        from_y = jnp.where(sub == 0, yg[pl.ds(ky * 4 + t, 1), :], pltpu.roll(c, 1, 0))
                        from_x = jnp.where(hole, ghost[n * 8 : n * 8 + 8], moved[n * 8 : n * 8 + 8])
                        new = (source + ax * from_x + ay * from_y) * inv
                        tiles[n, r, t] = new
            for (n, r, t), new in tiles.items():
                strip[tile((g * 2 + n) * 4 + r, t), :] = new
            if s < SWEEPS - 1:
                pack_strips(s + 1, g, tiles)

        loop(0, groups // 2, step)

    def next_edges(s):
        off = jnp.where(first, 0, PITCH * HALF + 8)
        beside = jnp.where(first, 1, -1)
        kx0 = jnp.where(first, 0, HALF)
        row = jnp.where(first, 0, 7)
        speeds = [jnp.where(first, speed_rows(q, False), speed_rows(q, True)) for q in range(HALF // 8)]
        pick = (sub == row).astype(F32)

        def row_of(a):
            return jnp.broadcast_to(jnp.sum(a * pick, axis=0, keepdims=True), (8, 128))

        inv_row = row_of(base_inv) if s == 0 else None

        def add(g, carry):
            main = list(carry[:4])
            thin_sum = list(carry[4:])
            for r in range(4):
                ky = g * 4 + r
                yy = speed_y(ky)
                ay = jnp.abs(yy)
                if s == 0:
                    bfac = row_of(b_of(yy))
                for q in range(0, HALF // 8, 2):
                    own = [gmain[gat(ky, off + PITCH * 8 * (q + d), PITCH), :] for d in range(2)]
                    turned = pltpu.roll(pair(*own), roll_by, 1).astype(F32)
                    for d in range(2):
                        moved = gmain[gat(ky, off + beside + PITCH * 8 * (q + d), PITCH), :]
                        at = pl.ds(pl.multiple_of(ky * HALF + (q + d) * 8, 8), 8)
                        ax = speeds[q + d]
                        if s == 0:
                            fac = afac[pl.ds((kx0 + 8 * (q + d)) * 8 + row, 8, stride=8), :]
                            source = own[d] * DT_INV + fac * bfac
                            inv = 1.0 / (inv_row + ax + ay)
                            esrc[at, :] = source
                            einv[at, :] = inv
                        else:
                            source = esrc[at, :]
                            inv = einv[at, :]
                        new = (source + ax * moved + ay * turned[d * 8 : d * 8 + 8]) * inv
                        main[q + d] = main[q + d] + new
                for h in range(2):
                    thin_sum[h] = thin_sum[h] + strip[tile(ky, kx0 // 16 + h), :]
            return (*main, *thin_sum)

        got = lax.fori_loop(0, groups, add, (zero,) * 6)
        main = thin = zero
        for q in range(HALF // 8):
            main = main + got[q] * speeds[q]
        for h in range(2):
            x = jnp.abs(vxl[pl.ds(pl.multiple_of((kx0 // 16 + h) * 8, 8), 8), :])
            thin = thin + got[4 + h] * jnp.where(cell == row, x, 0.0)
        thin = jnp.broadcast_to(jnp.sum(thin, axis=1, keepdims=True), (8, 128)) * sel_up
        fxs[s + 1] = (jnp.where(in_strip, 0.0, main) + thin) * FLUX_SCALE
        for k in range(1, nv):
            fluxx(s + 1, k).start()

    def fill_main(s, c):
        def put(ref, off):
            for r in range(per):
                ky = c * per + r
                block = ref[s, pl.ds(pl.multiple_of(ky * HALF, HALF), HALF), :].astype(F32)
                for q in range(HALF // 8):
                    gmain[gat(ky, off + PITCH * 8 * q, PITCH), :] = block[q * 8 : q * 8 + 8]

        @pl.when(not_first)
        def _():
            halo(s, c, 0).wait_recv()
            put(rr, PITCH * HALF)

        @pl.when(not_last)
        def _():
            halo(s, c, 1).wait_recv()
            put(rl, 8)

        @pl.when(edge)
        def _():
            flux = edge_flux(s) * kinds[0:8, :]

            def put_wall(positive, off):
                walls = []
                for q in range(HALF // 8):
                    x = speed_rows(q, positive)
                    walls.append(flux * jnp.exp(x * x * -0.5))
                for r in range(per):
                    ky = c * per + r
                    yy = speed_y(ky)
                    scale = jnp.exp(jnp.full((8, 128), yy * yy * -0.5))
                    for q in range(HALF // 8):
                        brought = inf[pl.ds(pl.multiple_of(ky * HALF + q * 8, 8), 8), :]
                        gmain[gat(ky, off + PITCH * 8 * q, PITCH), :] = brought + walls[q] * scale

            pl.when(first)(lambda: put_wall(True, PITCH * HALF))
            pl.when(last)(lambda: put_wall(False, 8))

    def main_row(ky, s, b_of):
        yy = speed_y(ky)
        ay = jnp.abs(yy)
        kyg = v * kyn + ky
        jj = jnp.where(kyg >= HALF, kyg - HALF, HALF - 1 - kyg)
        base = pl.multiple_of(ky * (NVX * 8), NVX * 8)
        if s == 0:
            bfac = b_of(yy)
        for i in range(0, HALF, 2):
            inv = [invd[pl.ds(pl.multiple_of((jj + i + d) * 8, 8), 8), :] for d in range(2)]
            owns = {}
            for positive in (True, False):
                for d in range(2):
                    kx = HALF + i + d if positive else HALF - 1 - i - d
                    owns[positive, d] = gmain[gat(ky, PITCH * kx + (1 if positive else 0)), :]
            turned = {}
            for positive in (True, False):
                pair = jnp.concatenate([owns[positive, d] for d in range(2)], axis=0).astype(BF16)
                turned[positive] = pltpu.roll(pair, roll_by, 1).astype(F32)
            for positive in (True, False):
                done = []
                for d in range(2):
                    kx = HALF + i + d if positive else HALF - 1 - i - d
                    own_off = PITCH * kx + (1 if positive else 0)
                    moved = gmain[gat(ky, PITCH * kx + (0 if positive else 1)), :]
                    at = pl.ds(base + kx * 8, 8)
                    if s == 0:
                        source = owns[positive, d] * DT_INV + afac[kx * 8 : kx * 8 + 8, :] * bfac
                        src[at, :] = source
                    else:
                        source = src[at, :]
                    beside = turned[positive][d * 8 : d * 8 + 8]
                    new = (source + moved * ABS[i + d] + beside * ay) * inv[d]
                    if s < SWEEPS - 1:
                        gmain[gat(ky, own_off), :] = new
                    else:
                        done.append(jnp.where(in_strip, ins[at, :], new))
                if s == SWEEPS - 1:
                    kx = HALF + i if positive else HALF - 2 - i
                    if not positive:
                        done = done[::-1]
                    prev[pl.ds(base + kx * 8, 16), :] = jnp.concatenate(done, axis=0).astype(BF16)

    def bring_back(ky):
        these = flat[pl.ds(pl.multiple_of(ky // 4 * 128, 128), 128), :]
        for t in range(4):
            at = pl.ds(pl.multiple_of(ky * 512 + t * 128, 128), 128)
            weights = back[pl.ds(pl.multiple_of((lax.rem(ky, 4) * 4 + t) * 128, 128), 128), :]
            ins[at, :] = jnp.dot(these, weights, preferred_element_type=F32)

    def store(c):
        at = pl.ds(pl.multiple_of(c * part, part), part)
        return pltpu.make_async_copy(prev.at[at], out_h.at[at], st.at[c])

    size_y = jnp.abs(p[2])
    top_y = None
    for y in ABS:
        e = (size_y + pq * y) * y
        top_y = e if top_y is None else jnp.maximum(top_y, e)
    amp = jnp.exp(height + top_y) * irel

    def b_of(yy):
        return amp * jnp.exp((p[2] + pq * yy) * yy - top_y)

    for s in range(SWEEPS):
        sweep_strips(s)
        if s < SWEEPS - 1:
            send_strips(s + 1)
            pl.when(edge)(lambda: next_edges(s))
        else:

            for g in range(groups):
                flat[g * 128 : g * 128 + 128, :] = strip[g * 128 : g * 128 + 128, :].T.astype(BF16)
            bring_back(0)

        def chunk(c):
            fill_main(s, c)

            def one(ky):
                main_row(ky, s, b_of)
                if s == SWEEPS - 1:
                    bring_back(jnp.minimum(ky + 1, kyn - 1))
                if s < SWEEPS - 1:
                    pack_halo(ky, s + 1)

            loop(c * per, c * per + per, one)
            if s < SWEEPS - 1:
                send_chunk(s + 1, c)
            else:
                store(c).start()

        loop(0, CHUNKS, chunk)

    for k in range(1, nv):
        moment(k).wait_send()

    def drain(s):
        def both(c):
            pl.when(not_last)(lambda: halo(s, c, 0).wait_send())
            pl.when(not_first)(lambda: halo(s, c, 1).wait_send())

        loop(0, CHUNKS, both)
        pl.when(not_last)(lambda: shalo(s, 0).wait_send())
        pl.when(not_first)(lambda: shalo(s, 1).wait_send())
        pl.when(upwind)(lambda: yhalo(s).wait_send())

        @pl.when(downwind)
        def _():
            for k in range(half):
                fluxy(s, k).wait_send()

        @pl.when(edge)
        def _():
            for k in range(1, nv):
                fluxx(s, k).wait_send()


    loop(0, SWEEPS, drain)
    for c in range(CHUNKS):
        store(c).wait()


def body(previous, relax_time, left_right_kind, bottom_top_kind, left_right_inflow, bottom_top_inflow, *, sizes):
    nv, nx, ny = sizes
    rows, cx, cy = previous.shape
    kyn = rows // NVX
    thin = rows * 8 // 128 * 8
    dma = pltpu.SemaphoreType.DMA
    vm = pltpu.VMEM
    hr = rows // 2
    ur = kyn * 4
    xr = kyn * 2
    scratch = [
        vm((rows * 8, 128), BF16), vm((rows * PITCH, 128), F32), vm((rows * 8, 128), F32),
        vm((NVX * 8, 128), F32), vm((NVX * 8, 128), F32),
        vm((SWEEPS, hr, 128), BF16), vm((SWEEPS, hr, 128), BF16),
        vm((SWEEPS, hr, 128), BF16), vm((SWEEPS, hr, 128), BF16),
        vm((32, 128), F32), vm((nv - 1, 32, 128), F32),
        vm((thin, 128), F32), vm((thin, 128), F32), vm((thin, 128), F32),
        vm((ur, 128), F32),
        vm((SWEEPS, xr, 128), BF16), vm((SWEEPS, xr, 128), BF16),
        vm((SWEEPS, xr, 128), BF16), vm((SWEEPS, xr, 128), BF16),
        vm((hr, 128), F32), vm((hr, 128), F32),
        vm((SWEEPS, ur, 128), BF16), vm((SWEEPS, ur, 128), BF16),
        vm((SWEEPS, 8, 128), F32), vm((SWEEPS, nv // 2, 8, 128), F32),
        vm((SWEEPS, 8, 128), F32), vm((SWEEPS, nv - 1, 8, 128), F32),
        vm((hr, 128), F32), vm((xr, 128), F32), vm((xr, 128), F32),
        vm((ur, 128), F32), vm((ur, 128), F32), vm((ur, 128), F32),
        vm((32, 128), F32), vm((24, 128), F32), vm((rows * 8, 128), F32),
        vm((kyn * 32, 128), BF16), vm((2048, 128), BF16),
        vm((8, 128), F32), vm((2, 128), jnp.int32), vm((2, 8), jnp.int32),
        vm((rows * 2, 128), BF16), vm((2, 8, rows), BF16),
        dma((CHUNKS,)), dma((5,)), dma((CHUNKS,)), dma((nv - 1,)), dma((nv - 1,)),
        dma((SWEEPS, CHUNKS)), dma((SWEEPS, CHUNKS)), dma((SWEEPS, CHUNKS)), dma((SWEEPS, CHUNKS)),
        dma((SWEEPS,)), dma((SWEEPS,)), dma((SWEEPS,)), dma((SWEEPS,)),
        dma((SWEEPS,)), dma((SWEEPS,)), dma((SWEEPS, nv // 2)), dma((SWEEPS, nv // 2)),
        dma((SWEEPS, nv - 1)), dma((SWEEPS, nv - 1)),
    ]
    far = pl.BlockSpec(memory_space=pl.ANY)
    out = pl.pallas_call(
        functools.partial(kernel, nv, nx, ny, rows),
        out_shape=jax.ShapeDtypeStruct((rows * 8, 128), BF16),
        in_specs=[far] * 6,
        out_specs=far,
        scratch_shapes=scratch,
        compiler_params=pltpu.CompilerParams(
            collective_id=0, has_side_effects=True, vmem_limit_bytes=62 * 1024 * 1024
        ),
        name="bgk_step",
    )(
        previous.reshape(rows * 8, 128),
        relax_time,
        left_right_kind,
        bottom_top_kind,
        left_right_inflow.reshape(rows * 2, 128),
        bottom_top_inflow.transpose(1, 2, 0),
    )
    return out.reshape(rows, cx, cy)


def solution(mesh):
    sizes = (mesh.shape["vel"], mesh.shape["gx"], mesh.shape["gy"])
    return jax.shard_map(
        functools.partial(body, sizes=sizes),
        mesh=mesh,
        in_specs=(
            P("vel", "gx", "gy"),
            P("gx", "gy"),
            P(None, "gy"),
            P(None, "gx"),
            P("vel", None, "gy"),
            P("vel", None, "gx"),
        ),
        out_specs=P("vel", "gx", "gy"),
        check_vma=False,
    )
```

```python
import functools
import math

import jax
import jax.numpy as jnp
import numpy as np
from jax import lax
from jax.experimental import pallas as pl
from jax.experimental.pallas import tpu as pltpu
from jax.sharding import PartitionSpec as P

NVX = 64
HALF = NVX // 2
NEWTON = 2
SWEEPS = 4
CHUNKS = 4
PARTS = 8
STEP = 12.0 / NVX
WEIGHT = STEP * STEP / (2.0 * math.pi)
DT_INV = (NVX - 1) * STEP / 100.0
PITCH = 9

NODES = (np.arange(NVX) - (NVX - 1) / 2.0) * STEP
ABS = [float((j + 0.5) * STEP) for j in range(HALF)]
WALL_1D = np.exp(-NODES * NODES / 2.0)
WALL_NORM = float(np.sum(np.maximum(NODES, 0.0) * WALL_1D) * np.sum(WALL_1D) * WEIGHT)
FLUX_SCALE = WEIGHT / WALL_NORM

F32 = jnp.float32
BF16 = jnp.bfloat16
MESH = pl.DeviceIdType.MESH


def dot_nt(a, b, **kw):
    return lax.dot_general(a, b, (((1,), (1,)), ((), ())), preferred_element_type=F32, **kw)


def dot_tn(a, b, **kw):
    return lax.dot_general(a, b, (((0,), (0,)), ((), ())), preferred_element_type=F32, **kw)


def loop(low, high, step):
    lax.fori_loop(low, high, lambda n, carry: (step(n), carry)[1], 0)


def iota(shape, dim):
    return lax.broadcasted_iota(jnp.int32, shape, dim)


def one_dim(lin, quad):
    top = None
    size = jnp.abs(lin)
    for x in ABS:
        e = (size + quad * x) * x
        top = e if top is None else jnp.maximum(top, e)
    for x in ABS:
        even = quad * (x * x) - top
        odd = lin * x
        yield x, jnp.exp(even + odd), jnp.exp(even - odd)
    yield None, top, None


def power_sums(lin, quad):
    sums = [None] * 5
    top = None
    for x, plus, minus in one_dim(lin, quad):
        if x is None:
            top = plus
            break
        s, d = plus + minus, plus - minus
        for n in range(5):
            term = (s if n % 2 == 0 else d) * (x**n)
            sums[n] = term if sums[n] is None else sums[n] + term
    return sums, top


def start_params(u):
    rho = u[0]
    inv = 1.0 / rho
    ux, uy = u[1] * inv, u[2] * inv
    sq = ux * ux + uy * uy
    t = u[3] * inv - sq / 2.0
    it = 1.0 / t
    return jnp.log(rho * it) - sq * 0.5 * it, ux * it, uy * it, -it


def solve_four(hessian, gradient):
    m = [list(r) for r in hessian]
    t = list(gradient)
    inv = [None] * 4
    for p in range(4):
        inv[p] = 1.0 / m[p][p]
        for low in range(p + 1, 4):
            f = m[low][p] * inv[p]
            for c in range(p + 1, 4):
                m[low][c] = m[low][c] - f * m[p][c]
            t[low] = t[low] - f * t[p]
    r = [None] * 4
    for p in (3, 2, 1, 0):
        a = t[p]
        for c in range(p + 1, 4):
            a = a - m[p][c] * r[c]
        r[p] = a * inv[p]
    return r


def newton_step(p, u):
    s, top_x = power_sums(p[1], p[3] * 0.5)
    q, top_y = power_sums(p[2], p[3] * 0.5)
    c = jnp.exp(p[0] + top_x + top_y) * WEIGHT
    s = [c * a for a in s]
    w = [
        s[0] * q[0],
        s[1] * q[0],
        s[0] * q[1],
        (s[2] * q[0] + s[0] * q[2]) * 0.5,
        s[2] * q[0],
        s[1] * q[1],
        (s[3] * q[0] + s[1] * q[2]) * 0.5,
        s[0] * q[2],
        (s[2] * q[1] + s[0] * q[3]) * 0.5,
        (s[4] * q[0] + 2.0 * s[2] * q[2] + s[0] * q[4]) * 0.25,
    ]
    layout = [[0, 1, 2, 3], [1, 4, 5, 6], [2, 5, 7, 8], [3, 6, 8, 9]]
    corr = solve_four([[w[layout[a][b]] for b in range(4)] for a in range(4)], [w[a] - u[a] for a in range(4)])
    return tuple(p[a] - corr[a] for a in range(4))


def kernel(
    nv, nx, ny, rows,
    prev_h, relax_h, lrk_h, btk_h, lri_h, bti_h,
    out_h,
    prev, gmain, src, afac, invd, sr, sl, rr, rl, moms, momr,
    strip, ssrc, sinv, yg, xsr, xsl, xrr, xrl, esrc, einv, ysend, yrecv,
    fys, fyr, fxs, fxr, inf, infp, mwp, yinf, mwy, wyt, vxl, kinds, ins, flat, back,
    relax, lrk, btk, lri, bti,
    ld, small, st, mom_s, mom_r, r_s, r_r, l_s, l_r, xr_s, xr_r, xl_s, xl_r,
    y_s, y_r, fy_s, fy_r, fx_s, fx_r,
):
    v, gx, gy = lax.axis_index("vel"), lax.axis_index("gx"), lax.axis_index("gy")
    kyn = rows // NVX
    per = kyn // CHUNKS
    up = v >= nv // 2
    first, last = gx == 0, gx == nx - 1
    not_first, not_last = gx > 0, gx < nx - 1
    edge = jnp.logical_or(first, last)
    upwind = lax.rem(v // (nv // 2) + gy, 2) == 1
    downwind = lax.rem(v // (nv // 2) + gy, 2) == 0
    roll_by = jnp.where(up, 1, 127)

    barrier = pltpu.get_barrier_semaphore()

    def greet(*dev):
        pl.semaphore_signal(barrier, inc=1, device_id=dev, device_id_type=MESH)

    for k in range(1, nv):
        greet(lax.rem(v + k, nv), gx, gy)
    greet(v, gx, 1 - gy)
    pl.when(not_first)(lambda: greet(v, gx - 1, gy))
    pl.when(not_last)(lambda: greet(v, gx + 1, gy))

    part = rows * 8 // CHUNKS

    def load(c):
        at = pl.ds(pl.multiple_of(c * part, part), part)
        return pltpu.make_async_copy(prev_h.at[at], prev.at[at], ld.at[c])

    def fetch(n):
        pair = ((relax_h, relax), (lrk_h, lrk), (btk_h, btk), (bti_h, bti), (lri_h, lri))[n]
        return pltpu.make_async_copy(*pair, small.at[n])

    fetch(0).start()
    for c in range(CHUNKS):
        load(c).start()
    for n in (1, 2, 3):
        fetch(n).start()
    pl.when(edge)(lambda: fetch(4).start())

    def remote(s, d, ss, rs, *dev):
        return pltpu.make_async_remote_copy(s, d, ss, rs, device_id=dev, device_id_type=MESH)

    hrow = rows // 2 // CHUNKS

    def halo(s, c, side):
        at = pl.ds(pl.multiple_of(c * hrow, hrow), hrow)
        if side == 0:
            return remote(sr.at[s, at], rr.at[s, at], r_s.at[s, c], r_r.at[s, c], v, gx + 1, gy)
        return remote(sl.at[s, at], rl.at[s, at], l_s.at[s, c], l_r.at[s, c], v, gx - 1, gy)

    def shalo(s, side):
        if side == 0:
            return remote(xsr.at[s], xrr.at[s], xr_s.at[s], xr_r.at[s], v, gx + 1, gy)
        return remote(xsl.at[s], xrl.at[s], xl_s.at[s], xl_r.at[s], v, gx - 1, gy)

    def yhalo(s):
        return remote(ysend.at[s], yrecv.at[s], y_s.at[s], y_r.at[s], v, gx, 1 - gy)

    def moment(k):
        return remote(moms, momr.at[k - 1], mom_s.at[k - 1], mom_r.at[k - 1], lax.rem(v + k, nv), gx, gy)

    def fluxx(s, k):
        return remote(fxs.at[s], fxr.at[s, k - 1], fx_s.at[s, k - 1], fx_r.at[s, k - 1], lax.rem(v + k, nv), gx, gy)

    half = nv // 2

    def fluxy(s, k):
        mine = lax.rem(v, half)
        return remote(fys.at[s], fyr.at[s, mine], fy_s.at[s, k], fy_r.at[s, mine], (1 - v // half) * half + k, gx, gy)

    def fluxy_in(s, k):
        return remote(fys.at[s], fyr.at[s, k], fy_s.at[s, k], fy_r.at[s, k], (1 - v // half) * half + k, gx, gy)

    lane = iota((8, 128), 1)
    sub = iota((8, 128), 0)
    cell = lax.rem(lane, 8)
    in_tile = lane // 8
    for t in range(4):
        vxl[t * 8 : t * 8 + 8, :] = ((t * 16 + in_tile).astype(F32) - (NVX - 1) / 2.0) * STEP
    for b in range(kyn * 4 // 8):
        t = b * 8 + sub
        ky = (v * kyn + t // 4).astype(F32)
        yy = (ky - (NVX - 1) / 2.0) * STEP
        xx = ((lax.rem(t, 4) * 16 + in_tile).astype(F32) - (NVX - 1) / 2.0) * STEP
        at = slice(b * 8, b * 8 + 8)
        mwy[at, :] = jnp.exp((xx * xx + yy * yy) * -0.5)
        wyt[at, :] = jnp.abs(yy) * FLUX_SCALE
    posn = jnp.where(up, lane, 127 - lane)
    want = sub + jnp.where(sub >= 4, 120, 0)
    sel = (posn == want).astype(F32)
    sel16 = sel.astype(BF16)
    sel_up = jnp.where(sub < 4, sel, 0.0)
    in_strip = posn < 4
    rep8 = (cell == sub).astype(F32)

    def gat(ky, off, stride=1):
        return pl.ds(ky * (NVX * PITCH) + off, 8, stride=stride)

    def pack_halo(ky, s):
        for q in range(0, HALF // 8, 2):
            right = [gmain[gat(ky, PITCH * (HALF + 8 * (q + d)) + 8, PITCH), :] for d in range(2)]
            left = [gmain[gat(ky, PITCH * 8 * (q + d), PITCH), :] for d in range(2)]
            at = pl.ds(pl.multiple_of(ky * HALF + q * 8, 16), 16)
            sr[s, at, :] = jnp.concatenate(right, axis=0).astype(BF16)
            sl[s, at, :] = jnp.concatenate(left, axis=0).astype(BF16)

    def send_chunk(s, c):
        pl.when(not_last)(lambda: halo(s, c, 0).start())
        pl.when(not_first)(lambda: halo(s, c, 1).start())

    def tile(ky, t):
        return pl.ds(pl.multiple_of(ky * 32 + t * 8, 8), 8)

    def take_row(ky, u):
        base = pl.multiple_of(ky * (NVX * 8), NVX * 8)
        s0 = s1 = s2 = jnp.zeros((8, 128), F32)
        for i in range(0, HALF, 2):
            pos = prev[pl.ds(base + (HALF + i) * 8, 16), :].astype(F32)
            neg = prev[pl.ds(base + (HALF - 2 - i) * 8, 16), :].astype(F32)
            for d in range(2):
                a, b = pos[8 * d : 8 * d + 8], neg[8 - 8 * d : 16 - 8 * d]
                gmain[gat(ky, PITCH * (HALF + i + d) + 1), :] = a
                gmain[gat(ky, PITCH * (HALF - 1 - i - d)), :] = b
                x = ABS[i + d]
                both = a + b
                s0 = s0 + both
                s1 = s1 + (a - b) * x
                s2 = s2 + both * (x * x)
        yy = ((v * kyn + ky).astype(F32) - (NVX - 1) / 2.0) * STEP
        return (u[0] + s0, u[1] + s1, u[2] + s0 * yy, u[3] + (s2 + s0 * (yy * yy)) * 0.5)

    def take_chunk(c, u):
        load(c).wait()
        return lax.fori_loop(c * per, c * per + per, take_row, u)

    zero = jnp.zeros((8, 128), F32)
    u = lax.fori_loop(0, CHUNKS, take_chunk, (zero, zero, zero, zero))
    for a in range(4):
        moms[a * 8 : a * 8 + 8, :] = u[a] * WEIGHT
    pl.semaphore_wait(barrier, nv + not_first.astype(jnp.int32) + not_last.astype(jnp.int32))
    for k in range(1, nv):
        moment(k).start()

    def take_strip(g):
        for r in range(4):
            ky = g * 4 + r
            got = dot_nt(sel16, prev[pl.ds(pl.multiple_of(ky * (NVX * 8), NVX * 8), NVX * 8), :])
            for t in range(4):
                strip[tile(ky, t), :] = got[:, t * 128 : t * 128 + 128]

    loop(0, kyn // 4, take_strip)

    groups = kyn // 4

    masks = [(lax.rem(iota((16, 128), 1), 8) == k).astype(F32).astype(BF16) for k in range(8)]

    def pair(a, b):
        return jnp.concatenate([a, b], axis=0).astype(BF16)

    def turn(a, by):
        return a if by % 128 == 0 else pltpu.roll(a, by % 128, 1)

    def pack_strips(s, g, tiles):
        right = left = None
        for k in range(8):
            r, h = k // 2, k % 2
            c = turn(pair(tiles[0, r, 2 + h], tiles[1, r, 2 + h]), k - 7) * masks[k]
            right = c if right is None else right + c
            c = turn(pair(tiles[0, r, h], tiles[1, r, h]), k) * masks[k]
            left = c if left is None else left + c
        at = pl.ds(pl.multiple_of(g * 16, 16), 16)
        xsr[s, at, :] = right
        xsl[s, at, :] = left

    def pack_first(g):
        pack_strips(
            0, g, {(n, r, t): strip[tile((g * 2 + n) * 4 + r, t), :] for n in range(2) for r in range(4) for t in range(4)}
        )

    def send_strips(s):
        pl.when(not_last)(lambda: shalo(s, 0).start())
        pl.when(not_first)(lambda: shalo(s, 1).start())

        acc = jnp.zeros((8, 128), F32)
        for b in range(0, kyn * 4 // 8, 2):
            two = []
            for d in range(2):
                row = strip[pl.ds((b + d) * 64 + 7, 8, stride=8), :]
                acc = acc + row * wyt[(b + d) * 8 : (b + d) * 8 + 8, :]
                two.append(row)
            ysend[s, b * 8 : b * 8 + 16, :] = jnp.concatenate(two, axis=0).astype(BF16)
        fys[s] = acc

        @pl.when(upwind)
        def _():
            yhalo(s).start()

        @pl.when(downwind)
        def _():
            for k in range(half):
                fluxy(s, k).start()

    def speed_rows(q, positive):
        j = (q * 8 + sub).astype(F32)
        return (j + 0.5) * STEP if positive else (HALF - 0.5 - j) * STEP

    def send_edges(s):
        def partial(rows_ref, tile_off, spot):
            def add(g, carry):
                main, thin = list(carry[:4]), list(carry[4:])
                for r in range(4):
                    ky = g * 4 + r
                    block = rows_ref[s, pl.ds(pl.multiple_of(ky * HALF, HALF), HALF), :].astype(F32)
                    for q in range(HALF // 8):
                        main[q] = main[q] + block[q * 8 : q * 8 + 8]
                    for h in range(2):
                        thin[h] = thin[h] + strip[tile(ky, tile_off + h), :]
                return (*main, *thin)

            got = lax.fori_loop(0, groups, add, (zero,) * 6)
            main = thin = zero
            for q in range(HALF // 8):
                main = main + got[q] * speed_rows(q, tile_off > 0)
            for h in range(2):
                x = jnp.abs(vxl[(tile_off + h) * 8 : (tile_off + h) * 8 + 8, :])
                thin = thin + got[4 + h] * jnp.where(cell == spot, x, 0.0)
            thin = jnp.broadcast_to(jnp.sum(thin, axis=1, keepdims=True), (8, 128)) * sel_up
            fxs[s] = (jnp.where(in_strip, 0.0, main) + thin) * FLUX_SCALE
            for k in range(1, nv):
                fluxx(s, k).start()

        pl.when(first)(lambda: partial(sl, 0, 0))
        pl.when(last)(lambda: partial(sr, 2, 7))

    loop(0, groups // 2, pack_first)
    send_strips(0)

    def first_halo(c):
        for r in range(per):
            pack_halo(c * per + r, 0)
        send_chunk(0, c)

    loop(0, CHUNKS, first_halo)
    send_edges(0)

    fetch(0).wait()
    irel = 1.0 / relax[...]
    base_inv = DT_INV + irel

    def inv_of(m):
        for d in range(7):
            at = pl.ds(pl.multiple_of(m * 56 + d * 8, 8), 8)
            invd[at, :] = 1.0 / (base_inv + (m * 7 + (d + 1)).astype(F32) * STEP)

    loop(0, (NVX - 1) // 7, inv_of)

    def place(t):
        row, col = iota((128, 128), 0), iota((128, 128), 1)
        there = jnp.where(up, col, 127 - col)
        hit = jnp.logical_and(row == t * 8 + there, there < 4)
        back[pl.ds(pl.multiple_of(t * 128, 128), 128), :] = hit.astype(F32).astype(BF16)

    loop(0, 16, place)

    permute = (iota((128, 128), 0) == lax.rem(iota((128, 128), 1), 8) * 16 + iota((128, 128), 1) // 8).astype(F32)
    fetch(1).wait()
    fetch(2).wait()
    fetch(3).wait()

    @pl.when(edge)
    def _():
        fetch(4).wait()
        side = jnp.where(first, 0, 1)
        off = jnp.where(first, HALF, 0)
        kind = jnp.broadcast_to(jnp.where(first, lrk[0:1, :], lrk[1:2, :]).astype(F32), (8, 128))
        kinds[0:8, :] = 1.0 - kind
        kind8 = jnp.broadcast_to(jnp.sum(kind * sel, axis=1, keepdims=True), (8, 128))
        kinds[8:16, :] = 1.0 - kind8

        def take(g):
            for r in range(4):
                ky = g * 4 + r
                at = pl.ds(pl.multiple_of((ky * NVX + off) * 2, 2 * HALF), 2 * HALF)
                src[pl.ds(pl.multiple_of(ky * 2 * HALF, 2 * HALF), 2 * HALF), :] = lri[at, :].astype(F32)
            for r in range(4):
                ky = g * 4 + r
                for q in range(HALF // 8):
                    at = pl.ds(pl.multiple_of(ky * HALF + q * 8, 8), 8)
                    inf[at, :] = src[pl.ds(ky * 2 * HALF + q * 16 + side, 8, stride=2), :]
            got = dot_nt(sel, inf[pl.ds(pl.multiple_of(g * 128, 128), 128), :])
            at = pl.ds(pl.multiple_of(g * 8, 8), 8)
            infp[at, :] = kind8 * jnp.dot(got, permute, preferred_element_type=F32)
            kyg = (v * kyn + g * 4 + cell // 2).astype(F32)
            kxg = (off // 16 * 16 + lax.rem(cell, 2) * 16 + in_tile).astype(F32)
            yy, xx = (kyg - (NVX - 1) / 2.0) * STEP, (kxg - (NVX - 1) / 2.0) * STEP
            mwp[at, :] = jnp.exp((xx * xx + yy * yy) * -0.5)
            for q in range(16):
                at = pl.ds(pl.multiple_of(g * 128 + q * 8, 8), 8)
                inf[at, :] = inf[at, :] * kind

        loop(0, groups, take)

    @pl.when(upwind)
    def _():
        block = jnp.where(up, bti[0].astype(F32), bti[1].astype(F32))
        stack = jnp.concatenate([block[:, b * 128 : b * 128 + 128] for b in range(rows // 128)], axis=0)
        kind = jnp.broadcast_to(jnp.where(up, btk[0:1, :], btk[1:2, :]).astype(F32), (8, 8))
        kind = jnp.dot(kind, rep8, preferred_element_type=F32)
        kinds[16:24, :] = 1.0 - kind
        for w in range(8):
            spread = (iota((128, 128), 0) == w * 16 + iota((128, 128), 1) // 8).astype(F32)
            wide = jnp.dot(stack, spread, preferred_element_type=F32)
            for b in range(rows // 128):
                one = jnp.where(cell == sub, wide[b * 8 : b * 8 + 8], 0.0) * kind
                yinf[b * 8 + w : b * 8 + w + 1, :] = jnp.sum(one, axis=0, keepdims=True)

    for k in range(1, nv):
        moment(k).wait_recv()
    u = [moms[a * 8 : a * 8 + 8, :] for a in range(4)]
    for k in range(nv - 1):
        u = [u[a] + momr[k, a * 8 : a * 8 + 8, :] for a in range(4)]
    p = start_params(u)
    p = lax.fori_loop(0, NEWTON, lambda n, q: newton_step(q, u), p)

    pq = p[3] * 0.5
    top_x = None
    for j, (x, plus, minus) in enumerate(one_dim(p[1], pq)):
        if x is None:
            top_x = plus
        else:
            afac[(HALF + j) * 8 : (HALF + j) * 8 + 8, :] = plus
            afac[(HALF - 1 - j) * 8 : (HALF - j) * 8, :] = minus
    height = p[0] + top_x

    def three(a):
        high = a.astype(BF16)
        rest = a - high.astype(F32)
        mid = rest.astype(BF16)
        low = (rest - mid.astype(F32)).astype(BF16)
        return high, mid, low

    def eightfold(a):
        twice = jnp.concatenate([a, a], axis=0)
        return jnp.concatenate([twice] * 8, axis=0)

    split = [three(a) for a in (*p, irel)]
    wide = jnp.concatenate(
        [jnp.concatenate([eightfold(part[n]) for part in split], axis=0) for n in range(3)], axis=1
    )
    wide = dot_nt(jnp.concatenate([sel16] * 3, axis=1), wide)
    thin = [wide[:, a * 128 : a * 128 + 128] for a in range(5)]

    def speed_y(ky):
        return ((v * kyn + ky).astype(F32) - (NVX - 1) / 2.0) * STEP

    def edge_flux(s):
        total = fxs[s]
        for k in range(nv - 1):
            total = total + fxr[s, k]
        return jnp.broadcast_to(jnp.sum(total, axis=0, keepdims=True), (8, 128))

    def sweep_strips(s):
        pl.when(not_first)(lambda: shalo(s, 0).wait_recv())
        pl.when(not_last)(lambda: shalo(s, 1).wait_recv())

        @pl.when(edge)
        def _():
            for k in range(1, nv):
                fluxx(s, k).wait_recv()
            flux = jnp.broadcast_to(jnp.sum(edge_flux(s) * sel, axis=1, keepdims=True), (8, 128)) * kinds[8:16, :]

            def fill(ref):
                ghost = [infp[g * 8 : g * 8 + 8, :] + flux * mwp[g * 8 : g * 8 + 8, :] for g in range(groups)]
                ref[s] = jnp.concatenate(ghost, axis=0).astype(BF16)

            pl.when(first)(lambda: fill(xrr))
            pl.when(last)(lambda: fill(xrl))

        @pl.when(downwind)
        def _():
            yhalo(s).wait_recv()
            yg[...] = yrecv[s].astype(F32)

        @pl.when(upwind)
        def _():
            for k in range(half):
                fluxy_in(s, k).wait_recv()
            total = fyr[s, 0]
            for k in range(1, half):
                total = total + fyr[s, k]
            flux = jnp.broadcast_to(jnp.sum(total, axis=0, keepdims=True), (8, 128))
            for k in (8, 16, 32, 64):
                flux = flux + pltpu.roll(flux, k, 1)
            flux = flux * kinds[16:24, :]
            for b in range(kyn * 4 // 8):
                at = slice(b * 8, b * 8 + 8)
                yg[at, :] = yinf[at, :] + flux * mwy[at, :]

        def step(g):
            at = pl.ds(pl.multiple_of(g * 16, 16), 16)
            right, left = xrr[s, at, :], xrl[s, at, :]
            tiles = {}
            for r in range(4):
                for t in range(4):
                    old = [strip[tile((g * 2 + n) * 4 + r, t), :] for n in range(2)]
                    moved = turn(pair(*old), 1 if t >= 2 else -1).astype(F32)
                    k = r * 2 + t % 2
                    ghost = (turn(right, -k) if t >= 2 else turn(left, 7 - k)).astype(F32)
                    hole = cell == (0 if t >= 2 else 7)
                    xx = vxl[t * 8 : t * 8 + 8, :]
                    ax = jnp.abs(xx)
                    for n in range(2):
                        ky = (g * 2 + n) * 4 + r
                        yy = speed_y(ky)
                        ay = jnp.abs(yy)
                        c = old[n]
                        if s == 0:
                            power = thin[0] + xx * thin[1] + yy * thin[2] + (xx * xx + yy * yy) * 0.5 * thin[3]
                            source = c * DT_INV + jnp.exp(power) * thin[4]
                            inv = 1.0 / (DT_INV + thin[4] + ax + ay)
                            ssrc[tile(ky, t), :] = source
                            sinv[tile(ky, t), :] = inv
                        else:
                            source = ssrc[tile(ky, t), :]
                            inv = sinv[tile(ky, t), :]
                        from_y = jnp.where(sub == 0, yg[pl.ds(ky * 4 + t, 1), :], pltpu.roll(c, 1, 0))
                        from_x = jnp.where(hole, ghost[n * 8 : n * 8 + 8], moved[n * 8 : n * 8 + 8])
                        new = (source + ax * from_x + ay * from_y) * inv
                        tiles[n, r, t] = new
            for (n, r, t), new in tiles.items():
                strip[tile((g * 2 + n) * 4 + r, t), :] = new
            if s < SWEEPS - 1:
                pack_strips(s + 1, g, tiles)

        loop(0, groups // 2, step)

    def next_edges(s):
        off = jnp.where(first, 0, PITCH * HALF + 8)
        beside = jnp.where(first, 1, -1)
        kx0 = jnp.where(first, 0, HALF)
        row = jnp.where(first, 0, 7)
        speeds = [jnp.where(first, speed_rows(q, False), speed_rows(q, True)) for q in range(HALF // 8)]
        pick = (sub == row).astype(F32)

        def row_of(a):
            return jnp.broadcast_to(jnp.sum(a * pick, axis=0, keepdims=True), (8, 128))

        inv_row = row_of(base_inv) if s == 0 else None

        def add(g, carry):
            main = list(carry[:4])
            thin_sum = list(carry[4:])
            for r in range(4):
                ky = g * 4 + r
                yy = speed_y(ky)
                ay = jnp.abs(yy)
                if s == 0:
                    bfac = row_of(b_of(yy))
                for q in range(0, HALF // 8, 2):
                    own = [gmain[gat(ky, off + PITCH * 8 * (q + d), PITCH), :] for d in range(2)]
                    turned = pltpu.roll(pair(*own), roll_by, 1).astype(F32)
                    for d in range(2):
                        moved = gmain[gat(ky, off + beside + PITCH * 8 * (q + d), PITCH), :]
                        at = pl.ds(pl.multiple_of(ky * HALF + (q + d) * 8, 8), 8)
                        ax = speeds[q + d]
                        if s == 0:
                            fac = afac[pl.ds((kx0 + 8 * (q + d)) * 8 + row, 8, stride=8), :]
                            source = own[d] * DT_INV + fac * bfac
                            inv = 1.0 / (inv_row + ax + ay)
                            esrc[at, :] = source
                            einv[at, :] = inv
                        else:
                            source = esrc[at, :]
                            inv = einv[at, :]
                        new = (source + ax * moved + ay * turned[d * 8 : d * 8 + 8]) * inv
                        main[q + d] = main[q + d] + new
                for h in range(2):
                    thin_sum[h] = thin_sum[h] + strip[tile(ky, kx0 // 16 + h), :]
            return (*main, *thin_sum)

        got = lax.fori_loop(0, groups, add, (zero,) * 6)
        main = thin = zero
        for q in range(HALF // 8):
            main = main + got[q] * speeds[q]
        for h in range(2):
            x = jnp.abs(vxl[pl.ds(pl.multiple_of((kx0 // 16 + h) * 8, 8), 8), :])
            thin = thin + got[4 + h] * jnp.where(cell == row, x, 0.0)
        thin = jnp.broadcast_to(jnp.sum(thin, axis=1, keepdims=True), (8, 128)) * sel_up
        fxs[s + 1] = (jnp.where(in_strip, 0.0, main) + thin) * FLUX_SCALE
        for k in range(1, nv):
            fluxx(s + 1, k).start()

    def fill_main(s, c):
        def put(ref, off):
            for r in range(per):
                ky = c * per + r
                block = ref[s, pl.ds(pl.multiple_of(ky * HALF, HALF), HALF), :].astype(F32)
                for q in range(HALF // 8):
                    gmain[gat(ky, off + PITCH * 8 * q, PITCH), :] = block[q * 8 : q * 8 + 8]

        @pl.when(not_first)
        def _():
            halo(s, c, 0).wait_recv()
            put(rr, PITCH * HALF)

        @pl.when(not_last)
        def _():
            halo(s, c, 1).wait_recv()
            put(rl, 8)

        @pl.when(edge)
        def _():
            flux = edge_flux(s) * kinds[0:8, :]

            def put_wall(positive, off):
                walls = []
                for q in range(HALF // 8):
                    x = speed_rows(q, positive)
                    walls.append(flux * jnp.exp(x * x * -0.5))
                for r in range(per):
                    ky = c * per + r
                    yy = speed_y(ky)
                    scale = jnp.exp(jnp.full((8, 128), yy * yy * -0.5))
                    for q in range(HALF // 8):
                        brought = inf[pl.ds(pl.multiple_of(ky * HALF + q * 8, 8), 8), :]
                        gmain[gat(ky, off + PITCH * 8 * q, PITCH), :] = brought + walls[q] * scale

            pl.when(first)(lambda: put_wall(True, PITCH * HALF))
            pl.when(last)(lambda: put_wall(False, 8))

    def main_row(ky, s, b_of):
        yy = speed_y(ky)
        ay = jnp.abs(yy)
        kyg = v * kyn + ky
        jj = jnp.where(kyg >= HALF, kyg - HALF, HALF - 1 - kyg)
        base = pl.multiple_of(ky * (NVX * 8), NVX * 8)
        if s == 0:
            bfac = b_of(yy)
        for i in range(0, HALF, 2):
            inv = [invd[pl.ds(pl.multiple_of((jj + i + d) * 8, 8), 8), :] for d in range(2)]
            owns = {}
            for positive in (True, False):
                for d in range(2):
                    kx = HALF + i + d if positive else HALF - 1 - i - d
                    owns[positive, d] = gmain[gat(ky, PITCH * kx + (1 if positive else 0)), :]
            turned = {}
            for positive in (True, False):
                pair = jnp.concatenate([owns[positive, d] for d in range(2)], axis=0).astype(BF16)
                turned[positive] = pltpu.roll(pair, roll_by, 1).astype(F32)
            for positive in (True, False):
                done = []
                for d in range(2):
                    kx = HALF + i + d if positive else HALF - 1 - i - d
                    own_off = PITCH * kx + (1 if positive else 0)
                    moved = gmain[gat(ky, PITCH * kx + (0 if positive else 1)), :]
                    at = pl.ds(base + kx * 8, 8)
                    if s == 0:
                        source = owns[positive, d] * DT_INV + afac[kx * 8 : kx * 8 + 8, :] * bfac
                        src[at, :] = source
                    else:
                        source = src[at, :]
                    beside = turned[positive][d * 8 : d * 8 + 8]
                    new = (source + moved * ABS[i + d] + beside * ay) * inv[d]
                    if s < SWEEPS - 1:
                        gmain[gat(ky, own_off), :] = new
                    else:
                        done.append(jnp.where(in_strip, ins[at, :], new))
                if s == SWEEPS - 1:
                    kx = HALF + i if positive else HALF - 2 - i
                    if not positive:
                        done = done[::-1]
                    prev[pl.ds(base + kx * 8, 16), :] = jnp.concatenate(done, axis=0).astype(BF16)

    def bring_back(ky):
        these = flat[pl.ds(pl.multiple_of(ky // 4 * 128, 128), 128), :]
        for t in range(4):
            at = pl.ds(pl.multiple_of(ky * 512 + t * 128, 128), 128)
            weights = back[pl.ds(pl.multiple_of((lax.rem(ky, 4) * 4 + t) * 128, 128), 128), :]
            ins[at, :] = jnp.dot(these, weights, preferred_element_type=F32)

    def store(c):
        at = pl.ds(pl.multiple_of(c * part, part), part)
        return pltpu.make_async_copy(prev.at[at], out_h.at[at], st.at[c])

    size_y = jnp.abs(p[2])
    top_y = None
    for y in ABS:
        e = (size_y + pq * y) * y
        top_y = e if top_y is None else jnp.maximum(top_y, e)
    amp = jnp.exp(height + top_y) * irel

    def b_of(yy):
        return amp * jnp.exp((p[2] + pq * yy) * yy - top_y)

    for s in range(SWEEPS):
        sweep_strips(s)
        if s < SWEEPS - 1:
            send_strips(s + 1)
            pl.when(edge)(lambda: next_edges(s))
        else:

            for g in range(groups):
                flat[g * 128 : g * 128 + 128, :] = strip[g * 128 : g * 128 + 128, :].T.astype(BF16)
            bring_back(0)

        def chunk(c):
            fill_main(s, c)

            def one(ky):
                main_row(ky, s, b_of)
                if s == SWEEPS - 1:
                    bring_back(jnp.minimum(ky + 1, kyn - 1))
                if s < SWEEPS - 1:
                    pack_halo(ky, s + 1)

            loop(c * per, c * per + per, one)
            if s < SWEEPS - 1:
                send_chunk(s + 1, c)
            else:
                store(c).start()

        loop(0, CHUNKS, chunk)

    for k in range(1, nv):
        moment(k).wait_send()

    def drain(s):
        def both(c):
            pl.when(not_last)(lambda: halo(s, c, 0).wait_send())
            pl.when(not_first)(lambda: halo(s, c, 1).wait_send())

        loop(0, CHUNKS, both)
        pl.when(not_last)(lambda: shalo(s, 0).wait_send())
        pl.when(not_first)(lambda: shalo(s, 1).wait_send())
        pl.when(upwind)(lambda: yhalo(s).wait_send())

        @pl.when(downwind)
        def _():
            for k in range(half):
                fluxy(s, k).wait_send()

        @pl.when(edge)
        def _():
            for k in range(1, nv):
                fluxx(s, k).wait_send()


    loop(0, SWEEPS, drain)
    for c in range(CHUNKS):
        store(c).wait()


def hand_over(src_h, dst_h, held, come, go):
    part = src_h.shape[0] // PARTS

    def copy_in(n):
        at = pl.ds(n * part, part)
        return pltpu.make_async_copy(src_h.at[at], held.at[at], come.at[n])

    def copy_out(n):
        at = pl.ds(n * part, part)
        return pltpu.make_async_copy(held.at[at], dst_h.at[at], go.at[n])

    for n in range(PARTS):
        copy_in(n).start()
    for n in range(PARTS):
        copy_in(n).wait()
        copy_out(n).start()
    for n in range(PARTS):
        copy_out(n).wait()


def body(previous, relax_time, left_right_kind, bottom_top_kind, left_right_inflow, bottom_top_inflow, *, sizes):
    nv, nx, ny = sizes
    rows, cx, cy = previous.shape
    kyn = rows // NVX
    thin = rows * 8 // 128 * 8
    dma = pltpu.SemaphoreType.DMA
    vm = pltpu.VMEM
    hr = rows // 2
    ur = kyn * 4
    xr = kyn * 2
    scratch = [
        vm((rows * 8, 128), BF16), vm((rows * PITCH, 128), F32), vm((rows * 8, 128), F32),
        vm((NVX * 8, 128), F32), vm((NVX * 8, 128), F32),
        vm((SWEEPS, hr, 128), BF16), vm((SWEEPS, hr, 128), BF16),
        vm((SWEEPS, hr, 128), BF16), vm((SWEEPS, hr, 128), BF16),
        vm((32, 128), F32), vm((nv - 1, 32, 128), F32),
        vm((thin, 128), F32), vm((thin, 128), F32), vm((thin, 128), F32),
        vm((ur, 128), F32),
        vm((SWEEPS, xr, 128), BF16), vm((SWEEPS, xr, 128), BF16),
        vm((SWEEPS, xr, 128), BF16), vm((SWEEPS, xr, 128), BF16),
        vm((hr, 128), F32), vm((hr, 128), F32),
        vm((SWEEPS, ur, 128), BF16), vm((SWEEPS, ur, 128), BF16),
        vm((SWEEPS, 8, 128), F32), vm((SWEEPS, nv // 2, 8, 128), F32),
        vm((SWEEPS, 8, 128), F32), vm((SWEEPS, nv - 1, 8, 128), F32),
        vm((hr, 128), F32), vm((xr, 128), F32), vm((xr, 128), F32),
        vm((ur, 128), F32), vm((ur, 128), F32), vm((ur, 128), F32),
        vm((32, 128), F32), vm((24, 128), F32), vm((rows * 8, 128), F32),
        vm((kyn * 32, 128), BF16), vm((2048, 128), BF16),
        vm((8, 128), F32), vm((2, 128), jnp.int32), vm((2, 8), jnp.int32),
        vm((rows * 2, 128), BF16), vm((2, 8, rows), BF16),
        dma((CHUNKS,)), dma((5,)), dma((CHUNKS,)), dma((nv - 1,)), dma((nv - 1,)),
        dma((SWEEPS, CHUNKS)), dma((SWEEPS, CHUNKS)), dma((SWEEPS, CHUNKS)), dma((SWEEPS, CHUNKS)),
        dma((SWEEPS,)), dma((SWEEPS,)), dma((SWEEPS,)), dma((SWEEPS,)),
        dma((SWEEPS,)), dma((SWEEPS,)), dma((SWEEPS, nv // 2)), dma((SWEEPS, nv // 2)),
        dma((SWEEPS, nv - 1)), dma((SWEEPS, nv - 1)),
    ]
    far = pl.BlockSpec(memory_space=pl.ANY)
    out = pl.pallas_call(
        functools.partial(kernel, nv, nx, ny, rows),
        out_shape=jax.ShapeDtypeStruct((rows * 8, 128), BF16),
        in_specs=[far] * 6,
        out_specs=far,
        scratch_shapes=scratch,
        compiler_params=pltpu.CompilerParams(
            collective_id=0, has_side_effects=True, vmem_limit_bytes=62 * 1024 * 1024
        ),
        name="bgk_step",
    )(
        previous.reshape(rows * 8, 128),
        relax_time,
        left_right_kind,
        bottom_top_kind,
        left_right_inflow.reshape(rows * 2, 128),
        bottom_top_inflow.transpose(1, 2, 0),
    )
    out = pl.pallas_call(
        hand_over,
        out_shape=jax.ShapeDtypeStruct((rows * 8, 128), BF16),
        in_specs=[far],
        out_specs=far,
        scratch_shapes=[pltpu.VMEM((rows * 8, 128), BF16), pltpu.SemaphoreType.DMA((PARTS,)), pltpu.SemaphoreType.DMA((PARTS,))],
        compiler_params=pltpu.CompilerParams(vmem_limit_bytes=62 * 1024 * 1024),
        name="hand_over",
    )(out)
    return out.reshape(rows, cx, cy)


def solution(mesh):
    sizes = (mesh.shape["vel"], mesh.shape["gx"], mesh.shape["gy"])
    return jax.shard_map(
        functools.partial(body, sizes=sizes),
        mesh=mesh,
        in_specs=(
            P("vel", "gx", "gy"),
            P("gx", "gy"),
            P(None, "gy"),
            P(None, "gx"),
            P("vel", None, "gy"),
            P("vel", None, "gx"),
        ),
        out_specs=P("vel", "gx", "gy"),
        check_vma=False,
    )
```

```python
import functools
import math

import jax
import jax.numpy as jnp
import numpy as np
from jax import lax
from jax.experimental import pallas as pl
from jax.experimental.pallas import tpu as pltpu
from jax.sharding import PartitionSpec as P

NVX = 64
HALF = NVX // 2
NEWTON = 2
SWEEPS = 4
CHUNKS = 8
PARTS = 8
STEP = 12.0 / NVX
WEIGHT = STEP * STEP / (2.0 * math.pi)
DT_INV = (NVX - 1) * STEP / 100.0
PITCH = 9

NODES = (np.arange(NVX) - (NVX - 1) / 2.0) * STEP
ABS = [float((j + 0.5) * STEP) for j in range(HALF)]
WALL_1D = np.exp(-NODES * NODES / 2.0)
WALL_NORM = float(np.sum(np.maximum(NODES, 0.0) * WALL_1D) * np.sum(WALL_1D) * WEIGHT)
FLUX_SCALE = WEIGHT / WALL_NORM

F32 = jnp.float32
BF16 = jnp.bfloat16
MESH = pl.DeviceIdType.MESH


def dot_nt(a, b, **kw):
    return lax.dot_general(a, b, (((1,), (1,)), ((), ())), preferred_element_type=F32, **kw)


def dot_tn(a, b, **kw):
    return lax.dot_general(a, b, (((0,), (0,)), ((), ())), preferred_element_type=F32, **kw)


def loop(low, high, step):
    lax.fori_loop(low, high, lambda n, carry: (step(n), carry)[1], 0)


def iota(shape, dim):
    return lax.broadcasted_iota(jnp.int32, shape, dim)


def one_dim(lin, quad):
    top = None
    size = jnp.abs(lin)
    for x in ABS:
        e = (size + quad * x) * x
        top = e if top is None else jnp.maximum(top, e)
    for x in ABS:
        even = quad * (x * x) - top
        odd = lin * x
        yield x, jnp.exp(even + odd), jnp.exp(even - odd)
    yield None, top, None


def power_sums(lin, quad):
    sums = [None] * 5
    top = None
    for x, plus, minus in one_dim(lin, quad):
        if x is None:
            top = plus
            break
        s, d = plus + minus, plus - minus
        for n in range(5):
            term = (s if n % 2 == 0 else d) * (x**n)
            sums[n] = term if sums[n] is None else sums[n] + term
    return sums, top


def start_params(u):
    rho = u[0]
    inv = 1.0 / rho
    ux, uy = u[1] * inv, u[2] * inv
    sq = ux * ux + uy * uy
    t = u[3] * inv - sq / 2.0
    it = 1.0 / t
    return jnp.log(rho * it) - sq * 0.5 * it, ux * it, uy * it, -it


def solve_four(hessian, gradient):
    m = [list(r) for r in hessian]
    t = list(gradient)
    inv = [None] * 4
    for p in range(4):
        inv[p] = 1.0 / m[p][p]
        for low in range(p + 1, 4):
            f = m[low][p] * inv[p]
            for c in range(p + 1, 4):
                m[low][c] = m[low][c] - f * m[p][c]
            t[low] = t[low] - f * t[p]
    r = [None] * 4
    for p in (3, 2, 1, 0):
        a = t[p]
        for c in range(p + 1, 4):
            a = a - m[p][c] * r[c]
        r[p] = a * inv[p]
    return r


def newton_step(p, u):
    s, top_x = power_sums(p[1], p[3] * 0.5)
    q, top_y = power_sums(p[2], p[3] * 0.5)
    c = jnp.exp(p[0] + top_x + top_y) * WEIGHT
    s = [c * a for a in s]
    w = [
        s[0] * q[0],
        s[1] * q[0],
        s[0] * q[1],
        (s[2] * q[0] + s[0] * q[2]) * 0.5,
        s[2] * q[0],
        s[1] * q[1],
        (s[3] * q[0] + s[1] * q[2]) * 0.5,
        s[0] * q[2],
        (s[2] * q[1] + s[0] * q[3]) * 0.5,
        (s[4] * q[0] + 2.0 * s[2] * q[2] + s[0] * q[4]) * 0.25,
    ]
    layout = [[0, 1, 2, 3], [1, 4, 5, 6], [2, 5, 7, 8], [3, 6, 8, 9]]
    corr = solve_four([[w[layout[a][b]] for b in range(4)] for a in range(4)], [w[a] - u[a] for a in range(4)])
    return tuple(p[a] - corr[a] for a in range(4))


def kernel(
    nv, nx, ny, rows,
    prev_h, relax_h, lrk_h, btk_h, lri_h, bti_h,
    out_h,
    prev, gmain, src, afac, invd, sr, sl, rr, rl, moms, momr,
    strip, ssrc, sinv, yg, xsr, xsl, xrr, xrl, esrc, einv, ysend, yrecv,
    fys, fyr, fxs, fxr, inf, infp, mwp, yinf, mwy, wyt, vxl, kinds, ins, flat, back,
    relax, lrk, btk, lri, bti,
    ld, small, st, mom_s, mom_r, r_s, r_r, l_s, l_r, xr_s, xr_r, xl_s, xl_r,
    y_s, y_r, fy_s, fy_r, fx_s, fx_r,
):
    v, gx, gy = lax.axis_index("vel"), lax.axis_index("gx"), lax.axis_index("gy")
    kyn = rows // NVX
    per = kyn // CHUNKS
    up = v >= nv // 2
    first, last = gx == 0, gx == nx - 1
    not_first, not_last = gx > 0, gx < nx - 1
    edge = jnp.logical_or(first, last)
    upwind = lax.rem(v // (nv // 2) + gy, 2) == 1
    downwind = lax.rem(v // (nv // 2) + gy, 2) == 0
    roll_by = jnp.where(up, 1, 127)

    barrier = pltpu.get_barrier_semaphore()

    def greet(*dev):
        pl.semaphore_signal(barrier, inc=1, device_id=dev, device_id_type=MESH)

    for k in range(1, nv):
        greet(lax.rem(v + k, nv), gx, gy)
    greet(v, gx, 1 - gy)
    pl.when(not_first)(lambda: greet(v, gx - 1, gy))
    pl.when(not_last)(lambda: greet(v, gx + 1, gy))

    part = rows * 8 // CHUNKS

    def load(c):
        at = pl.ds(pl.multiple_of(c * part, part), part)
        return pltpu.make_async_copy(prev_h.at[at], prev.at[at], ld.at[c])

    def fetch(n):
        pair = ((relax_h, relax), (lrk_h, lrk), (btk_h, btk), (bti_h, bti), (lri_h, lri))[n]
        return pltpu.make_async_copy(*pair, small.at[n])

    fetch(0).start()
    for c in range(CHUNKS):
        load(c).start()
    for n in (1, 2, 3):
        fetch(n).start()
    pl.when(edge)(lambda: fetch(4).start())

    def remote(s, d, ss, rs, *dev):
        return pltpu.make_async_remote_copy(s, d, ss, rs, device_id=dev, device_id_type=MESH)

    hrow = rows // 2 // CHUNKS

    def halo(s, c, side):
        at = pl.ds(pl.multiple_of(c * hrow, hrow), hrow)
        if side == 0:
            return remote(sr.at[s, at], rr.at[s, at], r_s.at[s, c], r_r.at[s, c], v, gx + 1, gy)
        return remote(sl.at[s, at], rl.at[s, at], l_s.at[s, c], l_r.at[s, c], v, gx - 1, gy)

    def shalo(s, side):
        if side == 0:
            return remote(xsr.at[s], xrr.at[s], xr_s.at[s], xr_r.at[s], v, gx + 1, gy)
        return remote(xsl.at[s], xrl.at[s], xl_s.at[s], xl_r.at[s], v, gx - 1, gy)

    def yhalo(s):
        return remote(ysend.at[s], yrecv.at[s], y_s.at[s], y_r.at[s], v, gx, 1 - gy)

    def moment(k):
        return remote(moms, momr.at[k - 1], mom_s.at[k - 1], mom_r.at[k - 1], lax.rem(v + k, nv), gx, gy)

    def fluxx(s, k):
        return remote(fxs.at[s], fxr.at[s, k - 1], fx_s.at[s, k - 1], fx_r.at[s, k - 1], lax.rem(v + k, nv), gx, gy)

    half = nv // 2

    def fluxy(s, k):
        mine = lax.rem(v, half)
        return remote(fys.at[s], fyr.at[s, mine], fy_s.at[s, k], fy_r.at[s, mine], (1 - v // half) * half + k, gx, gy)

    def fluxy_in(s, k):
        return remote(fys.at[s], fyr.at[s, k], fy_s.at[s, k], fy_r.at[s, k], (1 - v // half) * half + k, gx, gy)

    lane = iota((8, 128), 1)
    sub = iota((8, 128), 0)
    cell = lax.rem(lane, 8)
    in_tile = lane // 8
    for t in range(4):
        vxl[t * 8 : t * 8 + 8, :] = ((t * 16 + in_tile).astype(F32) - (NVX - 1) / 2.0) * STEP
    for b in range(kyn * 4 // 8):
        t = b * 8 + sub
        ky = (v * kyn + t // 4).astype(F32)
        yy = (ky - (NVX - 1) / 2.0) * STEP
        xx = ((lax.rem(t, 4) * 16 + in_tile).astype(F32) - (NVX - 1) / 2.0) * STEP
        at = slice(b * 8, b * 8 + 8)
        mwy[at, :] = jnp.exp((xx * xx + yy * yy) * -0.5)
        wyt[at, :] = jnp.abs(yy) * FLUX_SCALE
    posn = jnp.where(up, lane, 127 - lane)
    want = sub + jnp.where(sub >= 4, 120, 0)
    sel = (posn == want).astype(F32)
    sel16 = sel.astype(BF16)
    sel_up = jnp.where(sub < 4, sel, 0.0)
    in_strip = posn < 4
    rep8 = (cell == sub).astype(F32)

    def gat(ky, off, stride=1):
        return pl.ds(ky * (NVX * PITCH) + off, 8, stride=stride)

    def pack_halo(ky, s):
        for q in range(0, HALF // 8, 2):
            right = [gmain[gat(ky, PITCH * (HALF + 8 * (q + d)) + 8, PITCH), :] for d in range(2)]
            left = [gmain[gat(ky, PITCH * 8 * (q + d), PITCH), :] for d in range(2)]
            at = pl.ds(pl.multiple_of(ky * HALF + q * 8, 16), 16)
            sr[s, at, :] = jnp.concatenate(right, axis=0).astype(BF16)
            sl[s, at, :] = jnp.concatenate(left, axis=0).astype(BF16)

    def send_chunk(s, c):
        pl.when(not_last)(lambda: halo(s, c, 0).start())
        pl.when(not_first)(lambda: halo(s, c, 1).start())

    def tile(ky, t):
        return pl.ds(pl.multiple_of(ky * 32 + t * 8, 8), 8)

    def take_row(ky, u):
        base = pl.multiple_of(ky * (NVX * 8), NVX * 8)
        s0 = s1 = s2 = jnp.zeros((8, 128), F32)
        for i in range(0, HALF, 2):
            pos = prev[pl.ds(base + (HALF + i) * 8, 16), :].astype(F32)
            neg = prev[pl.ds(base + (HALF - 2 - i) * 8, 16), :].astype(F32)
            for d in range(2):
                a, b = pos[8 * d : 8 * d + 8], neg[8 - 8 * d : 16 - 8 * d]
                gmain[gat(ky, PITCH * (HALF + i + d) + 1), :] = a
                gmain[gat(ky, PITCH * (HALF - 1 - i - d)), :] = b
                x = ABS[i + d]
                both = a + b
                s0 = s0 + both
                s1 = s1 + (a - b) * x
                s2 = s2 + both * (x * x)
        yy = ((v * kyn + ky).astype(F32) - (NVX - 1) / 2.0) * STEP
        return (u[0] + s0, u[1] + s1, u[2] + s0 * yy, u[3] + (s2 + s0 * (yy * yy)) * 0.5)

    def take_chunk(c, u):
        load(c).wait()
        for r in range(per):
            u = take_row(c * per + r, u)
        return u

    zero = jnp.zeros((8, 128), F32)
    u = lax.fori_loop(0, CHUNKS, take_chunk, (zero, zero, zero, zero))
    for a in range(4):
        moms[a * 8 : a * 8 + 8, :] = u[a] * WEIGHT
    pl.semaphore_wait(barrier, nv + not_first.astype(jnp.int32) + not_last.astype(jnp.int32))
    for k in range(1, nv):
        moment(k).start()

    def take_strip(g):
        for r in range(4):
            ky = g * 4 + r
            got = dot_nt(sel16, prev[pl.ds(pl.multiple_of(ky * (NVX * 8), NVX * 8), NVX * 8), :])
            for t in range(4):
                strip[tile(ky, t), :] = got[:, t * 128 : t * 128 + 128]

    loop(0, kyn // 4, take_strip)

    groups = kyn // 4

    masks = [(lax.rem(iota((16, 128), 1), 8) == k).astype(F32).astype(BF16) for k in range(8)]

    def pair(a, b):
        return jnp.concatenate([a, b], axis=0).astype(BF16)

    def turn(a, by):
        return a if by % 128 == 0 else pltpu.roll(a, by % 128, 1)

    def pack_strips(s, g, tiles):
        right = left = None
        for k in range(8):
            r, h = k // 2, k % 2
            c = turn(pair(tiles[0, r, 2 + h], tiles[1, r, 2 + h]), k - 7) * masks[k]
            right = c if right is None else right + c
            c = turn(pair(tiles[0, r, h], tiles[1, r, h]), k) * masks[k]
            left = c if left is None else left + c
        at = pl.ds(pl.multiple_of(g * 16, 16), 16)
        xsr[s, at, :] = right
        xsl[s, at, :] = left

    def pack_first(g):
        pack_strips(
            0, g, {(n, r, t): strip[tile((g * 2 + n) * 4 + r, t), :] for n in range(2) for r in range(4) for t in range(4)}
        )

    def send_strips(s):
        pl.when(not_last)(lambda: shalo(s, 0).start())
        pl.when(not_first)(lambda: shalo(s, 1).start())

        acc = jnp.zeros((8, 128), F32)
        for b in range(0, kyn * 4 // 8, 2):
            two = []
            for d in range(2):
                row = strip[pl.ds((b + d) * 64 + 7, 8, stride=8), :]
                acc = acc + row * wyt[(b + d) * 8 : (b + d) * 8 + 8, :]
                two.append(row)
            ysend[s, b * 8 : b * 8 + 16, :] = jnp.concatenate(two, axis=0).astype(BF16)
        fys[s] = acc

        @pl.when(upwind)
        def _():
            yhalo(s).start()

        @pl.when(downwind)
        def _():
            for k in range(half):
                fluxy(s, k).start()

    def speed_rows(q, positive):
        j = (q * 8 + sub).astype(F32)
        return (j + 0.5) * STEP if positive else (HALF - 0.5 - j) * STEP

    def send_edges(s):
        def partial(rows_ref, tile_off, spot):
            def add(g, carry):
                main, thin = list(carry[:4]), list(carry[4:])
                for r in range(4):
                    ky = g * 4 + r
                    block = rows_ref[s, pl.ds(pl.multiple_of(ky * HALF, HALF), HALF), :].astype(F32)
                    for q in range(HALF // 8):
                        main[q] = main[q] + block[q * 8 : q * 8 + 8]
                    for h in range(2):
                        thin[h] = thin[h] + strip[tile(ky, tile_off + h), :]
                return (*main, *thin)

            got = lax.fori_loop(0, groups, add, (zero,) * 6)
            main = thin = zero
            for q in range(HALF // 8):
                main = main + got[q] * speed_rows(q, tile_off > 0)
            for h in range(2):
                x = jnp.abs(vxl[(tile_off + h) * 8 : (tile_off + h) * 8 + 8, :])
                thin = thin + got[4 + h] * jnp.where(cell == spot, x, 0.0)
            thin = jnp.broadcast_to(jnp.sum(thin, axis=1, keepdims=True), (8, 128)) * sel_up
            fxs[s] = (jnp.where(in_strip, 0.0, main) + thin) * FLUX_SCALE
            for k in range(1, nv):
                fluxx(s, k).start()

        pl.when(first)(lambda: partial(sl, 0, 0))
        pl.when(last)(lambda: partial(sr, 2, 7))

    loop(0, groups // 2, pack_first)
    send_strips(0)

    def first_halo(c):
        for r in range(per):
            pack_halo(c * per + r, 0)
        send_chunk(0, c)

    loop(0, CHUNKS, first_halo)
    send_edges(0)

    fetch(0).wait()
    irel = 1.0 / relax[...]
    base_inv = DT_INV + irel

    def inv_of(m):
        for d in range(7):
            at = pl.ds(pl.multiple_of(m * 56 + d * 8, 8), 8)
            invd[at, :] = 1.0 / (base_inv + (m * 7 + (d + 1)).astype(F32) * STEP)

    loop(0, (NVX - 1) // 7, inv_of)

    def place(t):
        row, col = iota((128, 128), 0), iota((128, 128), 1)
        there = jnp.where(up, col, 127 - col)
        hit = jnp.logical_and(row == t * 8 + there, there < 4)
        back[pl.ds(pl.multiple_of(t * 128, 128), 128), :] = hit.astype(F32).astype(BF16)

    loop(0, 16, place)

    permute = (iota((128, 128), 0) == lax.rem(iota((128, 128), 1), 8) * 16 + iota((128, 128), 1) // 8).astype(F32)
    fetch(1).wait()
    fetch(2).wait()
    fetch(3).wait()

    @pl.when(edge)
    def _():
        fetch(4).wait()
        side = jnp.where(first, 0, 1)
        off = jnp.where(first, HALF, 0)
        kind = jnp.broadcast_to(jnp.where(first, lrk[0:1, :], lrk[1:2, :]).astype(F32), (8, 128))
        kinds[0:8, :] = 1.0 - kind
        kind8 = jnp.broadcast_to(jnp.sum(kind * sel, axis=1, keepdims=True), (8, 128))
        kinds[8:16, :] = 1.0 - kind8

        def take(g):
            for r in range(4):
                ky = g * 4 + r
                at = pl.ds(pl.multiple_of((ky * NVX + off) * 2, 2 * HALF), 2 * HALF)
                src[pl.ds(pl.multiple_of(ky * 2 * HALF, 2 * HALF), 2 * HALF), :] = lri[at, :].astype(F32)
            for r in range(4):
                ky = g * 4 + r
                for q in range(HALF // 8):
                    at = pl.ds(pl.multiple_of(ky * HALF + q * 8, 8), 8)
                    inf[at, :] = src[pl.ds(ky * 2 * HALF + q * 16 + side, 8, stride=2), :]
            got = dot_nt(sel, inf[pl.ds(pl.multiple_of(g * 128, 128), 128), :])
            at = pl.ds(pl.multiple_of(g * 8, 8), 8)
            infp[at, :] = kind8 * jnp.dot(got, permute, preferred_element_type=F32)
            kyg = (v * kyn + g * 4 + cell // 2).astype(F32)
            kxg = (off // 16 * 16 + lax.rem(cell, 2) * 16 + in_tile).astype(F32)
            yy, xx = (kyg - (NVX - 1) / 2.0) * STEP, (kxg - (NVX - 1) / 2.0) * STEP
            mwp[at, :] = jnp.exp((xx * xx + yy * yy) * -0.5)
            for q in range(16):
                at = pl.ds(pl.multiple_of(g * 128 + q * 8, 8), 8)
                inf[at, :] = inf[at, :] * kind

        loop(0, groups, take)

    @pl.when(upwind)
    def _():
        block = jnp.where(up, bti[0].astype(F32), bti[1].astype(F32))
        stack = jnp.concatenate([block[:, b * 128 : b * 128 + 128] for b in range(rows // 128)], axis=0)
        kind = jnp.broadcast_to(jnp.where(up, btk[0:1, :], btk[1:2, :]).astype(F32), (8, 8))
        kind = jnp.dot(kind, rep8, preferred_element_type=F32)
        kinds[16:24, :] = 1.0 - kind
        for w in range(8):
            spread = (iota((128, 128), 0) == w * 16 + iota((128, 128), 1) // 8).astype(F32)
            wide = jnp.dot(stack, spread, preferred_element_type=F32)
            for b in range(rows // 128):
                one = jnp.where(cell == sub, wide[b * 8 : b * 8 + 8], 0.0) * kind
                yinf[b * 8 + w : b * 8 + w + 1, :] = jnp.sum(one, axis=0, keepdims=True)

    for k in range(1, nv):
        moment(k).wait_recv()
    u = [moms[a * 8 : a * 8 + 8, :] for a in range(4)]
    for k in range(nv - 1):
        u = [u[a] + momr[k, a * 8 : a * 8 + 8, :] for a in range(4)]
    p = start_params(u)
    p = lax.fori_loop(0, NEWTON, lambda n, q: newton_step(q, u), p)

    pq = p[3] * 0.5
    top_x = None
    for j, (x, plus, minus) in enumerate(one_dim(p[1], pq)):
        if x is None:
            top_x = plus
        else:
            afac[(HALF + j) * 8 : (HALF + j) * 8 + 8, :] = plus
            afac[(HALF - 1 - j) * 8 : (HALF - j) * 8, :] = minus
    height = p[0] + top_x

    def three(a):
        high = a.astype(BF16)
        rest = a - high.astype(F32)
        mid = rest.astype(BF16)
        low = (rest - mid.astype(F32)).astype(BF16)
        return high, mid, low

    def eightfold(a):
        twice = jnp.concatenate([a, a], axis=0)
        return jnp.concatenate([twice] * 8, axis=0)

    split = [three(a) for a in (*p, irel)]
    wide = jnp.concatenate(
        [jnp.concatenate([eightfold(part[n]) for part in split], axis=0) for n in range(3)], axis=1
    )
    wide = dot_nt(jnp.concatenate([sel16] * 3, axis=1), wide)
    thin = [wide[:, a * 128 : a * 128 + 128] for a in range(5)]

    def speed_y(ky):
        return ((v * kyn + ky).astype(F32) - (NVX - 1) / 2.0) * STEP

    def edge_flux(s):
        total = fxs[s]
        for k in range(nv - 1):
            total = total + fxr[s, k]
        return jnp.broadcast_to(jnp.sum(total, axis=0, keepdims=True), (8, 128))

    def sweep_strips(s):
        pl.when(not_first)(lambda: shalo(s, 0).wait_recv())
        pl.when(not_last)(lambda: shalo(s, 1).wait_recv())

        @pl.when(edge)
        def _():
            for k in range(1, nv):
                fluxx(s, k).wait_recv()
            flux = jnp.broadcast_to(jnp.sum(edge_flux(s) * sel, axis=1, keepdims=True), (8, 128)) * kinds[8:16, :]

            def fill(ref):
                ghost = [infp[g * 8 : g * 8 + 8, :] + flux * mwp[g * 8 : g * 8 + 8, :] for g in range(groups)]
                ref[s] = jnp.concatenate(ghost, axis=0).astype(BF16)

            pl.when(first)(lambda: fill(xrr))
            pl.when(last)(lambda: fill(xrl))

        @pl.when(downwind)
        def _():
            yhalo(s).wait_recv()
            yg[...] = yrecv[s].astype(F32)

        @pl.when(upwind)
        def _():
            for k in range(half):
                fluxy_in(s, k).wait_recv()
            total = fyr[s, 0]
            for k in range(1, half):
                total = total + fyr[s, k]
            flux = jnp.broadcast_to(jnp.sum(total, axis=0, keepdims=True), (8, 128))
            for k in (8, 32):
                flux = (flux + pltpu.roll(flux, k, 1)) + (pltpu.roll(flux, 2 * k, 1) + pltpu.roll(flux, 3 * k, 1))
            flux = flux * kinds[16:24, :]
            for b in range(kyn * 4 // 8):
                at = slice(b * 8, b * 8 + 8)
                yg[at, :] = yinf[at, :] + flux * mwy[at, :]

        def step(g):
            at = pl.ds(pl.multiple_of(g * 16, 16), 16)
            right, left = xrr[s, at, :], xrl[s, at, :]
            tiles = {}
            for r in range(4):
                for t in range(4):
                    old = [strip[tile((g * 2 + n) * 4 + r, t), :] for n in range(2)]
                    moved = turn(pair(*old), 1 if t >= 2 else -1).astype(F32)
                    k = r * 2 + t % 2
                    ghost = (turn(right, -k) if t >= 2 else turn(left, 7 - k)).astype(F32)
                    hole = cell == (0 if t >= 2 else 7)
                    xx = vxl[t * 8 : t * 8 + 8, :]
                    ax = jnp.abs(xx)
                    for n in range(2):
                        ky = (g * 2 + n) * 4 + r
                        yy = speed_y(ky)
                        ay = jnp.abs(yy)
                        c = old[n]
                        if s == 0:
                            power = thin[0] + xx * thin[1] + yy * thin[2] + (xx * xx + yy * yy) * 0.5 * thin[3]
                            source = c * DT_INV + jnp.exp(power) * thin[4]
                            inv = 1.0 / (DT_INV + thin[4] + ax + ay)
                            ssrc[tile(ky, t), :] = source
                            sinv[tile(ky, t), :] = inv
                        else:
                            source = ssrc[tile(ky, t), :]
                            inv = sinv[tile(ky, t), :]
                        from_y = jnp.where(sub == 0, yg[pl.ds(ky * 4 + t, 1), :], pltpu.roll(c, 1, 0))
                        from_x = jnp.where(hole, ghost[n * 8 : n * 8 + 8], moved[n * 8 : n * 8 + 8])
                        new = (source + ax * from_x + ay * from_y) * inv
                        tiles[n, r, t] = new
            for (n, r, t), new in tiles.items():
                strip[tile((g * 2 + n) * 4 + r, t), :] = new
            if s < SWEEPS - 1:
                pack_strips(s + 1, g, tiles)

        for g in range(groups // 2):
            step(g)

    def next_edges(s):
        off = jnp.where(first, 0, PITCH * HALF + 8)
        beside = jnp.where(first, 1, -1)
        kx0 = jnp.where(first, 0, HALF)
        row = jnp.where(first, 0, 7)
        speeds = [jnp.where(first, speed_rows(q, False), speed_rows(q, True)) for q in range(HALF // 8)]
        pick = (sub == row).astype(F32)

        def row_of(a):
            return jnp.broadcast_to(jnp.sum(a * pick, axis=0, keepdims=True), (8, 128))

        inv_row = row_of(base_inv) if s == 0 else None

        def add(g, carry):
            main = list(carry[:4])
            thin_sum = list(carry[4:])
            for r in range(4):
                ky = g * 4 + r
                yy = speed_y(ky)
                ay = jnp.abs(yy)
                if s == 0:
                    bfac = row_of(b_of(yy))
                for q in range(0, HALF // 8, 2):
                    own = [gmain[gat(ky, off + PITCH * 8 * (q + d), PITCH), :] for d in range(2)]
                    turned = pltpu.roll(pair(*own), roll_by, 1).astype(F32)
                    for d in range(2):
                        moved = gmain[gat(ky, off + beside + PITCH * 8 * (q + d), PITCH), :]
                        at = pl.ds(pl.multiple_of(ky * HALF + (q + d) * 8, 8), 8)
                        ax = speeds[q + d]
                        if s == 0:
                            fac = afac[pl.ds((kx0 + 8 * (q + d)) * 8 + row, 8, stride=8), :]
                            source = own[d] * DT_INV + fac * bfac
                            inv = 1.0 / (inv_row + ax + ay)
                            esrc[at, :] = source
                            einv[at, :] = inv
                        else:
                            source = esrc[at, :]
                            inv = einv[at, :]
                        new = (source + ax * moved + ay * turned[d * 8 : d * 8 + 8]) * inv
                        main[q + d] = main[q + d] + new
                for h in range(2):
                    thin_sum[h] = thin_sum[h] + strip[tile(ky, kx0 // 16 + h), :]
            return (*main, *thin_sum)

        got = lax.fori_loop(0, groups, add, (zero,) * 6)
        main = thin = zero
        for q in range(HALF // 8):
            main = main + got[q] * speeds[q]
        for h in range(2):
            x = jnp.abs(vxl[pl.ds(pl.multiple_of((kx0 // 16 + h) * 8, 8), 8), :])
            thin = thin + got[4 + h] * jnp.where(cell == row, x, 0.0)
        thin = jnp.broadcast_to(jnp.sum(thin, axis=1, keepdims=True), (8, 128)) * sel_up
        fxs[s + 1] = (jnp.where(in_strip, 0.0, main) + thin) * FLUX_SCALE
        for k in range(1, nv):
            fluxx(s + 1, k).start()

    def fill_main(s, c):
        def put(ref, off):
            for r in range(per):
                ky = c * per + r
                block = ref[s, pl.ds(pl.multiple_of(ky * HALF, HALF), HALF), :].astype(F32)
                for q in range(HALF // 8):
                    gmain[gat(ky, off + PITCH * 8 * q, PITCH), :] = block[q * 8 : q * 8 + 8]

        @pl.when(not_first)
        def _():
            halo(s, c, 0).wait_recv()
            put(rr, PITCH * HALF)

        @pl.when(not_last)
        def _():
            halo(s, c, 1).wait_recv()
            put(rl, 8)

        @pl.when(edge)
        def _():
            flux = edge_flux(s) * kinds[0:8, :]

            def put_wall(positive, off):
                walls = []
                for q in range(HALF // 8):
                    x = speed_rows(q, positive)
                    walls.append(flux * jnp.exp(x * x * -0.5))
                for r in range(per):
                    ky = c * per + r
                    yy = speed_y(ky)
                    scale = jnp.exp(jnp.full((8, 128), yy * yy * -0.5))
                    for q in range(HALF // 8):
                        brought = inf[pl.ds(pl.multiple_of(ky * HALF + q * 8, 8), 8), :]
                        gmain[gat(ky, off + PITCH * 8 * q, PITCH), :] = brought + walls[q] * scale

            pl.when(first)(lambda: put_wall(True, PITCH * HALF))
            pl.when(last)(lambda: put_wall(False, 8))

    def main_row(ky, s, b_of):
        yy = speed_y(ky)
        ay = jnp.abs(yy)
        kyg = v * kyn + ky
        jj = jnp.where(kyg >= HALF, kyg - HALF, HALF - 1 - kyg)
        base = pl.multiple_of(ky * (NVX * 8), NVX * 8)
        if s == 0:
            bfac = b_of(yy)
        for i in range(0, HALF, 2):
            inv = [invd[pl.ds(pl.multiple_of((jj + i + d) * 8, 8), 8), :] for d in range(2)]
            owns = {}
            for positive in (True, False):
                for d in range(2):
                    kx = HALF + i + d if positive else HALF - 1 - i - d
                    owns[positive, d] = gmain[gat(ky, PITCH * kx + (1 if positive else 0)), :]
            turned = {}
            for positive in (True, False):
                pair = jnp.concatenate([owns[positive, d] for d in range(2)], axis=0).astype(BF16)
                turned[positive] = pltpu.roll(pair, roll_by, 1).astype(F32)
            for positive in (True, False):
                done = []
                for d in range(2):
                    kx = HALF + i + d if positive else HALF - 1 - i - d
                    own_off = PITCH * kx + (1 if positive else 0)
                    moved = gmain[gat(ky, PITCH * kx + (0 if positive else 1)), :]
                    at = pl.ds(base + kx * 8, 8)
                    if s == 0:
                        source = owns[positive, d] * DT_INV + afac[kx * 8 : kx * 8 + 8, :] * bfac
                        src[at, :] = source
                    else:
                        source = src[at, :]
                    beside = turned[positive][d * 8 : d * 8 + 8]
                    new = (source + moved * ABS[i + d] + beside * ay) * inv[d]
                    if s < SWEEPS - 1:
                        gmain[gat(ky, own_off), :] = new
                    else:
                        done.append(jnp.where(in_strip, ins[at, :], new))
                if s == SWEEPS - 1:
                    kx = HALF + i if positive else HALF - 2 - i
                    if not positive:
                        done = done[::-1]
                    prev[pl.ds(base + kx * 8, 16), :] = jnp.concatenate(done, axis=0).astype(BF16)

    def bring_back(ky):
        these = flat[pl.ds(pl.multiple_of(ky // 4 * 128, 128), 128), :]
        for t in range(4):
            at = pl.ds(pl.multiple_of(ky * 512 + t * 128, 128), 128)
            weights = back[pl.ds(pl.multiple_of((lax.rem(ky, 4) * 4 + t) * 128, 128), 128), :]
            ins[at, :] = jnp.dot(these, weights, preferred_element_type=F32)

    def store(c):
        at = pl.ds(pl.multiple_of(c * part, part), part)
        return pltpu.make_async_copy(prev.at[at], out_h.at[at], st.at[c])

    size_y = jnp.abs(p[2])
    top_y = None
    for y in ABS:
        e = (size_y + pq * y) * y
        top_y = e if top_y is None else jnp.maximum(top_y, e)
    amp = jnp.exp(height + top_y) * irel

    def b_of(yy):
        return amp * jnp.exp((p[2] + pq * yy) * yy - top_y)

    for s in range(SWEEPS):
        sweep_strips(s)
        if s < SWEEPS - 1:
            send_strips(s + 1)
            pl.when(edge)(lambda: next_edges(s))
        else:

            for g in range(groups):
                flat[g * 128 : g * 128 + 128, :] = strip[g * 128 : g * 128 + 128, :].T.astype(BF16)
            bring_back(0)

        def chunk(c):
            fill_main(s, c)

            def one(ky):
                main_row(ky, s, b_of)
                if s == SWEEPS - 1:
                    bring_back(jnp.minimum(ky + 1, kyn - 1))
                if s < SWEEPS - 1:
                    pack_halo(ky, s + 1)

            for r in range(per):
                one(c * per + r)
            if s < SWEEPS - 1:
                send_chunk(s + 1, c)
            else:
                store(c).start()

        loop(0, CHUNKS, chunk)

    for k in range(1, nv):
        moment(k).wait_send()

    def drain(s):
        def both(c):
            pl.when(not_last)(lambda: halo(s, c, 0).wait_send())
            pl.when(not_first)(lambda: halo(s, c, 1).wait_send())

        loop(0, CHUNKS, both)
        pl.when(not_last)(lambda: shalo(s, 0).wait_send())
        pl.when(not_first)(lambda: shalo(s, 1).wait_send())
        pl.when(upwind)(lambda: yhalo(s).wait_send())

        @pl.when(downwind)
        def _():
            for k in range(half):
                fluxy(s, k).wait_send()

        @pl.when(edge)
        def _():
            for k in range(1, nv):
                fluxx(s, k).wait_send()


    loop(0, SWEEPS, drain)
    for c in range(CHUNKS):
        store(c).wait()


def hand_over(src_h, dst_h, held, come, go):
    part = src_h.shape[0] // PARTS

    def copy_in(n):
        at = pl.ds(n * part, part)
        return pltpu.make_async_copy(src_h.at[at], held.at[at], come.at[n])

    def copy_out(n):
        at = pl.ds(n * part, part)
        return pltpu.make_async_copy(held.at[at], dst_h.at[at], go.at[n])

    for n in range(PARTS):
        copy_in(n).start()
    for n in range(PARTS):
        copy_in(n).wait()
        copy_out(n).start()
    for n in range(PARTS):
        copy_out(n).wait()


def body(previous, relax_time, left_right_kind, bottom_top_kind, left_right_inflow, bottom_top_inflow, *, sizes):
    nv, nx, ny = sizes
    rows, cx, cy = previous.shape
    kyn = rows // NVX
    thin = rows * 8 // 128 * 8
    dma = pltpu.SemaphoreType.DMA
    vm = pltpu.VMEM
    hr = rows // 2
    ur = kyn * 4
    xr = kyn * 2
    scratch = [
        vm((rows * 8, 128), BF16), vm((rows * PITCH, 128), F32), vm((rows * 8, 128), F32),
        vm((NVX * 8, 128), F32), vm((NVX * 8, 128), F32),
        vm((SWEEPS, hr, 128), BF16), vm((SWEEPS, hr, 128), BF16),
        vm((SWEEPS, hr, 128), BF16), vm((SWEEPS, hr, 128), BF16),
        vm((32, 128), F32), vm((nv - 1, 32, 128), F32),
        vm((thin, 128), F32), vm((thin, 128), F32), vm((thin, 128), F32),
        vm((ur, 128), F32),
        vm((SWEEPS, xr, 128), BF16), vm((SWEEPS, xr, 128), BF16),
        vm((SWEEPS, xr, 128), BF16), vm((SWEEPS, xr, 128), BF16),
        vm((hr, 128), F32), vm((hr, 128), F32),
        vm((SWEEPS, ur, 128), BF16), vm((SWEEPS, ur, 128), BF16),
        vm((SWEEPS, 8, 128), F32), vm((SWEEPS, nv // 2, 8, 128), F32),
        vm((SWEEPS, 8, 128), F32), vm((SWEEPS, nv - 1, 8, 128), F32),
        vm((hr, 128), F32), vm((xr, 128), F32), vm((xr, 128), F32),
        vm((ur, 128), F32), vm((ur, 128), F32), vm((ur, 128), F32),
        vm((32, 128), F32), vm((24, 128), F32), vm((rows * 8, 128), F32),
        vm((kyn * 32, 128), BF16), vm((2048, 128), BF16),
        vm((8, 128), F32), vm((2, 128), jnp.int32), vm((2, 8), jnp.int32),
        vm((rows * 2, 128), BF16), vm((2, 8, rows), BF16),
        dma((CHUNKS,)), dma((5,)), dma((CHUNKS,)), dma((nv - 1,)), dma((nv - 1,)),
        dma((SWEEPS, CHUNKS)), dma((SWEEPS, CHUNKS)), dma((SWEEPS, CHUNKS)), dma((SWEEPS, CHUNKS)),
        dma((SWEEPS,)), dma((SWEEPS,)), dma((SWEEPS,)), dma((SWEEPS,)),
        dma((SWEEPS,)), dma((SWEEPS,)), dma((SWEEPS, nv // 2)), dma((SWEEPS, nv // 2)),
        dma((SWEEPS, nv - 1)), dma((SWEEPS, nv - 1)),
    ]
    far = pl.BlockSpec(memory_space=pl.ANY)
    out = pl.pallas_call(
        functools.partial(kernel, nv, nx, ny, rows),
        out_shape=jax.ShapeDtypeStruct((rows * 8, 128), BF16),
        in_specs=[far] * 6,
        out_specs=far,
        scratch_shapes=scratch,
        compiler_params=pltpu.CompilerParams(
            collective_id=0, has_side_effects=True, vmem_limit_bytes=62 * 1024 * 1024
        ),
        name="bgk_step",
    )(
        previous.reshape(rows * 8, 128),
        relax_time,
        left_right_kind,
        bottom_top_kind,
        left_right_inflow.reshape(rows * 2, 128),
        bottom_top_inflow.transpose(1, 2, 0),
    )
    out = pl.pallas_call(
        hand_over,
        out_shape=jax.ShapeDtypeStruct((rows * 8, 128), BF16),
        in_specs=[far],
        out_specs=far,
        scratch_shapes=[pltpu.VMEM((rows * 8, 128), BF16), pltpu.SemaphoreType.DMA((PARTS,)), pltpu.SemaphoreType.DMA((PARTS,))],
        compiler_params=pltpu.CompilerParams(vmem_limit_bytes=62 * 1024 * 1024),
        name="hand_over",
    )(out)
    return out.reshape(rows, cx, cy)


def solution(mesh):
    sizes = (mesh.shape["vel"], mesh.shape["gx"], mesh.shape["gy"])
    return jax.shard_map(
        functools.partial(body, sizes=sizes),
        mesh=mesh,
        in_specs=(
            P("vel", "gx", "gy"),
            P("gx", "gy"),
            P(None, "gy"),
            P(None, "gx"),
            P("vel", None, "gy"),
            P("vel", None, "gx"),
        ),
        out_specs=P("vel", "gx", "gy"),
        check_vma=False,
    )
```

```python
import functools
import math

import jax
import jax.numpy as jnp
import numpy as np
from jax import lax
from jax.experimental import pallas as pl
from jax.experimental.pallas import tpu as pltpu
from jax.sharding import PartitionSpec as P

NVX = 64
HALF = NVX // 2
NEWTON = 2
SWEEPS = 4
CHUNKS = 8
PARTS = 8
STEP = 12.0 / NVX
WEIGHT = STEP * STEP / (2.0 * math.pi)
DT_INV = (NVX - 1) * STEP / 100.0
PITCH = 9

NODES = (np.arange(NVX) - (NVX - 1) / 2.0) * STEP
ABS = [float((j + 0.5) * STEP) for j in range(HALF)]
WALL_1D = np.exp(-NODES * NODES / 2.0)
WALL_NORM = float(np.sum(np.maximum(NODES, 0.0) * WALL_1D) * np.sum(WALL_1D) * WEIGHT)
FLUX_SCALE = WEIGHT / WALL_NORM

F32 = jnp.float32
BF16 = jnp.bfloat16
MESH = pl.DeviceIdType.MESH


def dot_nt(a, b, **kw):
    return lax.dot_general(a, b, (((1,), (1,)), ((), ())), preferred_element_type=F32, **kw)


def dot_tn(a, b, **kw):
    return lax.dot_general(a, b, (((0,), (0,)), ((), ())), preferred_element_type=F32, **kw)


def loop(low, high, step):
    lax.fori_loop(low, high, lambda n, carry: (step(n), carry)[1], 0)


def iota(shape, dim):
    return lax.broadcasted_iota(jnp.int32, shape, dim)


def one_dim(lin, quad):
    top = None
    size = jnp.abs(lin)
    for x in ABS:
        e = (size + quad * x) * x
        top = e if top is None else jnp.maximum(top, e)
    for x in ABS:
        even = quad * (x * x) - top
        odd = lin * x
        yield x, jnp.exp(even + odd), jnp.exp(even - odd)
    yield None, top, None


def power_sums(lin, quad):
    sums = [None] * 5
    top = None
    for x, plus, minus in one_dim(lin, quad):
        if x is None:
            top = plus
            break
        s, d = plus + minus, plus - minus
        for n in range(5):
            term = (s if n % 2 == 0 else d) * (x**n)
            sums[n] = term if sums[n] is None else sums[n] + term
    return sums, top


def start_params(u):
    rho = u[0]
    inv = 1.0 / rho
    ux, uy = u[1] * inv, u[2] * inv
    sq = ux * ux + uy * uy
    t = u[3] * inv - sq / 2.0
    it = 1.0 / t
    return jnp.log(rho * it) - sq * 0.5 * it, ux * it, uy * it, -it


def solve_four(hessian, gradient):
    m = [list(r) for r in hessian]
    t = list(gradient)
    inv = [None] * 4
    for p in range(4):
        inv[p] = 1.0 / m[p][p]
        for low in range(p + 1, 4):
            f = m[low][p] * inv[p]
            for c in range(p + 1, 4):
                m[low][c] = m[low][c] - f * m[p][c]
            t[low] = t[low] - f * t[p]
    r = [None] * 4
    for p in (3, 2, 1, 0):
        a = t[p]
        for c in range(p + 1, 4):
            a = a - m[p][c] * r[c]
        r[p] = a * inv[p]
    return r


def newton_step(p, u):
    s, top_x = power_sums(p[1], p[3] * 0.5)
    q, top_y = power_sums(p[2], p[3] * 0.5)
    c = jnp.exp(p[0] + top_x + top_y) * WEIGHT
    s = [c * a for a in s]
    w = [
        s[0] * q[0],
        s[1] * q[0],
        s[0] * q[1],
        (s[2] * q[0] + s[0] * q[2]) * 0.5,
        s[2] * q[0],
        s[1] * q[1],
        (s[3] * q[0] + s[1] * q[2]) * 0.5,
        s[0] * q[2],
        (s[2] * q[1] + s[0] * q[3]) * 0.5,
        (s[4] * q[0] + 2.0 * s[2] * q[2] + s[0] * q[4]) * 0.25,
    ]
    layout = [[0, 1, 2, 3], [1, 4, 5, 6], [2, 5, 7, 8], [3, 6, 8, 9]]
    corr = solve_four([[w[layout[a][b]] for b in range(4)] for a in range(4)], [w[a] - u[a] for a in range(4)])
    return tuple(p[a] - corr[a] for a in range(4))


def kernel(
    nv, nx, ny, rows,
    prev_h, relax_h, lrk_h, btk_h, lri_h, bti_h,
    out_h,
    prev, gmain, src, afac, invd, sr, sl, rr, rl, moms, momr,
    strip, ssrc, sinv, yg, xsr, xsl, xrr, xrl, esrc, einv, ysend, yrecv,
    fys, fyr, fxs, fxr, inf, infp, mwp, yinf, mwy, wyt, vxl, kinds, ins, flat, back,
    relax, lrk, btk, lri, bti,
    ld, small, st, mom_s, mom_r, r_s, r_r, l_s, l_r, xr_s, xr_r, xl_s, xl_r,
    y_s, y_r, fy_s, fy_r, fx_s, fx_r,
):
    v, gx, gy = lax.axis_index("vel"), lax.axis_index("gx"), lax.axis_index("gy")
    kyn = rows // NVX
    per = kyn // CHUNKS
    up = v >= nv // 2
    first, last = gx == 0, gx == nx - 1
    not_first, not_last = gx > 0, gx < nx - 1
    edge = jnp.logical_or(first, last)
    upwind = lax.rem(v // (nv // 2) + gy, 2) == 1
    downwind = lax.rem(v // (nv // 2) + gy, 2) == 0
    roll_by = jnp.where(up, 1, 127)

    barrier = pltpu.get_barrier_semaphore()

    def greet(*dev):
        pl.semaphore_signal(barrier, inc=1, device_id=dev, device_id_type=MESH)

    for k in range(1, nv):
        greet(lax.rem(v + k, nv), gx, gy)
    greet(v, gx, 1 - gy)
    pl.when(not_first)(lambda: greet(v, gx - 1, gy))
    pl.when(not_last)(lambda: greet(v, gx + 1, gy))

    part = rows * 8 // CHUNKS

    def load(c):
        at = pl.ds(pl.multiple_of(c * part, part), part)
        return pltpu.make_async_copy(prev_h.at[at], prev.at[at], ld.at[c])

    def fetch(n):
        pair = ((relax_h, relax), (lrk_h, lrk), (btk_h, btk), (bti_h, bti), (lri_h, lri))[n]
        return pltpu.make_async_copy(*pair, small.at[n])

    fetch(0).start()
    for c in range(CHUNKS):
        load(c).start()
    for n in (1, 2, 3):
        fetch(n).start()
    pl.when(edge)(lambda: fetch(4).start())

    def remote(s, d, ss, rs, *dev):
        return pltpu.make_async_remote_copy(s, d, ss, rs, device_id=dev, device_id_type=MESH)

    hrow = rows // 2 // CHUNKS

    def halo(s, c, side):
        at = pl.ds(pl.multiple_of(c * hrow, hrow), hrow)
        if side == 0:
            return remote(sr.at[s, at], rr.at[s, at], r_s.at[s, c], r_r.at[s, c], v, gx + 1, gy)
        return remote(sl.at[s, at], rl.at[s, at], l_s.at[s, c], l_r.at[s, c], v, gx - 1, gy)

    def shalo(s, side):
        if side == 0:
            return remote(xsr.at[s], xrr.at[s], xr_s.at[s], xr_r.at[s], v, gx + 1, gy)
        return remote(xsl.at[s], xrl.at[s], xl_s.at[s], xl_r.at[s], v, gx - 1, gy)

    def yhalo(s):
        return remote(ysend.at[s], yrecv.at[s], y_s.at[s], y_r.at[s], v, gx, 1 - gy)

    def moment(k):
        return remote(moms, momr.at[k - 1], mom_s.at[k - 1], mom_r.at[k - 1], lax.rem(v + k, nv), gx, gy)

    def fluxx(s, k):
        return remote(fxs.at[s], fxr.at[s, k - 1], fx_s.at[s, k - 1], fx_r.at[s, k - 1], lax.rem(v + k, nv), gx, gy)

    half = nv // 2

    def fluxy(s, k):
        mine = lax.rem(v, half)
        return remote(fys.at[s], fyr.at[s, mine], fy_s.at[s, k], fy_r.at[s, mine], (1 - v // half) * half + k, gx, gy)

    def fluxy_in(s, k):
        return remote(fys.at[s], fyr.at[s, k], fy_s.at[s, k], fy_r.at[s, k], (1 - v // half) * half + k, gx, gy)

    lane = iota((8, 128), 1)
    sub = iota((8, 128), 0)
    cell = lax.rem(lane, 8)
    in_tile = lane // 8
    for t in range(4):
        vxl[t * 8 : t * 8 + 8, :] = ((t * 16 + in_tile).astype(F32) - (NVX - 1) / 2.0) * STEP
    for b in range(kyn * 4 // 8):
        t = b * 8 + sub
        ky = (v * kyn + t // 4).astype(F32)
        yy = (ky - (NVX - 1) / 2.0) * STEP
        xx = ((lax.rem(t, 4) * 16 + in_tile).astype(F32) - (NVX - 1) / 2.0) * STEP
        at = slice(b * 8, b * 8 + 8)
        mwy[at, :] = jnp.exp((xx * xx + yy * yy) * -0.5)
        wyt[at, :] = jnp.abs(yy) * FLUX_SCALE
    posn = jnp.where(up, lane, 127 - lane)
    want = sub + jnp.where(sub >= 4, 120, 0)
    sel = (posn == want).astype(F32)
    sel16 = sel.astype(BF16)
    sel_up = jnp.where(sub < 4, sel, 0.0)
    in_strip = posn < 4
    rep8 = (cell == sub).astype(F32)

    def gat(ky, off, stride=1):
        return pl.ds(ky * (NVX * PITCH) + off, 8, stride=stride)

    def pack_halo(ky, s):
        for q in range(0, HALF // 8, 2):
            right = [gmain[gat(ky, PITCH * (HALF + 8 * (q + d)) + 8, PITCH), :] for d in range(2)]
            left = [gmain[gat(ky, PITCH * 8 * (q + d), PITCH), :] for d in range(2)]
            at = pl.ds(pl.multiple_of(ky * HALF + q * 8, 16), 16)
            sr[s, at, :] = jnp.concatenate(right, axis=0).astype(BF16)
            sl[s, at, :] = jnp.concatenate(left, axis=0).astype(BF16)

    def send_chunk(s, c):
        pl.when(not_last)(lambda: halo(s, c, 0).start())
        pl.when(not_first)(lambda: halo(s, c, 1).start())

    def tile(ky, t):
        return pl.ds(pl.multiple_of(ky * 32 + t * 8, 8), 8)

    def take_row(ky, u):
        base = pl.multiple_of(ky * (NVX * 8), NVX * 8)
        s0 = s1 = s2 = jnp.zeros((8, 128), F32)
        for i in range(0, HALF, 2):
            pos = prev[pl.ds(base + (HALF + i) * 8, 16), :].astype(F32)
            neg = prev[pl.ds(base + (HALF - 2 - i) * 8, 16), :].astype(F32)
            for d in range(2):
                a, b = pos[8 * d : 8 * d + 8], neg[8 - 8 * d : 16 - 8 * d]
                gmain[gat(ky, PITCH * (HALF + i + d) + 1), :] = a
                gmain[gat(ky, PITCH * (HALF - 1 - i - d)), :] = b
                x = ABS[i + d]
                both = a + b
                s0 = s0 + both
                s1 = s1 + (a - b) * x
                s2 = s2 + both * (x * x)
        yy = ((v * kyn + ky).astype(F32) - (NVX - 1) / 2.0) * STEP
        return (u[0] + s0, u[1] + s1, u[2] + s0 * yy, u[3] + (s2 + s0 * (yy * yy)) * 0.5)

    def take_chunk(c, u):
        load(c).wait()
        for r in range(per):
            u = take_row(c * per + r, u)
        return u

    zero = jnp.zeros((8, 128), F32)
    u = lax.fori_loop(0, CHUNKS, take_chunk, (zero, zero, zero, zero))
    for a in range(4):
        moms[a * 8 : a * 8 + 8, :] = u[a] * WEIGHT
    pl.semaphore_wait(barrier, nv + not_first.astype(jnp.int32) + not_last.astype(jnp.int32))
    for k in range(1, nv):
        moment(k).start()

    def take_strip(g):
        for r in range(4):
            ky = g * 4 + r
            got = dot_nt(sel16, prev[pl.ds(pl.multiple_of(ky * (NVX * 8), NVX * 8), NVX * 8), :])
            for t in range(4):
                strip[tile(ky, t), :] = got[:, t * 128 : t * 128 + 128]

    loop(0, kyn // 4, take_strip)

    groups = kyn // 4

    masks = [(lax.rem(iota((16, 128), 1), 8) == k).astype(F32).astype(BF16) for k in range(8)]

    def pair(a, b):
        return jnp.concatenate([a, b], axis=0).astype(BF16)

    def turn(a, by):
        return a if by % 128 == 0 else pltpu.roll(a, by % 128, 1)

    def pack_strips(s, g, tiles):
        right = left = None
        for k in range(8):
            r, h = k // 2, k % 2
            c = turn(pair(tiles[0, r, 2 + h], tiles[1, r, 2 + h]), k - 7) * masks[k]
            right = c if right is None else right + c
            c = turn(pair(tiles[0, r, h], tiles[1, r, h]), k) * masks[k]
            left = c if left is None else left + c
        at = pl.ds(pl.multiple_of(g * 16, 16), 16)
        xsr[s, at, :] = right
        xsl[s, at, :] = left

    def pack_first(g):
        pack_strips(
            0, g, {(n, r, t): strip[tile((g * 2 + n) * 4 + r, t), :] for n in range(2) for r in range(4) for t in range(4)}
        )

    def send_strips(s):
        pl.when(not_last)(lambda: shalo(s, 0).start())
        pl.when(not_first)(lambda: shalo(s, 1).start())

        acc = jnp.zeros((8, 128), F32)
        for b in range(0, kyn * 4 // 8, 2):
            two = []
            for d in range(2):
                row = strip[pl.ds((b + d) * 64 + 7, 8, stride=8), :]
                acc = acc + row * wyt[(b + d) * 8 : (b + d) * 8 + 8, :]
                two.append(row)
            ysend[s, b * 8 : b * 8 + 16, :] = jnp.concatenate(two, axis=0).astype(BF16)
        fys[s] = acc

        @pl.when(upwind)
        def _():
            yhalo(s).start()

        @pl.when(downwind)
        def _():
            for k in range(half):
                fluxy(s, k).start()

    def speed_rows(q, positive):
        j = (q * 8 + sub).astype(F32)
        return (j + 0.5) * STEP if positive else (HALF - 0.5 - j) * STEP

    def send_edges(s):
        def partial(rows_ref, tile_off, spot):
            def add(g, carry):
                main, thin = list(carry[:4]), list(carry[4:])
                for r in range(4):
                    ky = g * 4 + r
                    block = rows_ref[s, pl.ds(pl.multiple_of(ky * HALF, HALF), HALF), :].astype(F32)
                    for q in range(HALF // 8):
                        main[q] = main[q] + block[q * 8 : q * 8 + 8]
                    for h in range(2):
                        thin[h] = thin[h] + strip[tile(ky, tile_off + h), :]
                return (*main, *thin)

            got = lax.fori_loop(0, groups, add, (zero,) * 6)
            main = thin = zero
            for q in range(HALF // 8):
                main = main + got[q] * speed_rows(q, tile_off > 0)
            for h in range(2):
                x = jnp.abs(vxl[(tile_off + h) * 8 : (tile_off + h) * 8 + 8, :])
                thin = thin + got[4 + h] * jnp.where(cell == spot, x, 0.0)
            thin = jnp.broadcast_to(jnp.sum(thin, axis=1, keepdims=True), (8, 128)) * sel_up
            fxs[s] = (jnp.where(in_strip, 0.0, main) + thin) * FLUX_SCALE
            for k in range(1, nv):
                fluxx(s, k).start()

        pl.when(first)(lambda: partial(sl, 0, 0))
        pl.when(last)(lambda: partial(sr, 2, 7))

    loop(0, groups // 2, pack_first)
    send_strips(0)

    def first_halo(c):
        for r in range(per):
            pack_halo(c * per + r, 0)
        send_chunk(0, c)

    loop(0, CHUNKS, first_halo)
    send_edges(0)

    fetch(0).wait()
    irel = 1.0 / relax[...]
    base_inv = DT_INV + irel

    def inv_of(m):
        for d in range(7):
            at = pl.ds(pl.multiple_of(m * 56 + d * 8, 8), 8)
            invd[at, :] = 1.0 / (base_inv + (m * 7 + (d + 1)).astype(F32) * STEP)

    loop(0, (NVX - 1) // 7, inv_of)

    def place(t):
        row, col = iota((128, 128), 0), iota((128, 128), 1)
        there = jnp.where(up, col, 127 - col)
        hit = jnp.logical_and(row == t * 8 + there, there < 4)
        back[pl.ds(pl.multiple_of(t * 128, 128), 128), :] = hit.astype(F32).astype(BF16)

    loop(0, 16, place)

    permute = (iota((128, 128), 0) == lax.rem(iota((128, 128), 1), 8) * 16 + iota((128, 128), 1) // 8).astype(F32)
    fetch(1).wait()
    fetch(2).wait()
    fetch(3).wait()

    @pl.when(edge)
    def _():
        fetch(4).wait()
        side = jnp.where(first, 0, 1)
        off = jnp.where(first, HALF, 0)
        kind = jnp.broadcast_to(jnp.where(first, lrk[0:1, :], lrk[1:2, :]).astype(F32), (8, 128))
        kinds[0:8, :] = 1.0 - kind
        kind8 = jnp.broadcast_to(jnp.sum(kind * sel, axis=1, keepdims=True), (8, 128))
        kinds[8:16, :] = 1.0 - kind8

        def take(g):
            for r in range(4):
                ky = g * 4 + r
                at = pl.ds(pl.multiple_of((ky * NVX + off) * 2, 2 * HALF), 2 * HALF)
                src[pl.ds(pl.multiple_of(ky * 2 * HALF, 2 * HALF), 2 * HALF), :] = lri[at, :].astype(F32)
            for r in range(4):
                ky = g * 4 + r
                for q in range(HALF // 8):
                    at = pl.ds(pl.multiple_of(ky * HALF + q * 8, 8), 8)
                    inf[at, :] = src[pl.ds(ky * 2 * HALF + q * 16 + side, 8, stride=2), :]
            got = dot_nt(sel, inf[pl.ds(pl.multiple_of(g * 128, 128), 128), :])
            at = pl.ds(pl.multiple_of(g * 8, 8), 8)
            infp[at, :] = kind8 * jnp.dot(got, permute, preferred_element_type=F32)
            kyg = (v * kyn + g * 4 + cell // 2).astype(F32)
            kxg = (off // 16 * 16 + lax.rem(cell, 2) * 16 + in_tile).astype(F32)
            yy, xx = (kyg - (NVX - 1) / 2.0) * STEP, (kxg - (NVX - 1) / 2.0) * STEP
            mwp[at, :] = jnp.exp((xx * xx + yy * yy) * -0.5)
            for q in range(16):
                at = pl.ds(pl.multiple_of(g * 128 + q * 8, 8), 8)
                inf[at, :] = inf[at, :] * kind

        loop(0, groups, take)

    @pl.when(upwind)
    def _():
        block = jnp.where(up, bti[0].astype(F32), bti[1].astype(F32))
        stack = jnp.concatenate([block[:, b * 128 : b * 128 + 128] for b in range(rows // 128)], axis=0)
        kind = jnp.broadcast_to(jnp.where(up, btk[0:1, :], btk[1:2, :]).astype(F32), (8, 8))
        kind = jnp.dot(kind, rep8, preferred_element_type=F32)
        kinds[16:24, :] = 1.0 - kind
        for w in range(8):
            spread = (iota((128, 128), 0) == w * 16 + iota((128, 128), 1) // 8).astype(F32)
            wide = jnp.dot(stack, spread, preferred_element_type=F32)
            for b in range(rows // 128):
                one = jnp.where(cell == sub, wide[b * 8 : b * 8 + 8], 0.0) * kind
                yinf[b * 8 + w : b * 8 + w + 1, :] = jnp.sum(one, axis=0, keepdims=True)

    for k in range(1, nv):
        moment(k).wait_recv()
    u = [moms[a * 8 : a * 8 + 8, :] for a in range(4)]
    for k in range(nv - 1):
        u = [u[a] + momr[k, a * 8 : a * 8 + 8, :] for a in range(4)]
    p = start_params(u)
    p = lax.fori_loop(0, NEWTON, lambda n, q: newton_step(q, u), p)

    pq = p[3] * 0.5
    top_x = None
    for j, (x, plus, minus) in enumerate(one_dim(p[1], pq)):
        if x is None:
            top_x = plus
        else:
            afac[(HALF + j) * 8 : (HALF + j) * 8 + 8, :] = plus
            afac[(HALF - 1 - j) * 8 : (HALF - j) * 8, :] = minus
    height = p[0] + top_x

    def three(a):
        high = a.astype(BF16)
        rest = a - high.astype(F32)
        mid = rest.astype(BF16)
        low = (rest - mid.astype(F32)).astype(BF16)
        return high, mid, low

    def eightfold(a):
        twice = jnp.concatenate([a, a], axis=0)
        return jnp.concatenate([twice] * 8, axis=0)

    split = [three(a) for a in (*p, irel)]
    wide = jnp.concatenate(
        [jnp.concatenate([eightfold(part[n]) for part in split], axis=0) for n in range(3)], axis=1
    )
    wide = dot_nt(jnp.concatenate([sel16] * 3, axis=1), wide)
    thin = [wide[:, a * 128 : a * 128 + 128] for a in range(5)]

    def speed_y(ky):
        return ((v * kyn + ky).astype(F32) - (NVX - 1) / 2.0) * STEP

    def edge_flux(s):
        total = fxs[s]
        for k in range(nv - 1):
            total = total + fxr[s, k]
        return jnp.broadcast_to(jnp.sum(total, axis=0, keepdims=True), (8, 128))

    def sweep_strips(s):
        pl.when(not_first)(lambda: shalo(s, 0).wait_recv())
        pl.when(not_last)(lambda: shalo(s, 1).wait_recv())

        @pl.when(edge)
        def _():
            for k in range(1, nv):
                fluxx(s, k).wait_recv()
            flux = jnp.broadcast_to(jnp.sum(edge_flux(s) * sel, axis=1, keepdims=True), (8, 128)) * kinds[8:16, :]

            def fill(ref):
                ghost = [infp[g * 8 : g * 8 + 8, :] + flux * mwp[g * 8 : g * 8 + 8, :] for g in range(groups)]
                ref[s] = jnp.concatenate(ghost, axis=0).astype(BF16)

            pl.when(first)(lambda: fill(xrr))
            pl.when(last)(lambda: fill(xrl))

        @pl.when(downwind)
        def _():
            yhalo(s).wait_recv()
            yg[...] = yrecv[s].astype(F32)

        @pl.when(upwind)
        def _():
            for k in range(half):
                fluxy_in(s, k).wait_recv()
            total = fyr[s, 0]
            for k in range(1, half):
                total = total + fyr[s, k]
            flux = jnp.broadcast_to(jnp.sum(total, axis=0, keepdims=True), (8, 128))
            for k in (8, 32):
                flux = (flux + pltpu.roll(flux, k, 1)) + (pltpu.roll(flux, 2 * k, 1) + pltpu.roll(flux, 3 * k, 1))
            flux = flux * kinds[16:24, :]
            for b in range(kyn * 4 // 8):
                at = slice(b * 8, b * 8 + 8)
                yg[at, :] = yinf[at, :] + flux * mwy[at, :]

        def step(g):
            at = pl.ds(pl.multiple_of(g * 16, 16), 16)
            right, left = xrr[s, at, :], xrl[s, at, :]
            tiles = {}
            for r in range(4):
                for t in range(4):
                    old = [strip[tile((g * 2 + n) * 4 + r, t), :] for n in range(2)]
                    moved = turn(pair(*old), 1 if t >= 2 else -1).astype(F32)
                    k = r * 2 + t % 2
                    ghost = (turn(right, -k) if t >= 2 else turn(left, 7 - k)).astype(F32)
                    hole = cell == (0 if t >= 2 else 7)
                    xx = vxl[t * 8 : t * 8 + 8, :]
                    ax = jnp.abs(xx)
                    for n in range(2):
                        ky = (g * 2 + n) * 4 + r
                        yy = speed_y(ky)
                        ay = jnp.abs(yy)
                        c = old[n]
                        if s == 0:
                            power = thin[0] + xx * thin[1] + yy * thin[2] + (xx * xx + yy * yy) * 0.5 * thin[3]
                            source = c * DT_INV + jnp.exp(power) * thin[4]
                            inv = 1.0 / (DT_INV + thin[4] + ax + ay)
                            ssrc[tile(ky, t), :] = source
                            sinv[tile(ky, t), :] = inv
                        else:
                            source = ssrc[tile(ky, t), :]
                            inv = sinv[tile(ky, t), :]
                        from_y = jnp.where(sub == 0, yg[pl.ds(ky * 4 + t, 1), :], pltpu.roll(c, 1, 0))
                        from_x = jnp.where(hole, ghost[n * 8 : n * 8 + 8], moved[n * 8 : n * 8 + 8])
                        new = (source + ax * from_x + ay * from_y) * inv
                        tiles[n, r, t] = new
            for (n, r, t), new in tiles.items():
                strip[tile((g * 2 + n) * 4 + r, t), :] = new
            if s < SWEEPS - 1:
                pack_strips(s + 1, g, tiles)

        for g in range(groups // 2):
            step(g)

    def next_edges(s):
        off = jnp.where(first, 0, PITCH * HALF + 8)
        beside = jnp.where(first, 1, -1)
        kx0 = jnp.where(first, 0, HALF)
        row = jnp.where(first, 0, 7)
        speeds = [jnp.where(first, speed_rows(q, False), speed_rows(q, True)) for q in range(HALF // 8)]
        pick = (sub == row).astype(F32)

        def row_of(a):
            return jnp.broadcast_to(jnp.sum(a * pick, axis=0, keepdims=True), (8, 128))

        inv_row = row_of(base_inv) if s == 0 else None

        def add(g, carry):
            main = list(carry[:4])
            thin_sum = list(carry[4:])
            for r in range(4):
                ky = g * 4 + r
                yy = speed_y(ky)
                ay = jnp.abs(yy)
                if s == 0:
                    bfac = row_of(b_of(yy))
                for q in range(0, HALF // 8, 2):
                    own = [gmain[gat(ky, off + PITCH * 8 * (q + d), PITCH), :] for d in range(2)]
                    turned = pltpu.roll(pair(*own), roll_by, 1).astype(F32)
                    for d in range(2):
                        moved = gmain[gat(ky, off + beside + PITCH * 8 * (q + d), PITCH), :]
                        at = pl.ds(pl.multiple_of(ky * HALF + (q + d) * 8, 8), 8)
                        ax = speeds[q + d]
                        if s == 0:
                            fac = afac[pl.ds((kx0 + 8 * (q + d)) * 8 + row, 8, stride=8), :]
                            source = own[d] * DT_INV + fac * bfac
                            inv = 1.0 / (inv_row + ax + ay)
                            esrc[at, :] = source
                            einv[at, :] = inv
                        else:
                            source = esrc[at, :]
                            inv = einv[at, :]
                        new = (source + ax * moved + ay * turned[d * 8 : d * 8 + 8]) * inv
                        main[q + d] = main[q + d] + new
                for h in range(2):
                    thin_sum[h] = thin_sum[h] + strip[tile(ky, kx0 // 16 + h), :]
            return (*main, *thin_sum)

        got = (zero,) * 6
        for g in range(groups):
            got = add(g, got)
        main = thin = zero
        for q in range(HALF // 8):
            main = main + got[q] * speeds[q]
        for h in range(2):
            x = jnp.abs(vxl[pl.ds(pl.multiple_of((kx0 // 16 + h) * 8, 8), 8), :])
            thin = thin + got[4 + h] * jnp.where(cell == row, x, 0.0)
        thin = jnp.broadcast_to(jnp.sum(thin, axis=1, keepdims=True), (8, 128)) * sel_up
        fxs[s + 1] = (jnp.where(in_strip, 0.0, main) + thin) * FLUX_SCALE
        for k in range(1, nv):
            fluxx(s + 1, k).start()

    def fill_main(s, c):
        def put(ref, off):
            for r in range(per):
                ky = c * per + r
                block = ref[s, pl.ds(pl.multiple_of(ky * HALF, HALF), HALF), :].astype(F32)
                for q in range(HALF // 8):
                    gmain[gat(ky, off + PITCH * 8 * q, PITCH), :] = block[q * 8 : q * 8 + 8]

        @pl.when(not_first)
        def _():
            halo(s, c, 0).wait_recv()
            put(rr, PITCH * HALF)

        @pl.when(not_last)
        def _():
            halo(s, c, 1).wait_recv()
            put(rl, 8)

        @pl.when(edge)
        def _():
            flux = edge_flux(s) * kinds[0:8, :]

            def put_wall(positive, off):
                walls = []
                for q in range(HALF // 8):
                    x = speed_rows(q, positive)
                    walls.append(flux * jnp.exp(x * x * -0.5))
                for r in range(per):
                    ky = c * per + r
                    yy = speed_y(ky)
                    scale = jnp.exp(jnp.full((8, 128), yy * yy * -0.5))
                    for q in range(HALF // 8):
                        brought = inf[pl.ds(pl.multiple_of(ky * HALF + q * 8, 8), 8), :]
                        gmain[gat(ky, off + PITCH * 8 * q, PITCH), :] = brought + walls[q] * scale

            pl.when(first)(lambda: put_wall(True, PITCH * HALF))
            pl.when(last)(lambda: put_wall(False, 8))

    def main_row(ky, s, b_of):
        yy = speed_y(ky)
        ay = jnp.abs(yy)
        kyg = v * kyn + ky
        jj = jnp.where(kyg >= HALF, kyg - HALF, HALF - 1 - kyg)
        base = pl.multiple_of(ky * (NVX * 8), NVX * 8)
        if s == 0:
            bfac = b_of(yy)
        for i in range(0, HALF, 2):
            inv = [invd[pl.ds(pl.multiple_of((jj + i + d) * 8, 8), 8), :] for d in range(2)]
            owns = {}
            for positive in (True, False):
                for d in range(2):
                    kx = HALF + i + d if positive else HALF - 1 - i - d
                    owns[positive, d] = gmain[gat(ky, PITCH * kx + (1 if positive else 0)), :]
            turned = {}
            for positive in (True, False):
                pair = jnp.concatenate([owns[positive, d] for d in range(2)], axis=0).astype(BF16)
                turned[positive] = pltpu.roll(pair, roll_by, 1).astype(F32)
            for positive in (True, False):
                done = []
                for d in range(2):
                    kx = HALF + i + d if positive else HALF - 1 - i - d
                    own_off = PITCH * kx + (1 if positive else 0)
                    moved = gmain[gat(ky, PITCH * kx + (0 if positive else 1)), :]
                    at = pl.ds(base + kx * 8, 8)
                    if s == 0:
                        source = owns[positive, d] * DT_INV + afac[kx * 8 : kx * 8 + 8, :] * bfac
                        src[at, :] = source
                    else:
                        source = src[at, :]
                    beside = turned[positive][d * 8 : d * 8 + 8]
                    new = (source + moved * ABS[i + d] + beside * ay) * inv[d]
                    if s < SWEEPS - 1:
                        gmain[gat(ky, own_off), :] = new
                    else:
                        done.append(jnp.where(in_strip, ins[at, :], new))
                if s == SWEEPS - 1:
                    kx = HALF + i if positive else HALF - 2 - i
                    if not positive:
                        done = done[::-1]
                    prev[pl.ds(base + kx * 8, 16), :] = jnp.concatenate(done, axis=0).astype(BF16)

    def bring_back(ky):
        these = flat[pl.ds(pl.multiple_of(ky // 4 * 128, 128), 128), :]
        for t in range(4):
            at = pl.ds(pl.multiple_of(ky * 512 + t * 128, 128), 128)
            weights = back[pl.ds(pl.multiple_of((lax.rem(ky, 4) * 4 + t) * 128, 128), 128), :]
            ins[at, :] = jnp.dot(these, weights, preferred_element_type=F32)

    def store(c):
        at = pl.ds(pl.multiple_of(c * part, part), part)
        return pltpu.make_async_copy(prev.at[at], out_h.at[at], st.at[c])

    size_y = jnp.abs(p[2])
    top_y = None
    for y in ABS:
        e = (size_y + pq * y) * y
        top_y = e if top_y is None else jnp.maximum(top_y, e)
    amp = jnp.exp(height + top_y) * irel

    def b_of(yy):
        return amp * jnp.exp((p[2] + pq * yy) * yy - top_y)

    for s in range(SWEEPS):
        sweep_strips(s)
        if s < SWEEPS - 1:
            send_strips(s + 1)
            pl.when(edge)(lambda: next_edges(s))
        else:

            for g in range(groups):
                flat[g * 128 : g * 128 + 128, :] = strip[g * 128 : g * 128 + 128, :].T.astype(BF16)
            bring_back(0)

        def chunk(c):
            fill_main(s, c)

            def one(ky):
                main_row(ky, s, b_of)
                if s == SWEEPS - 1:
                    bring_back(jnp.minimum(ky + 1, kyn - 1))
                if s < SWEEPS - 1:
                    pack_halo(ky, s + 1)

            for r in range(per):
                one(c * per + r)
            if s < SWEEPS - 1:
                send_chunk(s + 1, c)
            else:
                store(c).start()

        loop(0, CHUNKS, chunk)

    for k in range(1, nv):
        moment(k).wait_send()

    def drain(s):
        def both(c):
            pl.when(not_last)(lambda: halo(s, c, 0).wait_send())
            pl.when(not_first)(lambda: halo(s, c, 1).wait_send())

        loop(0, CHUNKS, both)
        pl.when(not_last)(lambda: shalo(s, 0).wait_send())
        pl.when(not_first)(lambda: shalo(s, 1).wait_send())
        pl.when(upwind)(lambda: yhalo(s).wait_send())

        @pl.when(downwind)
        def _():
            for k in range(half):
                fluxy(s, k).wait_send()

        @pl.when(edge)
        def _():
            for k in range(1, nv):
                fluxx(s, k).wait_send()


    loop(0, SWEEPS, drain)
    for c in range(CHUNKS):
        store(c).wait()


def hand_over(src_h, dst_h, held, come, go):
    part = src_h.shape[0] // PARTS

    def copy_in(n):
        at = pl.ds(n * part, part)
        return pltpu.make_async_copy(src_h.at[at], held.at[at], come.at[n])

    def copy_out(n):
        at = pl.ds(n * part, part)
        return pltpu.make_async_copy(held.at[at], dst_h.at[at], go.at[n])

    for n in range(PARTS):
        copy_in(n).start()
    for n in range(PARTS):
        copy_in(n).wait()
        copy_out(n).start()
    for n in range(PARTS):
        copy_out(n).wait()


def body(previous, relax_time, left_right_kind, bottom_top_kind, left_right_inflow, bottom_top_inflow, *, sizes):
    nv, nx, ny = sizes
    rows, cx, cy = previous.shape
    kyn = rows // NVX
    thin = rows * 8 // 128 * 8
    dma = pltpu.SemaphoreType.DMA
    vm = pltpu.VMEM
    hr = rows // 2
    ur = kyn * 4
    xr = kyn * 2
    scratch = [
        vm((rows * 8, 128), BF16), vm((rows * PITCH + 72, 128), F32), vm((rows * 8, 128), F32),
        vm((NVX * 8 + 64, 128), F32), vm((NVX * 8, 128), F32),
        vm((SWEEPS, hr, 128), BF16), vm((SWEEPS, hr, 128), BF16),
        vm((SWEEPS, hr, 128), BF16), vm((SWEEPS, hr, 128), BF16),
        vm((32, 128), F32), vm((nv - 1, 32, 128), F32),
        vm((thin + 64, 128), F32), vm((thin, 128), F32), vm((thin, 128), F32),
        vm((ur, 128), F32),
        vm((SWEEPS, xr, 128), BF16), vm((SWEEPS, xr, 128), BF16),
        vm((SWEEPS, xr, 128), BF16), vm((SWEEPS, xr, 128), BF16),
        vm((hr, 128), F32), vm((hr, 128), F32),
        vm((SWEEPS, ur, 128), BF16), vm((SWEEPS, ur, 128), BF16),
        vm((SWEEPS, 8, 128), F32), vm((SWEEPS, nv // 2, 8, 128), F32),
        vm((SWEEPS, 8, 128), F32), vm((SWEEPS, nv - 1, 8, 128), F32),
        vm((hr, 128), F32), vm((xr, 128), F32), vm((xr, 128), F32),
        vm((ur, 128), F32), vm((ur, 128), F32), vm((ur, 128), F32),
        vm((32, 128), F32), vm((24, 128), F32), vm((rows * 8, 128), F32),
        vm((kyn * 32, 128), BF16), vm((2048, 128), BF16),
        vm((8, 128), F32), vm((2, 128), jnp.int32), vm((2, 8), jnp.int32),
        vm((rows * 2, 128), BF16), vm((2, 8, rows), BF16),
        dma((CHUNKS,)), dma((5,)), dma((CHUNKS,)), dma((nv - 1,)), dma((nv - 1,)),
        dma((SWEEPS, CHUNKS)), dma((SWEEPS, CHUNKS)), dma((SWEEPS, CHUNKS)), dma((SWEEPS, CHUNKS)),
        dma((SWEEPS,)), dma((SWEEPS,)), dma((SWEEPS,)), dma((SWEEPS,)),
        dma((SWEEPS,)), dma((SWEEPS,)), dma((SWEEPS, nv // 2)), dma((SWEEPS, nv // 2)),
        dma((SWEEPS, nv - 1)), dma((SWEEPS, nv - 1)),
    ]
    far = pl.BlockSpec(memory_space=pl.ANY)
    out = pl.pallas_call(
        functools.partial(kernel, nv, nx, ny, rows),
        out_shape=jax.ShapeDtypeStruct((rows * 8, 128), BF16),
        in_specs=[far] * 6,
        out_specs=far,
        scratch_shapes=scratch,
        compiler_params=pltpu.CompilerParams(
            collective_id=0, has_side_effects=True, vmem_limit_bytes=62 * 1024 * 1024
        ),
        name="bgk_step",
    )(
        previous.reshape(rows * 8, 128),
        relax_time,
        left_right_kind,
        bottom_top_kind,
        left_right_inflow.reshape(rows * 2, 128),
        bottom_top_inflow.transpose(1, 2, 0),
    )
    out = pl.pallas_call(
        hand_over,
        out_shape=jax.ShapeDtypeStruct((rows * 8, 128), BF16),
        in_specs=[far],
        out_specs=far,
        scratch_shapes=[pltpu.VMEM((rows * 8, 128), BF16), pltpu.SemaphoreType.DMA((PARTS,)), pltpu.SemaphoreType.DMA((PARTS,))],
        compiler_params=pltpu.CompilerParams(vmem_limit_bytes=62 * 1024 * 1024),
        name="hand_over",
    )(out)
    return out.reshape(rows, cx, cy)


def solution(mesh):
    sizes = (mesh.shape["vel"], mesh.shape["gx"], mesh.shape["gy"])
    return jax.shard_map(
        functools.partial(body, sizes=sizes),
        mesh=mesh,
        in_specs=(
            P("vel", "gx", "gy"),
            P("gx", "gy"),
            P(None, "gy"),
            P(None, "gx"),
            P("vel", None, "gy"),
            P("vel", None, "gx"),
        ),
        out_specs=P("vel", "gx", "gy"),
        check_vma=False,
    )
```
